128 devices in a mesh: gx: 16 (over x, y), gy: 8 (over z, core).
Axes of the slice: x: 4, y: 4, z: 4, core: 2. Of those that a mesh axis runs over, the one named last changes fastest.
Arguments:
- fields: float32 [8, 32, 65536], P(None, None, ('gx', 'gy')), may hold values from -2 to 30, as said below
- refined: int32 [32, 16], replicated, may hold values from 0 to 1, as said below
Outputs:
- advanced: float32 [8, 32, 40960], P(None, None, ('gx', 'gy'))
The draws below stay inside these ranges and needn't reach their ends.
Inputs may be any that keep to these rules, and one draw needn't show every extreme that they name: Counting one block for a root with refined 0 and four for a root with refined 1, in order of L (gx major) and of the tiles' roots, the blocks before device L number 10 * L plus or minus at most 3; both 10 * L + 3 and 10 * L - 3 occur in every draw, and the blocks number 10 per device in all. `fields`: every slot, live or not, holds a state of density 0.2 to 2, pressure 0.5 to 18, and velocity and field components of size under 0.9.
All inputs are finite; a program needn't handle non-finite values.
Results may differ from the reference program's by a relative error of at most 0.0003.
Values sent between devices are 32-bit elements; how exact they have to be, the bound alone decides.
A program may use at most 64 MiB of HBM per device.

```python
import math
import jax
import jax.numpy as jnp
import numpy as np
from jax import lax

BS = 32
RD = 2
CAP = 10
RX = 32
RY = 16
BLOCKS_OLD = 2048
N_GX = 16
N_GY = 8


GAMMA = 5.0 / 3.0


def morton_order(side):
    code_list = []
    for row_index in range(side):
        for col_index in range(side):
            code_value = 0
            for bit_index in range(8):
                code_value = code_value | (row_index >> bit_index & 1) << 2 * bit_index + 1
                code_value = code_value | (col_index >> bit_index & 1) << 2 * bit_index
            code_list.append(code_value)
    return np.argsort(np.array(code_list), kind='stable').astype(np.int32)


def refined_flags(key):
    key = jax.random.fold_in(key, 11)
    tiles_x = RX // RD
    tiles_y = RY // RD
    tile_count = tiles_x * tiles_y
    reach = RD * RD // 4
    key_excess, key_up, key_down, key_perm = jax.random.split(key, 4)
    excess = jax.random.randint(key_excess, (tile_count - 1,), -reach, reach + 1, dtype=jnp.int32)
    upward = jax.random.randint(key_up, (), 0, tile_count - 1, dtype=jnp.int32)
    downward = (upward + 1 + jax.random.randint(key_down, (), 0, tile_count - 2, dtype=jnp.int32)) % (tile_count - 1)
    excess = excess.at[upward].set(reach).at[downward].set(-reach)
    edges = jnp.concatenate([jnp.zeros((1,), jnp.int32), excess, jnp.zeros((1,), jnp.int32)])
    refined_count = RD * RD // 2 + edges[1:] - edges[:-1]
    perm_keys = jax.random.split(key_perm, tile_count)

    def tile_ranks(tile_key):
        return jax.random.permutation(tile_key, RD * RD).astype(jnp.int32)
    ranks = jax.vmap(tile_ranks)(perm_keys)
    flags = (ranks < refined_count[:, None]).astype(jnp.int32)
    return flags.reshape(tiles_x, tiles_y, RD, RD).transpose(0, 2, 1, 3).reshape(RX, RY)


def draw_refined(key, part):
    return refined_flags(key)


def draw_fields(key, part):
    flags = refined_flags(key)
    key = jax.random.fold_in(key, 23)
    width = BLOCKS_OLD * BS
    shape = (BS, width)
    key_list = jax.random.split(key, 12)
    density = jnp.exp(jax.random.uniform(key_list[0], shape, jnp.float32, minval=math.log(0.5), maxval=math.log(2.0)))
    pressure = jnp.exp(jax.random.uniform(key_list[1], shape, jnp.float32, minval=math.log(0.5), maxval=math.log(2.0)))
    velocity = [0.3 * jnp.clip(jax.random.normal(key_list[2 + axis_id], shape, jnp.float32), -2.9, 2.9) for axis_id in range(3)]
    field = [0.3 * jnp.clip(jax.random.normal(key_list[5 + axis_id], shape, jnp.float32), -2.9, 2.9) for axis_id in range(3)]
    tiles_x = RX // RD
    tiles_y = RY // RD
    grid = flags.reshape(tiles_x, RD, tiles_y, RD).transpose(0, 2, 1, 3).reshape(tiles_x * tiles_y, RD * RD)
    roots = jnp.take(grid, jnp.asarray(morton_order(RD)), axis=1)
    fine_slot = jnp.repeat(roots, 4, axis=1).reshape(-1) > 0
    scores = jax.random.permutation(key_list[8], BLOCKS_OLD).astype(jnp.int32)
    hot_slot = jnp.argmax(jnp.where(fine_slot, scores, -1)).astype(jnp.int32)
    hot_row = jax.random.randint(key_list[9], (), 0, BS - 1, dtype=jnp.int32)
    hot_col = hot_slot * BS + jax.random.randint(key_list[10], (), 0, BS - 1, dtype=jnp.int32)
    hot_speed = jnp.exp(jax.random.uniform(key_list[11], (), jnp.float32, minval=math.log(8.0), maxval=math.log(12.0)))
    row_ids = jnp.arange(BS, dtype=jnp.int32)[:, None]
    col_ids = jnp.arange(width, dtype=jnp.int32)[None, :]
    hot_mask = (row_ids >= hot_row) & (row_ids < hot_row + 2) & (col_ids >= hot_col) & (col_ids < hot_col + 2)
    density = jnp.where(hot_mask, 0.2, density)
    pressure = jnp.where(hot_mask, 0.2 * hot_speed * hot_speed / GAMMA, pressure)
    kinetic = 0.5 * density * (velocity[0] * velocity[0] + velocity[1] * velocity[1] + velocity[2] * velocity[2])
    magnetic = 0.5 * (field[0] * field[0] + field[1] * field[1] + field[2] * field[2])
    energy = pressure / (GAMMA - 1.0) + kinetic + magnetic
    stacked = jnp.stack([density, density * velocity[0], density * velocity[1], density * velocity[2], energy, field[0], field[1], field[2]])
    return stacked.astype(jnp.float32)


def setup_inputs(seed: int = 0) -> dict:
    key_of = jax.random.split(jax.random.key(seed), 3)
    return {
        "fields": draw_fields(jax.random.fold_in(key_of[2], 71), 0),
        "refined": draw_refined(jax.random.fold_in(key_of[2], 71), 0),
    }


GAMMA = 5.0 / 3.0
COURANT = 0.2

def morton_table(side):
    code_list = []
    for row_index in range(side):
        for col_index in range(side):
            code_value = 0
            for bit_index in range(8):
                code_value = code_value | (row_index >> bit_index & 1) << 2 * bit_index + 1
                code_value = code_value | (col_index >> bit_index & 1) << 2 * bit_index
            code_list.append(code_value)
    return np.argsort(np.array(code_list), kind='stable').astype(np.int32)

def slab_of(array, along, begin_at, end_at):
    return lax.slice_in_dim(array, begin_at, end_at, axis=along)

def primitive(cons):
    density = cons[0]
    vel_x = cons[1] / density
    vel_y = cons[2] / density
    vel_z = cons[3] / density
    kinetic = 0.5 * density * (vel_x * vel_x + vel_y * vel_y + vel_z * vel_z)
    magnetic = 0.5 * (cons[5] * cons[5] + cons[6] * cons[6] + cons[7] * cons[7])
    pressure = (GAMMA - 1.0) * (cons[4] - kinetic - magnetic)
    return jnp.stack([density, vel_x, vel_y, vel_z, pressure, cons[5], cons[6], cons[7]])

def conserved(prim):
    density = prim[0]
    kinetic = 0.5 * density * (prim[1] * prim[1] + prim[2] * prim[2] + prim[3] * prim[3])
    magnetic = 0.5 * (prim[5] * prim[5] + prim[6] * prim[6] + prim[7] * prim[7])
    energy = prim[4] / (GAMMA - 1.0) + kinetic + magnetic
    return jnp.stack([density, density * prim[1], density * prim[2], density * prim[3], energy, prim[5], prim[6], prim[7]])

def fast_speed(prim, normal):
    density = prim[0]
    sound_sq = GAMMA * prim[4] / density
    field_sq = prim[5] * prim[5] + prim[6] * prim[6] + prim[7] * prim[7]
    alfven_sq = field_sq / density
    if normal == 1:
        trans_sq = prim[6] * prim[6] + prim[7] * prim[7]
    else:
        trans_sq = prim[5] * prim[5] + prim[7] * prim[7]
    discrim = (sound_sq - alfven_sq) * (sound_sq - alfven_sq) + 4.0 * sound_sq * trans_sq / density
    return jnp.sqrt(0.5 * (sound_sq + alfven_sq + jnp.sqrt(discrim)))

def physical_flux(prim, energy, normal):
    tangent = 3 - normal
    density = prim[0]
    vel_n = prim[normal]
    vel_t = prim[tangent]
    vel_z = prim[3]
    field_n = prim[4 + normal]
    field_t = prim[4 + tangent]
    field_z = prim[7]
    total_p = prim[4] + 0.5 * (field_n * field_n + field_t * field_t + field_z * field_z)
    vel_dot_b = vel_n * field_n + vel_t * field_t + vel_z * field_z
    flux_mn = density * vel_n * vel_n + total_p - field_n * field_n
    flux_mt = density * vel_n * vel_t - field_n * field_t
    flux_mz = density * vel_n * vel_z - field_n * field_z
    flux_en = (energy + total_p) * vel_n - field_n * vel_dot_b
    flux_bt = field_t * vel_n - field_n * vel_t
    flux_bz = field_z * vel_n - field_n * vel_z
    no_flux = jnp.zeros_like(density)
    if normal == 1:
        return jnp.stack([density * vel_n, flux_mn, flux_mt, flux_mz, flux_en, no_flux, flux_bt, flux_bz])
    return jnp.stack([density * vel_n, flux_mt, flux_mn, flux_mz, flux_en, flux_bt, no_flux, flux_bz])

def hlle_flux(left_prim, right_prim, normal):
    left_cons = conserved(left_prim)
    right_cons = conserved(right_prim)
    left_flux = physical_flux(left_prim, left_cons[4], normal)
    right_flux = physical_flux(right_prim, right_cons[4], normal)
    left_fast = fast_speed(left_prim, normal)
    right_fast = fast_speed(right_prim, normal)
    slow_edge = jnp.minimum(jnp.minimum(left_prim[normal] - left_fast, right_prim[normal] - right_fast), 0.0)
    fast_edge = jnp.maximum(jnp.maximum(left_prim[normal] + left_fast, right_prim[normal] + right_fast), 0.0)
    return (fast_edge * left_flux - slow_edge * right_flux + fast_edge * slow_edge * (right_cons - left_cons)) / (fast_edge - slow_edge)

def ppm_faces(prim, along):
    extent = prim.shape[along]
    lower = slab_of(prim, along, 1, extent - 2)
    upper = slab_of(prim, along, 2, extent - 1)
    outer_low = slab_of(prim, along, 0, extent - 3)
    outer_high = slab_of(prim, along, 3, extent)
    face_val = 7.0 / 12.0 * (lower + upper) - 1.0 / 12.0 * (outer_low + outer_high)
    face_val = jnp.clip(face_val, jnp.minimum(lower, upper), jnp.maximum(lower, upper))
    center = slab_of(prim, along, 2, extent - 2)
    left_val = slab_of(face_val, along, 0, extent - 4)
    right_val = slab_of(face_val, along, 1, extent - 3)
    is_flat = (right_val - center) * (center - left_val) <= 0.0
    left_val = jnp.where(is_flat, center, left_val)
    right_val = jnp.where(is_flat, center, right_val)
    spread = right_val - left_val
    offset = center - 0.5 * (left_val + right_val)
    bound = spread * spread / 6.0
    new_left = jnp.where(spread * offset > bound, 3.0 * center - 2.0 * right_val, left_val)
    new_right = jnp.where(spread * offset < -bound, 3.0 * center - 2.0 * left_val, right_val)
    return (new_left, new_right)

def advance(cons, inv_cols, time_step):
    size_p = cons.shape[1]
    size_q = cons.shape[2]
    prim = primitive(cons)
    flux_x = hlle_flux(slab_of(prim, 1, 0, size_p - 1), slab_of(prim, 1, 1, size_p), 1)
    flux_y = hlle_flux(slab_of(prim, 2, 0, size_q - 1), slab_of(prim, 2, 1, size_q), 2)
    half_rate = 0.5 * time_step * slab_of(inv_cols, 0, 1, size_q - 1)
    diff_x = slab_of(slab_of(flux_x, 1, 1, size_p - 1), 2, 1, size_q - 1) - slab_of(slab_of(flux_x, 1, 0, size_p - 2), 2, 1, size_q - 1)
    diff_y = slab_of(slab_of(flux_y, 1, 1, size_p - 1), 2, 1, size_q - 1) - slab_of(slab_of(flux_y, 1, 1, size_p - 1), 2, 0, size_q - 2)
    middle = slab_of(slab_of(cons, 1, 1, size_p - 1), 2, 1, size_q - 1) - half_rate * diff_x - half_rate * diff_y
    mid_prim = primitive(middle)
    size_a = size_p - 2
    size_b = size_q - 2
    x_strip = slab_of(mid_prim, 2, 3, size_b - 3)
    low_side, high_side = ppm_faces(x_strip, 1)
    face_x = hlle_flux(slab_of(high_side, 1, 0, size_a - 5), slab_of(low_side, 1, 1, size_a - 4), 1)
    change_x = slab_of(face_x, 1, 1, size_a - 5) - slab_of(face_x, 1, 0, size_a - 6)
    y_strip = slab_of(mid_prim, 1, 3, size_a - 3)
    low_side, high_side = ppm_faces(y_strip, 2)
    face_y = hlle_flux(slab_of(high_side, 2, 0, size_b - 5), slab_of(low_side, 2, 1, size_b - 4), 2)
    change_y = slab_of(face_y, 2, 1, size_b - 5) - slab_of(face_y, 2, 0, size_b - 6)
    full_rate = time_step * slab_of(inv_cols, 0, 4, size_q - 4)
    return slab_of(slab_of(cons, 1, 4, size_p - 4), 2, 4, size_q - 4) - full_rate * (change_x + change_y)

def advance_group(windows, inv_cols, time_step):
    updated = advance(windows, inv_cols, time_step)
    extent = windows.shape[1]
    per_group = windows.shape[2] // extent
    padded = jnp.concatenate([updated, jnp.zeros((8, extent - 8, 8), jnp.float32)], axis=2)
    shaped = padded.reshape(8, extent - 8, per_group, extent)[:, :, :, :extent - 8]
    return shaped.reshape(8, extent - 8, per_group * (extent - 8))

def signal_rate(cons):
    prim = primitive(cons)
    return jnp.maximum(jnp.abs(prim[1]) + fast_speed(prim, 1), jnp.abs(prim[2]) + fast_speed(prim, 2))

def peak_rate(fields, weights):
    rates = signal_rate(fields)
    spread_weights = jnp.repeat(weights, BS)[None, :]
    return jnp.max(jnp.where(spread_weights > 0.0, rates * spread_weights, 0.0))

def restrict(grid):
    return (grid[:, 0::2, 0::2] + grid[:, 0::2, 1::2] + (grid[:, 1::2, 0::2] + grid[:, 1::2, 1::2])) * 0.25

def assemble(fields, refined, tiles_x, tiles_y):
    blocks = fields.reshape(8, BS, tiles_x, tiles_y, RD * RD, 2, 2, BS)
    inverse = np.argsort(morton_table(RD)).astype(np.int32)
    blocks = jnp.take(blocks, jnp.asarray(inverse), axis=4).reshape(8, BS, tiles_x, tiles_y, RD, RD, 2, 2, BS)
    fine_part = blocks.transpose(0, 2, 4, 7, 1, 3, 5, 6, 8).reshape(8, tiles_x * RD * 2 * BS, tiles_y * RD * 2 * BS)
    coarse_part = blocks[:, :, :, :, :, :, 0, 0, :].transpose(0, 2, 4, 1, 3, 5, 6).reshape(8, tiles_x * RD * BS, tiles_y * RD * BS)
    injected = jnp.repeat(jnp.repeat(coarse_part, 2, axis=1), 2, axis=2)
    refined_mask = jnp.repeat(jnp.repeat(refined, 2 * BS, axis=0), 2 * BS, axis=1)
    return jnp.where(refined_mask[None] > 0, fine_part, injected)

def block_table(refined, tiles_x, tiles_y):
    grid = refined.reshape(tiles_x, RD, tiles_y, RD).transpose(0, 2, 1, 3).reshape(tiles_x * tiles_y, RD * RD)
    roots = jnp.take(grid, jnp.asarray(morton_table(RD)), axis=1)
    fine_slots = jnp.repeat(roots, 4, axis=1) > 0
    child_index = jnp.tile(jnp.arange(4, dtype=jnp.int32), RD * RD)
    live = fine_slots | (child_index[None, :] == 0)
    return (live, fine_slots)

def placement_of(slot_ids, tile_y_count):
    slot_total = 4 * RD * RD
    tile_index = slot_ids // slot_total
    slot_index = slot_ids % slot_total
    root_index = slot_index // 4
    child_index = slot_index % 4
    grid_x = tile_index // tile_y_count
    grid_y = tile_index % tile_y_count
    row_major = jnp.asarray(morton_table(RD))[root_index]
    root_x = grid_x * RD + row_major // RD
    root_y = grid_y * RD + row_major % RD
    fine_row = (root_x * 2 * BS + child_index % 2 * BS).astype(jnp.int32)
    fine_col = (root_y * 2 * BS + child_index // 2 * BS).astype(jnp.int32)
    coarse_row = (root_x * BS).astype(jnp.int32)
    coarse_col = (root_y * BS).astype(jnp.int32)
    return (fine_row, fine_col, coarse_row, coarse_col)

def cut_windows(fine_pad, coarse_pad, is_fine, fine_row, fine_col, coarse_row, coarse_col):
    extent = BS + 8

    def one_window(flag_value, row_fine, col_fine, row_coarse, col_coarse):
        anchor = jnp.zeros((), jnp.int32)
        fine_win = lax.dynamic_slice(fine_pad, (anchor, row_fine, col_fine), (8, extent, extent))
        coarse_win = lax.dynamic_slice(coarse_pad, (anchor, row_coarse, col_coarse), (8, extent, extent))
        return jnp.where(flag_value, fine_win, coarse_win)
    window_set = jax.vmap(one_window)(is_fine, fine_row, fine_col, coarse_row, coarse_col)
    block_count = is_fine.shape[0]
    return window_set.transpose(1, 2, 0, 3).reshape(8, extent, block_count * extent)

def reference(fields, refined):
    tiles_x = N_GX
    tiles_y = N_GY
    fine_grid = assemble(fields, refined, tiles_x, tiles_y)
    fine_pad = jnp.pad(fine_grid, ((0, 0), (4, 4), (4, 4)), mode='wrap')
    coarse_pad = jnp.pad(restrict(fine_grid), ((0, 0), (4, 4), (4, 4)), mode='wrap')
    live, fine_slots = block_table(refined, tiles_x, tiles_y)
    live = live.reshape(-1)
    fine_slots = fine_slots.reshape(-1)
    slot_count = live.shape[0]
    total_blocks = CAP * tiles_x * tiles_y
    position = jnp.cumsum(live.astype(jnp.int32)) - 1
    target = jnp.where(live, position, total_blocks).astype(jnp.int32)
    block_order = jnp.zeros((total_blocks,), jnp.int32).at[target].set(jnp.arange(slot_count, dtype=jnp.int32), mode='drop')
    weights = jnp.where(live, jnp.where(fine_slots, 1.0, 0.5), 0.0).astype(jnp.float32)
    time_step = COURANT / peak_rate(fields, weights)
    is_fine = fine_slots[block_order]
    fine_row, fine_col, coarse_row, coarse_col = placement_of(block_order, tiles_y)
    inv_width = jnp.where(is_fine, 1.0, 0.5).astype(jnp.float32)
    group_count = total_blocks // RD

    def run_group(payload):
        flags, rows_fine, cols_fine, rows_coarse, cols_coarse, inv_group = payload
        windows = cut_windows(fine_pad, coarse_pad, flags, rows_fine, cols_fine, rows_coarse, cols_coarse)
        return advance_group(windows, jnp.repeat(inv_group, BS + 8), time_step)
    payload = (is_fine.reshape(group_count, RD), fine_row.reshape(group_count, RD), fine_col.reshape(group_count, RD), coarse_row.reshape(group_count, RD), coarse_col.reshape(group_count, RD), inv_width.reshape(group_count, RD))
    results = lax.map(run_group, payload)
    return results.transpose(1, 2, 0, 3).reshape(8, BS, total_blocks * BS)
```

```python
import functools

import jax
import jax.numpy as jnp
from jax import lax
from jax.experimental import pallas as pl
from jax.experimental.pallas import tpu as pltpu
from jax.sharding import PartitionSpec as P

BS = 32
CAP = 10
EXT = BS + 8
GAMMA = 5.0 / 3.0
COURANT = 0.2
MESH = pl.DeviceIdType.MESH
F32 = jnp.float32

BASE = (4, 140, 276)
PAD_ROWS = 352
ROWS = (0, 8, 16, 24, 32)
FACE1 = (0, 8, 16, 24, 31)
MID = (1, 9, 17, 25, 31)
SLOPE = (2, 10, 18, 26, 29)
FACE2 = (3, 11, 19, 27, 28)
LAST = (4, 12, 20, 28)


def lanes(rows):
    return lax.broadcasted_iota(jnp.int32, (rows, 128), 1)


def roll(x, by):
    if isinstance(by, int):
        by = by % 128
        return x if by == 0 else pltpu.roll(x, by, 1)
    return pltpu.roll(x, lax.rem(by + 256, 128), 1)


def recip(x):
    r = pltpu.reciprocal(x, approx=True)
    return r * (2.0 - x * r)


def root(x):
    return x * lax.rsqrt(jnp.maximum(x, 1e-30))


def limited(value, other):
    return jnp.minimum(jnp.maximum(value, jnp.minimum(other, 0.0)), jnp.maximum(other, 0.0))


def primitive(u):
    rho, mx, my, mz, energy, bx, by, bz = u
    inv = recip(rho)
    vx, vy, vz = mx * inv, my * inv, mz * inv
    half_b2 = 0.5 * (bx * bx + by * by + bz * bz)
    kinetic = 0.5 * (mx * vx + my * vy + mz * vz)
    pressure = (GAMMA - 1.0) * (energy - kinetic - half_b2)
    return inv, vx, vy, vz, pressure, half_b2


def fast_pair(inv, pressure, half_b2, trans_x, trans_y):
    sound = GAMMA * pressure * inv
    alfven = 2.0 * half_b2 * inv
    total = sound + alfven
    diff = sound - alfven
    square = diff * diff
    four = 4.0 * sound * inv
    fast_x = root(0.5 * (total + root(square + four * trans_x)))
    fast_y = root(0.5 * (total + root(square + four * trans_y)))
    return fast_x, fast_y


def cell_state(u):
    rho, mx, my, mz, energy, bx, by, bz = u
    inv, vx, vy, vz, pressure, half_b2 = primitive(u)
    xx, yy, zz = bx * bx, by * by, bz * bz
    fast_x, fast_y = fast_pair(inv, pressure, half_b2, yy + zz, xx + zz)
    total_p = pressure + half_b2
    enthalpy = energy + total_p
    vb = vx * bx + vy * by + vz * bz
    cross = mx * vy - bx * by
    emf = by * vx - bx * vy
    flux_x = (mx * vx + total_p - xx, cross, mx * vz - bx * bz, enthalpy * vx - bx * vb, emf, bz * vx - bx * vz)
    flux_y = (cross, my * vy + total_p - yy, my * vz - by * bz, enthalpy * vy - by * vb, -emf, bz * vy - by * vz)
    return flux_x, (vx - fast_x, vx + fast_x), flux_y, (vy - fast_y, vy + fast_y)


def edge_weights(slow_l, fast_l, slow_r, fast_r):
    slow = jnp.minimum(jnp.minimum(slow_l, slow_r), 0.0)
    fast = jnp.maximum(jnp.maximum(fast_l, fast_r), 0.0)
    inv = recip(fast - slow)
    a = fast * inv
    b = -slow * inv
    return slow, fast, a, b, slow * a


def side(w, normal):
    rho, vx, vy, vz, pressure, bx, by, bz = w
    vn, vt, bn, bt = (vx, vy, bx, by) if normal == 1 else (vy, vx, by, bx)
    inv = recip(rho)
    trans = bt * bt + bz * bz
    nn = bn * bn
    b2 = trans + nn
    sound = GAMMA * pressure * inv
    alfven = b2 * inv
    diff = sound - alfven
    fast = root(0.5 * (sound + alfven + root(diff * diff + 4.0 * sound * inv * trans)))
    half_b2 = 0.5 * b2
    total_p = pressure + half_b2
    energy = 1.5 * pressure + half_b2 + 0.5 * rho * (vn * vn + vt * vt + vz * vz)
    vb = vn * bn + vt * bt + vz * bz
    return vn - fast, vn + fast, (rho, vn, vt, vz, bn, bt, bz, energy, total_p, total_p - nn, vb)


def moved(state, speed):
    rho, vn, vt, vz, bn, bt, bz, energy, total_p, stress, vb = state
    rel = vn - speed
    mass = rho * rel
    return (
        mass,
        mass * vn + stress,
        mass * vt - bn * bt,
        mass * vz - bn * bz,
        energy * rel + total_p * vn - bn * vb,
        bt * rel - bn * vt,
        bz * rel - bn * vz,
    )


def face_flux(left, right, normal):
    slow_l, fast_l, state_l = side(left, normal)
    slow_r, fast_r, state_r = side(right, normal)
    slow, fast, a, b, c = edge_weights(slow_l, fast_l, slow_r, fast_r)
    from_l = moved(state_l, slow)
    from_r = moved(state_r, fast)
    mass, mn, mt, mz, en, bt, bz = (a * p + b * q for p, q in zip(from_l, from_r))
    bn = c * (state_r[4] - state_l[4])
    if normal == 1:
        return (mass, mn, mt, mz, en, bn, bt, bz)
    return (mass, mt, mn, mz, en, bt, bn, bz)


def kernel(ngx, ngy, ref_s, ref_v, fields, out, *scratch):
    (X, F, C, G, U, ML, MR, RL, RR, SR, RB, SK, RK, SY, RY, VM, P1, P2, SX, GX, DY, W, RA, EA, GX2, O, in_sem, send, recv) = scratch
    gx = lax.axis_index("gx")
    gy = lax.axis_index("gy")
    me = gx * ngy + gy
    load = pltpu.make_async_copy(fields, X, in_sem)
    load.start()

    def at(dx, dy):
        return lax.rem(gx + dx + ngx, ngx), lax.rem(gy + dy + ngy, ngy)

    partners = [at(0, s) for s in range(1, ngy)] + [at(s, 0) for s in range(1, ngx)]
    partners += [at(1, 1), at(1, -1), at(-1, 1), at(-1, -1)]
    barrier = pltpu.get_barrier_semaphore()
    for who in partners:
        pl.semaphore_signal(barrier, inc=1, device_id=who, device_id_type=MESH)

    sems = iter(range(64))

    def remote(src, dst, who):
        i = next(sems)
        return pltpu.make_async_remote_copy(
            src_ref=src, dst_ref=dst, send_sem=send.at[i], recv_sem=recv.at[i], device_id=who, device_id_type=MESH
        )

    def flags_of(tile):
        tx, ty = lax.div(tile, ngy), lax.rem(tile, ngy)
        return [ref_s[2 * tx + r // 2, 2 * ty + r % 2] for r in range(4)]

    tile_of = lax.broadcasted_iota(jnp.int32, (2 * ngx, 2 * ngy), 0) // 2 * ngy
    tile_of = tile_of + lax.broadcasted_iota(jnp.int32, (2 * ngx, 2 * ngy), 1) // 2
    before = jnp.sum(jnp.where(tile_of < me, ref_v[...], 0))
    excess = 4 * me + 3 * before - CAP * me
    mine = flags_of(me)
    prev = flags_of(lax.rem(me + ngx * ngy - 1, ngx * ngy))
    following = flags_of(lax.rem(me + 1, ngx * ngy))

    def count_of(fl):
        return 4 + 3 * (fl[0] + fl[1] + fl[2] + fl[3])

    count = count_of(mine)

    def ge(a, b):
        return jnp.where(a >= b, 1, 0)

    def find(index, fl):
        index = jnp.clip(index, 0, count_of(fl) - 1)
        p1 = 1 + 3 * fl[0]
        p2 = p1 + 1 + 3 * fl[1]
        p3 = p2 + 1 + 3 * fl[2]
        a1, a2, a3 = ge(index, p1), ge(index, p2), ge(index, p3)
        child = index - (a1 * p1 + a2 * (p2 - p1) + a3 * (p3 - p2))
        flag = fl[0] + a1 * (fl[1] - fl[0]) + a2 * (fl[2] - fl[1]) + a3 * (fl[3] - fl[2])
        rx = a2
        ry = a1 + a2 + a3 - 2 * rx
        cx, cy = child & 1, child >> 1
        row = flag * (BASE[0] + 136 * ry + 64 * rx + 32 * cx) + (1 - flag) * (BASE[2] + 32 * rx)
        lane = 32 * (flag * cy + (1 - flag) * ry)
        return row, lane, flag

    place = {w: find(w - excess, mine) for w in range(-3, 13)}
    wide = {}
    for w in range(CAP):
        flag = place[w][2]
        index = w - excess
        if w < 3:
            flag = jnp.where(index >= 0, flag, find(index + count_of(prev), prev)[2])
        if w >= 7:
            flag = jnp.where(index < count, flag, find(index - count, following)[2])
        wide[w] = 0.5 + 0.5 * flag.astype(F32)

    lane8, lane32, lane40 = lanes(8), lanes(32), lanes(EXT)
    load.wait()

    def build(c, carry):
        for rx in range(2):
            a = X[c, :, 256 * rx : 256 * rx + 128]
            b = X[c, :, 256 * rx + 128 : 256 * rx + 256]
            a32, a64, b64, b32 = roll(a, -32), roll(a, -64), roll(b, 64), roll(b, 32)
            top = jnp.where(lane32 < 32, a, jnp.where(lane32 < 64, a32, jnp.where(lane32 < 96, b64, b32)))
            low = jnp.where(lane32 < 32, a32, jnp.where(lane32 < 64, a64, jnp.where(lane32 < 96, b32, b)))
            z = jnp.where(lane32 < 32, a, b32)
            z = jnp.take_along_axis(z, lane32 // 2, axis=1)
            F[c, pl.ds(64 * rx, 32, stride=2), :] = z
            F[c, pl.ds(64 * rx + 1, 32, stride=2), :] = z
            keep = jnp.where(lane32 < 64, mine[2 * rx], mine[2 * rx + 1]) > 0
            F[c, 64 * rx : 64 * rx + 32, :] = jnp.where(keep, top, F[c, 64 * rx : 64 * rx + 32, :])
            F[c, 64 * rx + 32 : 64 * rx + 64, :] = jnp.where(keep, low, F[c, 64 * rx + 32 : 64 * rx + 64, :])
        for rx in range(2):
            s = F[c, pl.ds(64 * rx, 32, stride=2), :] + F[c, pl.ds(64 * rx + 1, 32, stride=2), :]
            s = (s + roll(s, -1)) * 0.25
            C[c, 32 * rx : 32 * rx + 32, :] = jnp.take_along_axis(s, lane32 * 2 % 128, axis=1)
        SR[0, c, 0:4, :] = F[c, 124:128, :]
        SR[0, c, 4:8, :] = C[c, 60:64, :]
        SR[1, c, 0:4, :] = F[c, 0:4, :]
        SR[1, c, 4:8, :] = C[c, 0:4, :]
        return carry

    lax.fori_loop(0, 8, build, 0)

    def corners(c, carry):
        s = 8 * c + 4
        inside = (lane8 >= s - 4) & (lane8 < s + 4)
        return tuple(jnp.where(inside, roll(SR[d, c], s), carry[d]) for d in range(2))

    zero8 = jnp.zeros((8, 128), F32)
    down, up = lax.fori_loop(0, 8, corners, (zero8, zero8))
    SK[0] = down
    SK[1] = up

    def columns(h, carry):
        for q in range(4):
            acc_r, acc_l = zero8, zero8
            for cc in range(4):
                for k in range(6):
                    s = 32 * cc + 4 * k + 4
                    source = F if k < 4 else C
                    row = 32 * (k if k < 4 else k - 4) + 8 * q
                    x = roll(source[4 * h + cc, row : row + 8, :], s)
                    acc_r = jnp.where((lane8 >= s - 4) & (lane8 < s), x, acc_r)
                    acc_l = jnp.where((lane8 >= s) & (lane8 < s + 4), x, acc_l)
            SY[0, h, 8 * q : 8 * q + 8, :] = acc_r
            SY[1, h, 8 * q : 8 * q + 8, :] = acc_l
        return carry

    lax.fori_loop(0, 2, columns, 0)

    ghosts = [
        remote(SY.at[0], RY.at[0], at(0, 1)),
        remote(SY.at[1], RY.at[1], at(0, -1)),
        remote(SR.at[0], RB.at[0], at(1, 0)),
        remote(SR.at[1], RB.at[1], at(-1, 0)),
        remote(SK.at[0], RK.at[0], at(1, 1)),
        remote(SK.at[0], RK.at[1], at(1, -1)),
        remote(SK.at[1], RK.at[2], at(-1, 1)),
        remote(SK.at[1], RK.at[3], at(-1, -1)),
    ]
    pl.semaphore_wait(barrier, len(partners))
    for copy in ghosts:
        copy.start()

    peak = zero8
    for r in range(4):
        on = mine[r] > 0
        weight = jnp.where(lane8 < 32, jnp.where(on, 1.0, 0.5), jnp.where(on, 1.0, 0.0)).astype(F32)
        for q in range(4):
            u = [X[c, 8 * q : 8 * q + 8, 128 * r : 128 * r + 128] for c in range(8)]
            inv, vx, vy, vz, pressure, half_b2 = primitive(u)
            xx, yy, zz = (b * b for b in u[5:])
            fast_x, fast_y = fast_pair(inv, pressure, half_b2, yy + zz, xx + zz)
            rate = jnp.maximum(jnp.abs(vx) + fast_x, jnp.abs(vy) + fast_y)
            peak = jnp.maximum(peak, jnp.where(weight > 0.0, rate * weight, 0.0))
    VM[0] = peak
    round1 = [remote(VM.at[0], P1.at[s - 1], at(0, s)) for s in range(1, ngy)]
    for copy in round1:
        copy.start()

    for copy in ghosts:
        copy.wait_recv()

    def fill(h, carry):
        for cc in range(4):
            c = 4 * h + cc
            for d in range(2):
                from_l = roll(RK[2 * d], -8 * c)
                from_r = roll(RK[2 * d + 1], 64 - 8 * c)
                row = RB[d, c]
                row4, row60 = roll(row, 4), roll(row, -60)
                start = [b + (0, 132)[d] for b in BASE[:2]] + [BASE[2] + (0, 68)[d]]
                G[c, start[0] : start[0] + 4, :] = jnp.where(lane8 < 4, from_l, row4)[0:4]
                G[c, start[1] : start[1] + 4, :] = jnp.where(lane8 < 68, row60, from_r)[0:4]
                G[c, start[2] : start[2] + 4, :] = jnp.where(lane8 < 4, from_l, jnp.where(lane8 < 68, row4, from_r))[4:8]
            for k in range(6):
                s = 32 * cc + 4 * k
                from_l = roll(RY[0, h], -s)
                from_r = roll(RY[1, h], 64 - s)
                if k < 4:
                    x = F[c, 32 * k : 32 * k + 32, :]
                    row = BASE[0] + 4 + 32 * k
                    G[c, row : row + 32, :] = jnp.where(lane32 < 4, from_l, roll(x, 4))
                    row = BASE[1] + 4 + 32 * k
                    G[c, row : row + 32, :] = jnp.where(lane32 < 68, roll(x, -60), from_r)
                else:
                    x = C[c, 32 * (k - 4) : 32 * (k - 4) + 32, :]
                    row = BASE[2] + 4 + 32 * (k - 4)
                    G[c, row : row + 32, :] = jnp.where(lane32 < 4, from_l, jnp.where(lane32 < 68, roll(x, 4), from_r))
        return carry

    lax.fori_loop(0, 2, fill, 0)

    def gather(dst, which):
        def body(c, carry):
            parts = [roll(G[c, pl.ds(place[w][0], EXT), :], EXT * g - place[w][1]) for g, w in enumerate(which)]
            x = parts[0]
            for g, part in enumerate(parts[1:]):
                x = jnp.where(lane40 < EXT * (g + 1), x, part)
            dst[c] = x
            return carry

        lax.fori_loop(0, 8, body, 0)

    gather(MR, (10, 11, 12))
    gather(ML, (-3, -2, -1))
    carry_up = lax.div(gy + 1, ngy)
    carry_down = lax.div(ngy - gy, ngy)
    ahead = (lax.rem(gx + carry_up, ngx), lax.rem(gy + 1, ngy))
    behind = (lax.rem(gx + ngx - carry_down, ngx), lax.rem(gy + ngy - 1, ngy))
    moves = [remote(MR, RL, ahead), remote(ML, RR, behind)]
    for copy in moves:
        copy.start()

    for copy in round1:
        copy.wait_recv()
    for s in range(ngy - 1):
        peak = jnp.maximum(peak, P1[s])
    VM[1] = peak
    round2 = [remote(VM.at[1], P2.at[s - 1], at(s, 0)) for s in range(1, ngx)]
    for copy in round2:
        copy.start()

    gather(U.at[0], (3, 4, 5))
    gather(U.at[1], (6,))
    gather(U.at[2], (0, 1, 2))
    gather(U.at[3], (7, 8, 9))

    def first(t, carry):
        for r in ROWS:
            u = [U[t, c, r : r + 8, :] for c in range(8)]
            flux_x, edge_x, flux_y, edge_y = cell_state(u)
            for i, v in enumerate(flux_x + edge_x):
                SX[i, r : r + 8, :] = v
            _, _, a, b, w = edge_weights(*edge_y, roll(edge_y[0], -1), roll(edge_y[1], -1))
            cell = (u[2],) + flux_y[:5] + (None,) + flux_y[5:]
            for c in range(8):
                jump = w * (roll(u[c], -1) - u[c])
                flux = jump if cell[c] is None else a * cell[c] + b * roll(cell[c], -1) + jump
                DY[t, c, r : r + 8, :] = flux - roll(flux, 1)
        for r in FACE1:
            edges = [SX[i, r + d : r + d + 8, :] for d in range(2) for i in (6, 7)]
            _, _, a, b, w = edge_weights(*edges)
            for c in range(8):
                low, high = U[t, c, r : r + 8, :], U[t, c, r + 1 : r + 9, :]
                flux = w * (high - low)
                if c == 0:
                    flux = a * U[t, 1, r : r + 8, :] + b * U[t, 1, r + 1 : r + 9, :] + flux
                elif c != 5:
                    i = c - 1 if c < 5 else c - 2
                    flux = a * SX[i, r : r + 8, :] + b * SX[i, r + 1 : r + 9, :] + flux
                GX[t, c, r : r + 8, :] = flux
        return carry

    lax.fori_loop(0, 2, first, 0)

    for copy in moves:
        copy.wait_recv()

    def merge(c, carry):
        U[2, c] = jnp.where(lane40 // EXT < excess, RL[c], U[2, c])
        U[3, c] = jnp.where(lane40 // EXT + 7 >= count + excess, RR[c], U[3, c])
        return carry

    lax.fori_loop(0, 8, merge, 0)
    lax.fori_loop(2, 4, first, 0)

    for copy in round2:
        copy.wait_recv()
    for s in range(ngx - 1):
        peak = jnp.maximum(peak, P2[s])
    peak = jnp.max(jnp.max(peak, axis=0, keepdims=True), axis=1, keepdims=True)
    time_step = COURANT / jnp.broadcast_to(peak, (8, 128))

    def widths(ws):
        v = jnp.full((8, 128), wide[ws[0]], F32)
        for g, w in enumerate(ws[1:]):
            v = jnp.where(lane8 < EXT * (g + 1), v, wide[w])
        return v

    VM[2] = time_step * widths((3, 4, 5))
    VM[3] = time_step * widths((6,))
    VM[4] = time_step * widths((0, 1, 2))
    VM[5] = time_step * widths((7, 8, 9))

    def second(t, carry):
        rate = VM[2 + t]
        half = 0.5 * rate
        for r in MID:
            u = []
            for c in range(8):
                change = GX[t, c, r : r + 8, :] - GX[t, c, r - 1 : r + 7, :] + DY[t, c, r : r + 8, :]
                u.append(U[t, c, r : r + 8, :] - half * change)
            _, vx, vy, vz, pressure, _ = primitive(u)
            for c, v in enumerate((u[0], vx, vy, vz, pressure, u[5], u[6], u[7])):
                W[c, r : r + 8, :] = v
        for r in SLOPE:
            for c in range(8):
                w = [W[c, r + d : r + d + 8, :] for d in (-1, 0, 1, 2)]
                low, d, high = w[1] - w[0], w[2] - w[1], w[3] - w[2]
                rise = limited(0.5 * d + (low - high) * (1.0 / 12.0), d)
                RA[c, r : r + 8, :] = rise
                EA[c, r : r + 8, :] = d - rise
        for r in FACE2:
            left, right = [], []
            for c in range(8):
                rise, rise_next = RA[c, r : r + 8, :], RA[c, r + 1 : r + 9, :]
                fall, fall_next = EA[c, r - 1 : r + 7, :], EA[c, r : r + 8, :]
                left.append(W[c, r : r + 8, :] + limited(rise, 2.0 * fall))
                right.append(W[c, r + 1 : r + 9, :] - limited(fall_next, 2.0 * rise_next))
            for c, v in enumerate(face_flux(left, right, 1)):
                GX2[c, r : r + 8, :] = v
        for r in LAST:
            left, right = [], []
            for c in range(8):
                w = W[c, r : r + 8, :]
                ahead_w = roll(w, -1)
                d = ahead_w - w
                rise = limited(0.5 * d + (roll(d, 1) - roll(d, -1)) * (1.0 / 12.0), d)
                fall = d - rise
                left.append(w + limited(rise, 2.0 * roll(fall, 1)))
                right.append(ahead_w - limited(fall, 2.0 * roll(rise, -1)))
            for c, v in enumerate(face_flux(left, right, 2)):
                change = GX2[c, r : r + 8, :] - GX2[c, r - 1 : r + 7, :] + (v - roll(v, 1))
                O[t, c, r - 4 : r + 4, :] = U[t, c, r : r + 8, :] - rate * change
        return carry

    lax.fori_loop(0, 4, second, 0)

    def finish(c, carry):
        o = [O[t, c] for t in range(4)]
        o0 = jnp.where(lane32 < 32, roll(o[2], -4), jnp.where(lane32 < 64, roll(o[2], -12), roll(o[2], -20)))
        out[c, :, 0:128] = jnp.where(lane32 < 96, o0, roll(o[0], 92))
        o1 = jnp.where(lane32 < 32, roll(o[0], -44), roll(o[0], -52))
        out[c, :, 128:256] = jnp.where(lane32 < 64, o1, jnp.where(lane32 < 96, roll(o[1], 60), roll(o[3], 92)))
        o2 = jnp.where(lane32 < 32, roll(o[3], -44), roll(o[3], -52))
        out[c, :, 256:320] = o2[:, 0:64]
        return carry

    lax.fori_loop(0, 8, finish, 0)

    for copy in ghosts + moves + round1 + round2:
        copy.wait_send()


def shards(ngx, ngy, fields, refined):
    vmem = lambda *shape: pltpu.VMEM(shape, F32)
    scratch = [
        vmem(8, 32, 512),
        vmem(8, 128, 128),
        vmem(8, 64, 128),
        vmem(8, PAD_ROWS, 128),
        vmem(4, 8, EXT, 128),
        vmem(8, EXT, 128),
        vmem(8, EXT, 128),
        vmem(8, EXT, 128),
        vmem(8, EXT, 128),
        vmem(2, 8, 8, 128),
        vmem(2, 8, 8, 128),
        vmem(2, 8, 128),
        vmem(4, 8, 128),
        vmem(2, 2, 32, 128),
        vmem(2, 2, 32, 128),
        vmem(6, 8, 128),
        vmem(ngy - 1, 8, 128),
        vmem(ngx - 1, 8, 128),
        vmem(8, EXT, 128),
        vmem(4, 8, EXT, 128),
        vmem(4, 8, EXT, 128),
        vmem(8, EXT, 128),
        vmem(8, EXT, 128),
        vmem(8, EXT, 128),
        vmem(8, EXT, 128),
        vmem(4, 8, BS, 128),
        pltpu.SemaphoreType.DMA,
        pltpu.SemaphoreType.DMA((ngx + ngy + 8,)),
        pltpu.SemaphoreType.DMA((ngx + ngy + 8,)),
    ]
    return pl.pallas_call(
        functools.partial(kernel, ngx, ngy),
        out_shape=jax.ShapeDtypeStruct((8, BS, CAP * BS), F32),
        in_specs=[
            pl.BlockSpec(memory_space=pltpu.SMEM),
            pl.BlockSpec(memory_space=pltpu.VMEM),
            pl.BlockSpec(memory_space=pl.ANY),
        ],
        out_specs=pl.BlockSpec(memory_space=pltpu.VMEM),
        scratch_shapes=scratch,
        compiler_params=pltpu.CompilerParams(
            collective_id=0, has_side_effects=True, vmem_limit_bytes=32 * 1024 * 1024
        ),
    )(refined, refined, fields)


def solution(mesh):
    ngx, ngy = mesh.shape["gx"], mesh.shape["gy"]
    return jax.shard_map(
        functools.partial(shards, ngx, ngy),
        mesh=mesh,
        in_specs=(P(None, None, ("gx", "gy")), P()),
        out_specs=P(None, None, ("gx", "gy")),
        check_vma=False,
    )
```

```python
import functools

import jax
import jax.numpy as jnp
from jax import lax
from jax.experimental import pallas as pl
from jax.experimental.pallas import tpu as pltpu
from jax.sharding import PartitionSpec as P

BS = 32
CAP = 10
EXT = BS + 8
GAMMA = 5.0 / 3.0
COURANT = 0.2
MESH = pl.DeviceIdType.MESH
F32 = jnp.float32

FINE = (4, 140)
COARSE = (276, 348)
PAD_ROWS = 424
ROWS = (0, 8, 16, 24, 32)
FACE1 = (0, 8, 16, 24, 31)
MID = (1, 9, 17, 25, 31)
SLOPE = (2, 10, 18, 26, 29)
FACE2 = (3, 11, 19, 27, 28)
LAST = (4, 12, 20, 28)


def lanes(rows):
    return lax.broadcasted_iota(jnp.int32, (rows, 128), 1)


def roll(x, by):
    if isinstance(by, int):
        by = by % 128
        return x if by == 0 else pltpu.roll(x, by, 1)
    return pltpu.roll(x, lax.rem(by + 256, 128), 1)


def recip(x):
    r = pltpu.reciprocal(x, approx=True)
    return r * (2.0 - x * r)


def root(x):
    return x * lax.rsqrt(jnp.maximum(x, 1e-30))


def limited(value, other):
    return jnp.minimum(jnp.maximum(value, jnp.minimum(other, 0.0)), jnp.maximum(other, 0.0))


def primitive(u):
    rho, mx, my, mz, energy, bx, by, bz = u
    inv = recip(rho)
    vx, vy, vz = mx * inv, my * inv, mz * inv
    half_b2 = 0.5 * (bx * bx + by * by + bz * bz)
    kinetic = 0.5 * (mx * vx + my * vy + mz * vz)
    pressure = (GAMMA - 1.0) * (energy - kinetic - half_b2)
    return inv, vx, vy, vz, pressure, half_b2


def fast_pair(inv, pressure, half_b2, trans_x, trans_y):
    sound = GAMMA * pressure * inv
    alfven = 2.0 * half_b2 * inv
    total = sound + alfven
    diff = sound - alfven
    square = diff * diff
    four = 4.0 * sound * inv
    fast_x = root(0.5 * (total + root(square + four * trans_x)))
    fast_y = root(0.5 * (total + root(square + four * trans_y)))
    return fast_x, fast_y


def cell_state(u):
    rho, mx, my, mz, energy, bx, by, bz = u
    inv, vx, vy, vz, pressure, half_b2 = primitive(u)
    xx, yy, zz = bx * bx, by * by, bz * bz
    fast_x, fast_y = fast_pair(inv, pressure, half_b2, yy + zz, xx + zz)
    total_p = pressure + half_b2
    enthalpy = energy + total_p
    vb = vx * bx + vy * by + vz * bz
    cross = mx * vy - bx * by
    emf = by * vx - bx * vy
    flux_x = (mx * vx + total_p - xx, cross, mx * vz - bx * bz, enthalpy * vx - bx * vb, emf, bz * vx - bx * vz)
    flux_y = (cross, my * vy + total_p - yy, my * vz - by * bz, enthalpy * vy - by * vb, -emf, bz * vy - by * vz)
    return flux_x, (vx - fast_x, vx + fast_x), flux_y, (vy - fast_y, vy + fast_y)


def edge_weights(slow_l, fast_l, slow_r, fast_r):
    slow = jnp.minimum(jnp.minimum(slow_l, slow_r), 0.0)
    fast = jnp.maximum(jnp.maximum(fast_l, fast_r), 0.0)
    inv = recip(fast - slow)
    a = fast * inv
    b = -slow * inv
    return slow, fast, a, b, slow * a


def side(w, normal):
    rho, vx, vy, vz, pressure, bx, by, bz = w
    vn, vt, bn, bt = (vx, vy, bx, by) if normal == 1 else (vy, vx, by, bx)
    inv = recip(rho)
    trans = bt * bt + bz * bz
    nn = bn * bn
    b2 = trans + nn
    sound = GAMMA * pressure * inv
    alfven = b2 * inv
    diff = sound - alfven
    fast = root(0.5 * (sound + alfven + root(diff * diff + 4.0 * sound * inv * trans)))
    half_b2 = 0.5 * b2
    total_p = pressure + half_b2
    energy = 1.5 * pressure + half_b2 + 0.5 * rho * (vn * vn + vt * vt + vz * vz)
    vb = vn * bn + vt * bt + vz * bz
    return vn - fast, vn + fast, (rho, vn, vt, vz, bn, bt, bz, energy, total_p, total_p - nn, vb)


def moved(state, speed):
    rho, vn, vt, vz, bn, bt, bz, energy, total_p, stress, vb = state
    rel = vn - speed
    mass = rho * rel
    return (
        mass,
        mass * vn + stress,
        mass * vt - bn * bt,
        mass * vz - bn * bz,
        energy * rel + total_p * vn - bn * vb,
        bt * rel - bn * vt,
        bz * rel - bn * vz,
    )


def face_flux(left, right, normal):
    slow_l, fast_l, state_l = side(left, normal)
    slow_r, fast_r, state_r = side(right, normal)
    slow, fast, a, b, c = edge_weights(slow_l, fast_l, slow_r, fast_r)
    from_l = moved(state_l, slow)
    from_r = moved(state_r, fast)
    mass, mn, mt, mz, en, bt, bz = (a * p + b * q for p, q in zip(from_l, from_r))
    bn = c * (state_r[4] - state_l[4])
    if normal == 1:
        return (mass, mn, mt, mz, en, bn, bt, bz)
    return (mass, mt, mn, mz, en, bt, bn, bz)


def kernel(ngx, ngy, refined, fields, out, *scratch):
    (ref_s, ref_v, X, J, G, U, ML, MR, SR, RB, SK, RK, SY, RY, VM, P1, P2, SX, GX, DY, W, RA, EA, GX2, O, in_sem, send, recv) = scratch
    gx = lax.axis_index("gx")
    gy = lax.axis_index("gy")
    me = gx * ngy + gy
    load = pltpu.make_async_copy(fields, X, in_sem.at[0])
    load.start()
    load_s = pltpu.make_async_copy(refined, ref_s, in_sem.at[1])
    load_s.start()
    load_v = pltpu.make_async_copy(refined, ref_v, in_sem.at[2])
    load_v.start()

    def at(dx, dy):
        return lax.rem(gx + dx + ngx, ngx), lax.rem(gy + dy + ngy, ngy)

    partners = [at(0, s) for s in range(1, ngy)] + [at(s, 0) for s in range(1, ngx)]
    partners += [at(1, 1), at(1, -1), at(-1, 1), at(-1, -1)]
    barrier = pltpu.get_barrier_semaphore()
    for who in partners:
        pl.semaphore_signal(barrier, inc=1, device_id=who, device_id_type=MESH)

    sems = iter(range(64))

    def remote(src, dst, who):
        i = next(sems)
        return pltpu.make_async_remote_copy(
            src_ref=src, dst_ref=dst, send_sem=send.at[i], recv_sem=recv.at[i], device_id=who, device_id_type=MESH
        )

    def flags_of(tile):
        tx, ty = lax.div(tile, ngy), lax.rem(tile, ngy)
        return [ref_s[2 * ty + r % 2, 2 * tx + r // 2] for r in range(4)]

    load_s.wait()
    mine = flags_of(me)
    lane8, lane32, lane40 = lanes(8), lanes(32), lanes(EXT)
    load.wait()

    zero8 = jnp.zeros((8, 128), F32)
    peak = zero8
    for r in range(4):
        on = mine[r] > 0
        weight = jnp.where(lane8 < 32, jnp.where(on, 1.0, 0.5), jnp.where(on, 1.0, 0.0)).astype(F32)
        for q in range(4):
            u = [X[c, 8 * q : 8 * q + 8, 128 * r : 128 * r + 128] for c in range(8)]
            inv, vx, vy, vz, pressure, half_b2 = primitive(u)
            xx, yy, zz = (b * b for b in u[5:])
            fast_x, fast_y = fast_pair(inv, pressure, half_b2, yy + zz, xx + zz)
            rate = jnp.maximum(jnp.abs(vx) + fast_x, jnp.abs(vy) + fast_y)
            peak = jnp.maximum(peak, jnp.where(weight > 0.0, rate * weight, 0.0))
    VM[0] = peak
    round1 = [remote(VM.at[0], P1.at[s - 1], at(0, s)) for s in range(1, ngy)]
    pl.semaphore_wait(barrier, len(partners))
    for copy in round1:
        copy.start()

    turn_even = (lane32 - 4) % 128 // 2
    turn_half = (2 * ((lane32 - 4) % 64) + 4) % 128
    columns = (lane32 - 4) % 128
    first32, first64, first96 = columns < 32, columns < 64, columns < 96
    for c in range(8):
        for rx in range(2):
            a = X[c, :, 256 * rx : 256 * rx + 128]
            b = X[c, :, 256 * rx + 128 : 256 * rx + 256]
            a28, b36 = roll(a, -28), roll(b, 36)
            top = jnp.where(first32, roll(a, 4), jnp.where(first64, a28, jnp.where(first96, roll(b, 68), b36)))
            low = jnp.where(first32, a28, jnp.where(first64, roll(a, -60), jnp.where(first96, b36, roll(b, 4))))
            z = jnp.where(lane32 < 32, a, roll(b, 32))
            z = jnp.take_along_axis(z, turn_even, axis=1)
            J[c, rx, pl.ds(0, 32, stride=2), :] = z
            J[c, rx, pl.ds(1, 32, stride=2), :] = z
            keep = jnp.where(first64, mine[2 * rx], mine[2 * rx + 1]) > 0
            top = jnp.where(keep, top, J[c, rx, 0:32, :])
            low = jnp.where(keep, low, J[c, rx, 32:64, :])
            for base in FINE:
                row = base + 4 + 64 * rx
                G[c, row : row + 32, :] = top
                G[c, row + 32 : row + 64, :] = low
    for c in range(8):
        for rx in range(2):
            row = FINE[0] + 4 + 64 * rx
            x = G[c, pl.ds(row, 32, stride=2), :] + G[c, pl.ds(row + 1, 32, stride=2), :]
            x = (x + roll(x, -1)) * 0.25
            x = jnp.take_along_axis(x, turn_half, axis=1)
            for base in COARSE:
                G[c, base + 4 + 32 * rx : base + 36 + 32 * rx, :] = x

    for copy in round1:
        copy.wait_recv()
    for s in range(ngy - 1):
        peak = jnp.maximum(peak, P1[s])
    VM[1] = peak
    round2 = [remote(VM.at[1], P2.at[s - 1], at(s, 0)) for s in range(1, ngx)]
    for copy in round2:
        copy.start()

    for h in range(2):
        for q in range(4):
            acc_r, acc_l = zero8, zero8
            for cc in range(4):
                for k in range(6):
                    s = 32 * cc + 4 * k
                    row = (FINE[0] + 4 + 32 * k if k < 4 else COARSE[0] + 4 + 32 * (k - 4)) + 8 * q
                    x = roll(G[4 * h + cc, row : row + 8, :], s)
                    acc_r = jnp.where((lane8 >= s) & (lane8 < s + 4), x, acc_r)
                    acc_l = jnp.where((lane8 >= s + 4) & (lane8 < s + 8), x, acc_l)
            SY[0, h, 8 * q : 8 * q + 8, :] = acc_r
            SY[1, h, 8 * q : 8 * q + 8, :] = acc_l
    ghosts = [remote(SY.at[0], RY.at[0], at(0, 1)), remote(SY.at[1], RY.at[1], at(0, -1))]
    for copy in ghosts:
        copy.start()
    for d in range(2):
        corner = zero8
        fine, coarse = FINE[0] + 4 + (124, 0)[d], COARSE[0] + 4 + (60, 0)[d]
        for c in range(8):
            SR[d, c, 0:4, :] = G[c, fine : fine + 4, :]
            SR[d, c, 4:8, :] = G[c, coarse : coarse + 4, :]
            corner = jnp.where(lane8 // 8 == c, roll(SR[d, c], 8 * c), corner)
        SK[d] = corner
    edges = [
        remote(SR.at[0], RB.at[0], at(1, 0)),
        remote(SR.at[1], RB.at[1], at(-1, 0)),
        remote(SK.at[0], RK.at[0], at(1, 1)),
        remote(SK.at[0], RK.at[1], at(1, -1)),
        remote(SK.at[1], RK.at[2], at(-1, 1)),
        remote(SK.at[1], RK.at[3], at(-1, -1)),
    ]
    for copy in edges:
        copy.start()
    ghosts += edges

    load_v.wait()
    tile_of = lax.broadcasted_iota(jnp.int32, (2 * ngy, 2 * ngx), 1) // 2 * ngy
    tile_of = tile_of + lax.broadcasted_iota(jnp.int32, (2 * ngy, 2 * ngx), 0) // 2
    before = jnp.sum(jnp.where(tile_of < me, ref_v[...], 0))
    excess = 4 * me + 3 * before - CAP * me
    prev = flags_of(lax.rem(me + ngx * ngy - 1, ngx * ngy))
    following = flags_of(lax.rem(me + 1, ngx * ngy))

    def count_of(fl):
        return 4 + 3 * (fl[0] + fl[1] + fl[2] + fl[3])

    count = count_of(mine)

    def ge(a, b):
        return jnp.where(a >= b, 1, 0)

    def find(index, fl):
        index = jnp.clip(index, 0, count_of(fl) - 1)
        p1 = 1 + 3 * fl[0]
        p2 = p1 + 1 + 3 * fl[1]
        p3 = p2 + 1 + 3 * fl[2]
        a1, a2, a3 = ge(index, p1), ge(index, p2), ge(index, p3)
        child = index - (a1 * p1 + a2 * (p2 - p1) + a3 * (p3 - p2))
        flag = fl[0] + a1 * (fl[1] - fl[0]) + a2 * (fl[2] - fl[1]) + a3 * (fl[3] - fl[2])
        rx = a2
        ry = a1 + a2 + a3 - 2 * rx
        cx, cy = child & 1, child >> 1
        row = flag * (FINE[0] + 136 * ry + 64 * rx + 32 * cx) + (1 - flag) * (COARSE[0] + 72 * ry + 32 * rx)
        lane = flag * (64 * ry + 32 * cy) + (1 - flag) * 96 * ry
        return row, lane, flag

    place = {w: find(w - excess, mine) for w in range(-3, 13)}
    wide = {}
    for w in range(CAP):
        flag = place[w][2]
        index = w - excess
        if w < 3:
            flag = jnp.where(index >= 0, flag, find(index + count_of(prev), prev)[2])
        if w >= 7:
            flag = jnp.where(index < count, flag, find(index - count, following)[2])
        wide[w] = 0.5 + 0.5 * flag.astype(F32)

    for copy in ghosts:
        copy.wait_recv()
    left8, right8 = lane8 < 4, (lane8 >= 4) & (lane8 < 8)
    left32, right32 = lane32 < 4, (lane32 >= 4) & (lane32 < 8)
    for d in range(2):
        corner = jnp.where(lane8 % 8 < 4, RK[2 * d], RK[2 * d + 1])
        for c in range(8):
            piece = roll(corner, -8 * c)
            row = RB[d, c]
            for i, mask in enumerate((left8, right8)):
                x = jnp.where(mask, piece, row)
                fine, coarse = FINE[i] + 132 * d, COARSE[i] + 68 * d
                G[c, fine : fine + 4, :] = x[0:4]
                G[c, coarse : coarse + 4, :] = x[4:8]
    for h in range(2):
        low4 = lane32 % 8 < 4
        pair = (jnp.where(low4, RY[0, h], RY[1, h]), jnp.where(low4, RY[1, h], RY[0, h]))
        for cc in range(4):
            for k in range(6):
                x = roll(pair[k % 2], -(32 * cc + 4 * k))
                for i, mask in enumerate((left32, right32)):
                    row = FINE[i] + 4 + 32 * k if k < 4 else COARSE[i] + 4 + 32 * (k - 4)
                    pltpu.store(G.at[4 * h + cc, pl.ds(row, 32), :], x, mask=mask)

    def gather(dst, which):
        for c in range(8):
            parts = [roll(G[c, pl.ds(place[w][0], EXT), :], EXT * g - place[w][1]) for g, w in enumerate(which)]
            x = parts[0]
            for g, part in enumerate(parts[1:]):
                x = jnp.where(lane40 < EXT * (g + 1), x, part)
            dst[c] = x

    gather(MR, (10, 11, 12))
    gather(ML, (-3, -2, -1))
    carry_up = lax.div(gy + 1, ngy)
    carry_down = lax.div(ngy - gy, ngy)
    ahead = (lax.rem(gx + carry_up, ngx), lax.rem(gy + 1, ngy))
    behind = (lax.rem(gx + ngx - carry_down, ngx), lax.rem(gy + ngy - 1, ngy))
    moves = [remote(MR, U.at[4], ahead), remote(ML, U.at[5], behind)]
    for copy in moves:
        copy.start()

    gather(U.at[0], (3, 4, 5))
    gather(U.at[1], (6,))
    gather(U.at[2], (0, 1, 2))
    gather(U.at[3], (7, 8, 9))

    def first(t, carry, pick=lambda t: t):
        at_u = pick(t)
        for r in ROWS:
            u = [U[at_u, c, r : r + 8, :] for c in range(8)]
            flux_x, edge_x, flux_y, edge_y = cell_state(u)
            for i, v in enumerate(flux_x + edge_x):
                SX[i, r : r + 8, :] = v
            _, _, a, b, w = edge_weights(*edge_y, roll(edge_y[0], -1), roll(edge_y[1], -1))
            cell = (u[2],) + flux_y[:5] + (None,) + flux_y[5:]
            for c in range(8):
                jump = w * (roll(u[c], -1) - u[c])
                flux = jump if cell[c] is None else a * cell[c] + b * roll(cell[c], -1) + jump
                DY[t, c, r : r + 8, :] = flux - roll(flux, 1)
        for r in FACE1:
            edges = [SX[i, r + d : r + d + 8, :] for d in range(2) for i in (6, 7)]
            _, _, a, b, w = edge_weights(*edges)
            for c in range(8):
                low, high = U[at_u, c, r : r + 8, :], U[at_u, c, r + 1 : r + 9, :]
                flux = w * (high - low)
                if c == 0:
                    flux = a * U[at_u, 1, r : r + 8, :] + b * U[at_u, 1, r + 1 : r + 9, :] + flux
                elif c != 5:
                    i = c - 1 if c < 5 else c - 2
                    flux = a * SX[i, r : r + 8, :] + b * SX[i, r + 1 : r + 9, :] + flux
                GX[t, c, r : r + 8, :] = flux
        return carry

    lax.fori_loop(0, 2, first, 0)

    for copy in moves:
        copy.wait_recv()

    def pick(t):
        from_left = jnp.where(excess > 0, 4, 2)
        from_right = jnp.where(excess + count < CAP, 5, 3)
        return jnp.where(t == 2, from_left, jnp.where(t == 3, from_right, t))

    lax.fori_loop(2, 4, functools.partial(first, pick=pick), 0)

    for copy in round2:
        copy.wait_recv()
    for s in range(ngx - 1):
        peak = jnp.maximum(peak, P2[s])
    peak = jnp.max(jnp.max(peak, axis=0, keepdims=True), axis=1, keepdims=True)
    time_step = COURANT / jnp.broadcast_to(peak, (8, 128))

    def widths(ws):
        v = jnp.full((8, 128), wide[ws[0]], F32)
        for g, w in enumerate(ws[1:]):
            v = jnp.where(lane8 < EXT * (g + 1), v, wide[w])
        return v

    VM[2] = time_step * widths((3, 4, 5))
    VM[3] = time_step * widths((6,))
    VM[4] = time_step * widths((0, 1, 2))
    VM[5] = time_step * widths((7, 8, 9))

    def second(t, carry):
        rate = VM[2 + t]
        at_u = pick(t)
        half = 0.5 * rate
        for r in MID:
            u = []
            for c in range(8):
                change = GX[t, c, r : r + 8, :] - GX[t, c, r - 1 : r + 7, :] + DY[t, c, r : r + 8, :]
                u.append(U[at_u, c, r : r + 8, :] - half * change)
            _, vx, vy, vz, pressure, _ = primitive(u)
            for c, v in enumerate((u[0], vx, vy, vz, pressure, u[5], u[6], u[7])):
                W[c, r : r + 8, :] = v
        for r in SLOPE:
            for c in range(8):
                w = [W[c, r + d : r + d + 8, :] for d in (-1, 0, 1, 2)]
                low, d, high = w[1] - w[0], w[2] - w[1], w[3] - w[2]
                rise = limited(0.5 * d + (low - high) * (1.0 / 12.0), d)
                RA[c, r : r + 8, :] = rise
                EA[c, r : r + 8, :] = d - rise
        for r in FACE2:
            left, right = [], []
            for c in range(8):
                rise, rise_next = RA[c, r : r + 8, :], RA[c, r + 1 : r + 9, :]
                fall, fall_next = EA[c, r - 1 : r + 7, :], EA[c, r : r + 8, :]
                left.append(W[c, r : r + 8, :] + limited(rise, 2.0 * fall))
                right.append(W[c, r + 1 : r + 9, :] - limited(fall_next, 2.0 * rise_next))
            for c, v in enumerate(face_flux(left, right, 1)):
                GX2[c, r : r + 8, :] = v
        for r in LAST:
            left, right = [], []
            for c in range(8):
                w = W[c, r : r + 8, :]
                ahead_w = roll(w, -1)
                d = ahead_w - w
                rise = limited(0.5 * d + (roll(d, 1) - roll(d, -1)) * (1.0 / 12.0), d)
                fall = d - rise
                left.append(w + limited(rise, 2.0 * roll(fall, 1)))
                right.append(ahead_w - limited(fall, 2.0 * roll(rise, -1)))
            for c, v in enumerate(face_flux(left, right, 2)):
                change = GX2[c, r : r + 8, :] - GX2[c, r - 1 : r + 7, :] + (v - roll(v, 1))
                O[t, c, r - 4 : r + 4, :] = U[at_u, c, r : r + 8, :] - rate * change
        return carry

    lax.fori_loop(0, 4, second, 0)

    for c in range(8):
        o = [O[t, c] for t in range(4)]
        o0 = jnp.where(lane32 < 32, roll(o[2], -4), jnp.where(lane32 < 64, roll(o[2], -12), roll(o[2], -20)))
        out[c, :, 0:128] = jnp.where(lane32 < 96, o0, roll(o[0], 92))
        o1 = jnp.where(lane32 < 32, roll(o[0], -44), roll(o[0], -52))
        out[c, :, 128:256] = jnp.where(lane32 < 64, o1, jnp.where(lane32 < 96, roll(o[1], 60), roll(o[3], 92)))
        o2 = jnp.where(lane32 < 32, roll(o[3], -44), roll(o[3], -52))
        out[c, :, 256:320] = o2[:, 0:64]

    for copy in ghosts + moves + round1 + round2:
        copy.wait_send()


def shards(ngx, ngy, fields, refined):
    vmem = lambda *shape: pltpu.VMEM(shape, F32)
    scratch = [
        pltpu.SMEM((2 * ngy, 2 * ngx), jnp.int32),
        pltpu.VMEM((2 * ngy, 2 * ngx), jnp.int32),
        vmem(8, 32, 512),
        vmem(8, 2, 64, 128),
        vmem(8, PAD_ROWS, 128),
        vmem(6, 8, EXT, 128),
        vmem(8, EXT, 128),
        vmem(8, EXT, 128),
        vmem(2, 8, 8, 128),
        vmem(2, 8, 8, 128),
        vmem(2, 8, 128),
        vmem(4, 8, 128),
        vmem(2, 2, 32, 128),
        vmem(2, 2, 32, 128),
        vmem(6, 8, 128),
        vmem(ngy - 1, 8, 128),
        vmem(ngx - 1, 8, 128),
        vmem(8, EXT, 128),
        vmem(4, 8, EXT, 128),
        vmem(4, 8, EXT, 128),
        vmem(8, EXT, 128),
        vmem(8, EXT, 128),
        vmem(8, EXT, 128),
        vmem(8, EXT, 128),
        vmem(4, 8, BS, 128),
        pltpu.SemaphoreType.DMA((3,)),
        pltpu.SemaphoreType.DMA((ngx + ngy + 8,)),
        pltpu.SemaphoreType.DMA((ngx + ngy + 8,)),
    ]
    return pl.pallas_call(
        functools.partial(kernel, ngx, ngy),
        out_shape=jax.ShapeDtypeStruct((8, BS, CAP * BS), F32),
        in_specs=[
            pl.BlockSpec(memory_space=pltpu.HBM),
            pl.BlockSpec(memory_space=pltpu.HBM),
        ],
        out_specs=pl.BlockSpec(memory_space=pltpu.VMEM),
        scratch_shapes=scratch,
        compiler_params=pltpu.CompilerParams(
            collective_id=0, has_side_effects=True, vmem_limit_bytes=60 * 1024 * 1024
        ),
    )(refined.T, fields)


def solution(mesh):
    ngx, ngy = mesh.shape["gx"], mesh.shape["gy"]
    return jax.shard_map(
        functools.partial(shards, ngx, ngy),
        mesh=mesh,
        in_specs=(P(None, None, ("gx", "gy")), P()),
        out_specs=P(None, None, ("gx", "gy")),
        check_vma=False,
    )
```

```python
import functools

import jax
import jax.numpy as jnp
from jax import lax
from jax.experimental import pallas as pl
from jax.experimental.pallas import tpu as pltpu
from jax.sharding import PartitionSpec as P

BS = 32
CAP = 10
EXT = BS + 8
GAMMA = 5.0 / 3.0
COURANT = 0.2
MESH = pl.DeviceIdType.MESH
F32 = jnp.float32

FINE = (4, 140)
COARSE = (276, 348)
PAD_ROWS = 424
ROWS = (0, 8, 16, 24, 32)
FACE1 = (0, 8, 16, 24, 31)
MID = (1, 9, 17, 25, 31)
SLOPE = (2, 10, 18, 26, 29)
FACE2 = (3, 11, 19, 27, 28)
LAST = (4, 12, 20, 28)


def lanes(rows):
    return lax.broadcasted_iota(jnp.int32, (rows, 128), 1)


def roll(x, by):
    if isinstance(by, int):
        by = by % 128
        return x if by == 0 else pltpu.roll(x, by, 1)
    return pltpu.roll(x, lax.rem(by + 256, 128), 1)


def recip(x):
    r = pltpu.reciprocal(x, approx=True)
    return r * (2.0 - x * r)


def root(x):
    return x * lax.rsqrt(jnp.maximum(x, 1e-30))


def limited(value, other):
    return jnp.minimum(jnp.maximum(value, jnp.minimum(other, 0.0)), jnp.maximum(other, 0.0))


def primitive(u):
    rho, mx, my, mz, energy, bx, by, bz = u
    inv = recip(rho)
    vx, vy, vz = mx * inv, my * inv, mz * inv
    half_b2 = 0.5 * (bx * bx + by * by + bz * bz)
    kinetic = 0.5 * (mx * vx + my * vy + mz * vz)
    pressure = (GAMMA - 1.0) * (energy - kinetic - half_b2)
    return inv, vx, vy, vz, pressure, half_b2


def fast_pair(inv, pressure, half_b2, trans_x, trans_y):
    sound = GAMMA * pressure * inv
    alfven = 2.0 * half_b2 * inv
    total = sound + alfven
    diff = sound - alfven
    square = diff * diff
    four = 4.0 * sound * inv
    fast_x = root(0.5 * (total + root(square + four * trans_x)))
    fast_y = root(0.5 * (total + root(square + four * trans_y)))
    return fast_x, fast_y


def cell_state(u):
    rho, mx, my, mz, energy, bx, by, bz = u
    inv, vx, vy, vz, pressure, half_b2 = primitive(u)
    xx, yy, zz = bx * bx, by * by, bz * bz
    fast_x, fast_y = fast_pair(inv, pressure, half_b2, yy + zz, xx + zz)
    total_p = pressure + half_b2
    enthalpy = energy + total_p
    vb = vx * bx + vy * by + vz * bz
    cross = mx * vy - bx * by
    emf = by * vx - bx * vy
    flux_x = (mx * vx + total_p - xx, cross, mx * vz - bx * bz, enthalpy * vx - bx * vb, emf, bz * vx - bx * vz)
    flux_y = (cross, my * vy + total_p - yy, my * vz - by * bz, enthalpy * vy - by * vb, -emf, bz * vy - by * vz)
    return flux_x, (vx - fast_x, vx + fast_x), flux_y, (vy - fast_y, vy + fast_y)


def edge_weights(slow_l, fast_l, slow_r, fast_r):
    slow = jnp.minimum(jnp.minimum(slow_l, slow_r), 0.0)
    fast = jnp.maximum(jnp.maximum(fast_l, fast_r), 0.0)
    inv = recip(fast - slow)
    a = fast * inv
    b = -slow * inv
    return slow, fast, a, b, slow * a


def side(w, normal):
    rho, vx, vy, vz, pressure, bx, by, bz = w
    vn, vt, bn, bt = (vx, vy, bx, by) if normal == 1 else (vy, vx, by, bx)
    inv = recip(rho)
    trans = bt * bt + bz * bz
    nn = bn * bn
    b2 = trans + nn
    sound = GAMMA * pressure * inv
    alfven = b2 * inv
    diff = sound - alfven
    fast = root(0.5 * (sound + alfven + root(diff * diff + 4.0 * sound * inv * trans)))
    half_b2 = 0.5 * b2
    total_p = pressure + half_b2
    energy = 1.5 * pressure + half_b2 + 0.5 * rho * (vn * vn + vt * vt + vz * vz)
    vb = vn * bn + vt * bt + vz * bz
    return vn - fast, vn + fast, (rho, vn, vt, vz, bn, bt, bz, energy, total_p, total_p - nn, vb)


def moved(state, speed):
    rho, vn, vt, vz, bn, bt, bz, energy, total_p, stress, vb = state
    rel = vn - speed
    mass = rho * rel
    return (
        mass,
        mass * vn + stress,
        mass * vt - bn * bt,
        mass * vz - bn * bz,
        energy * rel + total_p * vn - bn * vb,
        bt * rel - bn * vt,
        bz * rel - bn * vz,
    )


def face_flux(left, right, normal):
    slow_l, fast_l, state_l = side(left, normal)
    slow_r, fast_r, state_r = side(right, normal)
    slow, fast, a, b, c = edge_weights(slow_l, fast_l, slow_r, fast_r)
    from_l = moved(state_l, slow)
    from_r = moved(state_r, fast)
    mass, mn, mt, mz, en, bt, bz = (a * p + b * q for p, q in zip(from_l, from_r))
    bn = c * (state_r[4] - state_l[4])
    if normal == 1:
        return (mass, mn, mt, mz, en, bn, bt, bz)
    return (mass, mt, mn, mz, en, bt, bn, bz)


def kernel(ngx, ngy, refined, fields, out, *scratch):
    (ref_s, ref_v, X, Z, G, U, ML, MR, SR, RB, SK, RK, SY, RY, VM, P1, P2, SX, GX, DY, W, RA, EA, GX2, O, in_sem, send, recv) = scratch
    gx = lax.axis_index("gx")
    gy = lax.axis_index("gy")
    me = gx * ngy + gy
    load = pltpu.make_async_copy(fields, X, in_sem.at[0])
    load.start()
    load_s = pltpu.make_async_copy(refined, ref_s, in_sem.at[1])
    load_s.start()
    load_v = pltpu.make_async_copy(refined, ref_v, in_sem.at[2])
    load_v.start()

    def at(dx, dy):
        return lax.rem(gx + dx + ngx, ngx), lax.rem(gy + dy + ngy, ngy)

    partners = [at(0, s) for s in range(1, ngy)] + [at(s, 0) for s in range(1, ngx)]
    partners += [at(1, 1), at(1, -1), at(-1, 1), at(-1, -1)]
    barrier = pltpu.get_barrier_semaphore()
    for who in partners:
        pl.semaphore_signal(barrier, inc=1, device_id=who, device_id_type=MESH)

    sems = iter(range(64))

    def remote(src, dst, who):
        i = next(sems)
        return pltpu.make_async_remote_copy(
            src_ref=src, dst_ref=dst, send_sem=send.at[i], recv_sem=recv.at[i], device_id=who, device_id_type=MESH
        )

    def flags_of(tile):
        tx, ty = lax.div(tile, ngy), lax.rem(tile, ngy)
        return [ref_s[2 * ty + r % 2, 2 * tx + r // 2] for r in range(4)]

    load_s.wait()
    mine = flags_of(me)
    lane8, lane32, lane40 = lanes(8), lanes(32), lanes(EXT)
    load.wait()

    zero8 = jnp.zeros((8, 128), F32)
    peak = zero8
    for r in range(4):
        on = mine[r] > 0
        weight = jnp.where(lane8 < 32, jnp.where(on, 1.0, 0.5), jnp.where(on, 1.0, 0.0)).astype(F32)
        for q in range(4):
            u = [X[c, 8 * q : 8 * q + 8, 128 * r : 128 * r + 128] for c in range(8)]
            inv, vx, vy, vz, pressure, half_b2 = primitive(u)
            xx, yy, zz = (b * b for b in u[5:])
            fast_x, fast_y = fast_pair(inv, pressure, half_b2, yy + zz, xx + zz)
            rate = jnp.maximum(jnp.abs(vx) + fast_x, jnp.abs(vy) + fast_y)
            peak = jnp.maximum(peak, jnp.where(weight > 0.0, rate * weight, 0.0))
    VM[0] = peak
    round1 = [remote(VM.at[0], P1.at[s - 1], at(0, s)) for s in range(1, ngy)]
    pl.semaphore_wait(barrier, len(partners))
    for copy in round1:
        copy.start()

    def rotate(h, carry):
        for cc in range(4):
            c = 4 * h + cc
            for rx in range(2):
                for q in range(4):
                    a = X[c, 8 * q : 8 * q + 8, 256 * rx : 256 * rx + 128]
                    b = X[c, 8 * q : 8 * q + 8, 256 * rx + 128 : 256 * rx + 256]
                    a32, b32 = roll(a, -32), roll(b, 32)
                    top = jnp.where(lane8 < 32, a, jnp.where(lane8 < 64, a32, jnp.where(lane8 < 96, roll(b, 64), b32)))
                    low = jnp.where(lane8 < 32, a32, jnp.where(lane8 < 64, roll(a, -64), jnp.where(lane8 < 96, b32, b)))
                    row = FINE[0] + 4 + 64 * rx + 8 * q
                    G[c, row : row + 8, :] = top
                    G[c, row + 32 : row + 40, :] = low
                    Z[c, rx, 8 * q : 8 * q + 8, :] = jnp.where(lane8 < 32, a, b32)
        return carry

    def spread(h, carry):
        row8 = lax.broadcasted_iota(jnp.int32, (8, 128), 0)
        half = row8 % 4 * 2
        halves = lane8 * 2 % 128
        for cc in range(4):
            c = 4 * h + cc
            for rx in range(2):
                keep = jnp.where(lane8 < 64, mine[2 * rx], mine[2 * rx + 1]) > 0
                fine = []
                for q in range(4):
                    z = jnp.take_along_axis(Z[c, rx, 8 * q : 8 * q + 8, :], lane8 // 2, axis=1)
                    for i in range(2):
                        row = FINE[0] + 4 + 64 * rx + 16 * q + 8 * i
                        x = jnp.take_along_axis(z, row8 // 2 + 4 * i, axis=0)
                        x = jnp.where(keep, G[c, row : row + 8, :], x)
                        G[c, row : row + 8, :] = x
                        G[c, row + 136 : row + 144, :] = x
                        x = x + pltpu.roll(x, 7, 0)
                        fine.append(jnp.take_along_axis(x, half, axis=0))
                for q in range(4):
                    x = jnp.where(row8 < 4, fine[2 * q], fine[2 * q + 1])
                    x = 0.25 * (jnp.take_along_axis(x, halves, axis=1) + jnp.take_along_axis(x, halves + 1, axis=1))
                    for base in COARSE:
                        row = base + 4 + 32 * rx + 8 * q
                        G[c, row : row + 8, :] = x
        return carry

    lax.fori_loop(0, 2, rotate, 0)
    lax.fori_loop(0, 2, spread, 0)

    def pack_columns():
        for h in range(2):
            for q in range(4):
                acc_r, acc_l = zero8, zero8
                for cc in range(4):
                    for k in range(6):
                        s = 32 * cc + 4 * k
                        row = (FINE[0] + 4 + 32 * k if k < 4 else COARSE[0] + 4 + 32 * (k - 4)) + 8 * q
                        x = roll(G[4 * h + cc, row : row + 8, :], s + 4)
                        acc_r = jnp.where((lane8 >= s) & (lane8 < s + 4), x, acc_r)
                        acc_l = jnp.where((lane8 >= s + 4) & (lane8 < s + 8), x, acc_l)
                SY[0, h, 8 * q : 8 * q + 8, :] = acc_r
                SY[1, h, 8 * q : 8 * q + 8, :] = acc_l

    pack_columns()

    ghosts = [remote(SY.at[0], RY.at[0], at(0, 1)), remote(SY.at[1], RY.at[1], at(0, -1))]
    for copy in ghosts:
        copy.start()
    def pack_rows():
        for d in range(2):
            corner = zero8
            fine, coarse = FINE[0] + 4 + (124, 0)[d], COARSE[0] + 4 + (60, 0)[d]
            for c in range(8):
                SR[d, c, 0:4, :] = G[c, fine : fine + 4, :]
                SR[d, c, 4:8, :] = G[c, coarse : coarse + 4, :]
                corner = jnp.where(lane8 // 8 == c, roll(SR[d, c], 8 * c + 4), corner)
            SK[d] = corner

    pack_rows()

    edges = [
        remote(SR.at[0], RB.at[0], at(1, 0)),
        remote(SR.at[1], RB.at[1], at(-1, 0)),
        remote(SK.at[0], RK.at[0], at(1, 1)),
        remote(SK.at[0], RK.at[1], at(1, -1)),
        remote(SK.at[1], RK.at[2], at(-1, 1)),
        remote(SK.at[1], RK.at[3], at(-1, -1)),
    ]
    for copy in edges:
        copy.start()
    ghosts += edges

    for copy in round1:
        copy.wait_recv()
    for s in range(ngy - 1):
        peak = jnp.maximum(peak, P1[s])
    VM[1] = peak
    round2 = [remote(VM.at[1], P2.at[s - 1], at(s, 0)) for s in range(1, ngx)]
    for copy in round2:
        copy.start()

    load_v.wait()
    tile_of = lax.broadcasted_iota(jnp.int32, (2 * ngy, 2 * ngx), 1) // 2 * ngy
    tile_of = tile_of + lax.broadcasted_iota(jnp.int32, (2 * ngy, 2 * ngx), 0) // 2
    before = jnp.sum(jnp.where(tile_of < me, ref_v[...], 0))
    excess = 4 * me + 3 * before - CAP * me
    prev = flags_of(lax.rem(me + ngx * ngy - 1, ngx * ngy))
    following = flags_of(lax.rem(me + 1, ngx * ngy))

    def count_of(fl):
        return 4 + 3 * (fl[0] + fl[1] + fl[2] + fl[3])

    count = count_of(mine)

    def ge(a, b):
        return jnp.where(a >= b, 1, 0)

    def find(index, fl):
        index = jnp.clip(index, 0, count_of(fl) - 1)
        p1 = 1 + 3 * fl[0]
        p2 = p1 + 1 + 3 * fl[1]
        p3 = p2 + 1 + 3 * fl[2]
        a1, a2, a3 = ge(index, p1), ge(index, p2), ge(index, p3)
        child = index - (a1 * p1 + a2 * (p2 - p1) + a3 * (p3 - p2))
        flag = fl[0] + a1 * (fl[1] - fl[0]) + a2 * (fl[2] - fl[1]) + a3 * (fl[3] - fl[2])
        rx = a2
        ry = a1 + a2 + a3 - 2 * rx
        cx, cy = child & 1, child >> 1
        row = flag * (FINE[0] + 136 * ry + 64 * rx + 32 * cx) + (1 - flag) * (COARSE[0] + 72 * ry + 32 * rx)
        lane = flag * (64 * ry + 32 * cy) + (1 - flag) * 96 * ry - 4
        return row, lane, flag

    place = {w: find(w - excess, mine) for w in range(-3, 13)}
    wide = {}
    for w in range(CAP):
        flag = place[w][2]
        index = w - excess
        if w < 3:
            flag = jnp.where(index >= 0, flag, find(index + count_of(prev), prev)[2])
        if w >= 7:
            flag = jnp.where(index < count, flag, find(index - count, following)[2])
        wide[w] = 0.5 + 0.5 * flag.astype(F32)

    for copy in ghosts:
        copy.wait_recv()
    def fill():
        left8, right8 = lane8 >= 124, lane8 < 4
        left32, right32 = lane32 >= 124, lane32 < 4
        for d in range(2):
            corner = jnp.where(lane8 % 8 < 4, RK[2 * d], RK[2 * d + 1])
            for c in range(8):
                piece = roll(corner, -8 * c - 4)
                row = RB[d, c]
                for i, mask in enumerate((left8, right8)):
                    x = jnp.where(mask, piece, row)
                    fine, coarse = FINE[i] + 132 * d, COARSE[i] + 68 * d
                    G[c, fine : fine + 4, :] = x[0:4]
                    G[c, coarse : coarse + 4, :] = x[4:8]
        for h in range(2):
            low4 = lane32 % 8 < 4
            pair = (jnp.where(low4, RY[0, h], RY[1, h]), jnp.where(low4, RY[1, h], RY[0, h]))
            for cc in range(4):
                for k in range(6):
                    x = roll(pair[k % 2], -(32 * cc + 4 * k) - 4)
                    for i, mask in enumerate((left32, right32)):
                        row = FINE[i] + 4 + 32 * k if k < 4 else COARSE[i] + 4 + 32 * (k - 4)
                        pltpu.store(G.at[4 * h + cc, pl.ds(row, 32), :], x, mask=mask)

    fill()

    def gather(dst, which):
        for c in range(8):
            parts = [roll(G[c, pl.ds(place[w][0], EXT), :], EXT * g - place[w][1]) for g, w in enumerate(which)]
            x = parts[0]
            for g, part in enumerate(parts[1:]):
                x = jnp.where(lane40 < EXT * (g + 1), x, part)
            dst[c] = x

    gather(MR, (10, 11, 12))
    gather(ML, (-3, -2, -1))
    carry_up = lax.div(gy + 1, ngy)
    carry_down = lax.div(ngy - gy, ngy)
    ahead = (lax.rem(gx + carry_up, ngx), lax.rem(gy + 1, ngy))
    behind = (lax.rem(gx + ngx - carry_down, ngx), lax.rem(gy + ngy - 1, ngy))
    moves = [remote(MR, U.at[4], ahead), remote(ML, U.at[5], behind)]
    for copy in moves:
        copy.start()

    gather(U.at[0], (3, 4, 5))
    gather(U.at[1], (6,))
    gather(U.at[2], (0, 1, 2))
    gather(U.at[3], (7, 8, 9))

    def first(t, carry, pick=lambda t: t):
        at_u = pick(t)
        for r in ROWS:
            u = [U[at_u, c, r : r + 8, :] for c in range(8)]
            flux_x, edge_x, flux_y, edge_y = cell_state(u)
            for i, v in enumerate(flux_x + edge_x):
                SX[i, r : r + 8, :] = v
            _, _, a, b, w = edge_weights(*edge_y, roll(edge_y[0], -1), roll(edge_y[1], -1))
            cell = (u[2],) + flux_y[:5] + (None,) + flux_y[5:]
            for c in range(8):
                jump = w * (roll(u[c], -1) - u[c])
                flux = jump if cell[c] is None else a * cell[c] + b * roll(cell[c], -1) + jump
                DY[t, c, r : r + 8, :] = flux - roll(flux, 1)
        for r in FACE1:
            edges = [SX[i, r + d : r + d + 8, :] for d in range(2) for i in (6, 7)]
            _, _, a, b, w = edge_weights(*edges)
            for c in range(8):
                low, high = U[at_u, c, r : r + 8, :], U[at_u, c, r + 1 : r + 9, :]
                flux = w * (high - low)
                if c == 0:
                    flux = a * U[at_u, 1, r : r + 8, :] + b * U[at_u, 1, r + 1 : r + 9, :] + flux
                elif c != 5:
                    i = c - 1 if c < 5 else c - 2
                    flux = a * SX[i, r : r + 8, :] + b * SX[i, r + 1 : r + 9, :] + flux
                GX[t, c, r : r + 8, :] = flux
        return carry

    lax.fori_loop(0, 2, first, 0)

    for copy in round2:
        copy.wait_recv()
    for s in range(ngx - 1):
        peak = jnp.maximum(peak, P2[s])
    peak = jnp.max(jnp.max(peak, axis=0, keepdims=True), axis=1, keepdims=True)
    time_step = COURANT / jnp.broadcast_to(peak, (8, 128))

    def widths(ws):
        v = jnp.full((8, 128), wide[ws[0]], F32)
        for g, w in enumerate(ws[1:]):
            v = jnp.where(lane8 < EXT * (g + 1), v, wide[w])
        return v

    VM[2] = time_step * widths((3, 4, 5))
    VM[3] = time_step * widths((6,))
    VM[4] = time_step * widths((0, 1, 2))
    VM[5] = time_step * widths((7, 8, 9))

    def second(t, carry, pick=lambda t: t):
        rate = VM[2 + t]
        at_u = pick(t)
        half = 0.5 * rate
        for r in MID:
            u = []
            for c in range(8):
                change = GX[t, c, r : r + 8, :] - GX[t, c, r - 1 : r + 7, :] + DY[t, c, r : r + 8, :]
                u.append(U[at_u, c, r : r + 8, :] - half * change)
            _, vx, vy, vz, pressure, _ = primitive(u)
            for c, v in enumerate((u[0], vx, vy, vz, pressure, u[5], u[6], u[7])):
                W[c, r : r + 8, :] = v
        for r in SLOPE:
            for c in range(8):
                w = [W[c, r + d : r + d + 8, :] for d in (-1, 0, 1, 2)]
                low, d, high = w[1] - w[0], w[2] - w[1], w[3] - w[2]
                rise = limited(0.5 * d + (low - high) * (1.0 / 12.0), d)
                RA[c, r : r + 8, :] = rise
                EA[c, r : r + 8, :] = d - rise
        for r in FACE2:
            left, right = [], []
            for c in range(8):
                rise, rise_next = RA[c, r : r + 8, :], RA[c, r + 1 : r + 9, :]
                fall, fall_next = EA[c, r - 1 : r + 7, :], EA[c, r : r + 8, :]
                left.append(W[c, r : r + 8, :] + limited(rise, 2.0 * fall))
                right.append(W[c, r + 1 : r + 9, :] - limited(fall_next, 2.0 * rise_next))
            for c, v in enumerate(face_flux(left, right, 1)):
                GX2[c, r : r + 8, :] = v
        for r in LAST:
            left, right = [], []
            for c in range(8):
                w = W[c, r : r + 8, :]
                ahead_w = roll(w, -1)
                d = ahead_w - w
                rise = limited(0.5 * d + (roll(d, 1) - roll(d, -1)) * (1.0 / 12.0), d)
                fall = d - rise
                left.append(w + limited(rise, 2.0 * roll(fall, 1)))
                right.append(ahead_w - limited(fall, 2.0 * roll(rise, -1)))
            for c, v in enumerate(face_flux(left, right, 2)):
                change = GX2[c, r : r + 8, :] - GX2[c, r - 1 : r + 7, :] + (v - roll(v, 1))
                O[t, c, r - 4 : r + 4, :] = U[at_u, c, r : r + 8, :] - rate * change
        return carry

    lax.fori_loop(0, 2, second, 0)

    for copy in moves:
        copy.wait_recv()

    def pick(t):
        from_left = jnp.where(excess > 0, 4, 2)
        from_right = jnp.where(excess + count < CAP, 5, 3)
        return jnp.where(t == 2, from_left, jnp.where(t == 3, from_right, t))

    lax.fori_loop(2, 4, functools.partial(first, pick=pick), 0)
    lax.fori_loop(2, 4, functools.partial(second, pick=pick), 0)

    def finish():
        for c in range(8):
            o = [O[t, c] for t in range(4)]
            o0 = jnp.where(lane32 < 32, roll(o[2], -4), jnp.where(lane32 < 64, roll(o[2], -12), roll(o[2], -20)))
            out[c, :, 0:128] = jnp.where(lane32 < 96, o0, roll(o[0], 92))
            o1 = jnp.where(lane32 < 32, roll(o[0], -44), roll(o[0], -52))
            out[c, :, 128:256] = jnp.where(lane32 < 64, o1, jnp.where(lane32 < 96, roll(o[1], 60), roll(o[3], 92)))
            o2 = jnp.where(lane32 < 32, roll(o[3], -44), roll(o[3], -52))
            out[c, :, 256:320] = o2[:, 0:64]

    finish()

    for copy in ghosts + moves + round1 + round2:
        copy.wait_send()


def shards(ngx, ngy, fields, refined):
    vmem = lambda *shape: pltpu.VMEM(shape, F32)
    scratch = [
        pltpu.SMEM((2 * ngy, 2 * ngx), jnp.int32),
        pltpu.VMEM((2 * ngy, 2 * ngx), jnp.int32),
        vmem(8, 32, 512),
        vmem(8, 2, BS, 128),
        vmem(8, PAD_ROWS, 128),
        vmem(6, 8, EXT, 128),
        vmem(8, EXT, 128),
        vmem(8, EXT, 128),
        vmem(2, 8, 8, 128),
        vmem(2, 8, 8, 128),
        vmem(2, 8, 128),
        vmem(4, 8, 128),
        vmem(2, 2, 32, 128),
        vmem(2, 2, 32, 128),
        vmem(6, 8, 128),
        vmem(ngy - 1, 8, 128),
        vmem(ngx - 1, 8, 128),
        vmem(8, EXT, 128),
        vmem(4, 8, EXT, 128),
        vmem(4, 8, EXT, 128),
        vmem(8, EXT, 128),
        vmem(8, EXT, 128),
        vmem(8, EXT, 128),
        vmem(8, EXT, 128),
        vmem(4, 8, BS, 128),
        pltpu.SemaphoreType.DMA((3,)),
        pltpu.SemaphoreType.DMA((ngx + ngy + 8,)),
        pltpu.SemaphoreType.DMA((ngx + ngy + 8,)),
    ]
    return pl.pallas_call(
        functools.partial(kernel, ngx, ngy),
        out_shape=jax.ShapeDtypeStruct((8, BS, CAP * BS), F32),
        in_specs=[
            pl.BlockSpec(memory_space=pltpu.HBM),
            pl.BlockSpec(memory_space=pltpu.HBM),
        ],
        out_specs=pl.BlockSpec(memory_space=pltpu.VMEM),
        scratch_shapes=scratch,
        compiler_params=pltpu.CompilerParams(
            collective_id=0, has_side_effects=True, vmem_limit_bytes=60 * 1024 * 1024
        ),
    )(refined.T, fields)


def solution(mesh):
    ngx, ngy = mesh.shape["gx"], mesh.shape["gy"]
    return jax.shard_map(
        functools.partial(shards, ngx, ngy),
        mesh=mesh,
        in_specs=(P(None, None, ("gx", "gy")), P()),
        out_specs=P(None, None, ("gx", "gy")),
        check_vma=False,
    )
```

```python
import functools

import jax
import jax.numpy as jnp
from jax import lax
from jax.experimental import pallas as pl
from jax.experimental.pallas import tpu as pltpu
from jax.sharding import PartitionSpec as P

BS = 32
CAP = 10
EXT = BS + 8
GAMMA = 5.0 / 3.0
COURANT = 0.2
MESH = pl.DeviceIdType.MESH
F32 = jnp.float32

FINE = (4, 140)
COARSE = (276, 348)
PAD_ROWS = 424
ROWS = (0, 8, 16, 24, 32)
FACE1 = (0, 8, 16, 24, 31)
MID = (1, 9, 17, 25, 31)
SLOPE = (2, 10, 18, 26, 29)
FACE2 = (3, 11, 19, 27, 28)
LAST = (4, 12, 20, 28)


def lanes(rows):
    return lax.broadcasted_iota(jnp.int32, (rows, 128), 1)


def roll(x, by):
    if isinstance(by, int):
        by = by % 128
        return x if by == 0 else pltpu.roll(x, by, 1)
    return pltpu.roll(x, lax.rem(by + 256, 128), 1)


def recip(x):
    r = pltpu.reciprocal(x, approx=True)
    return r * (2.0 - x * r)


def root(x):
    return x * lax.rsqrt(jnp.maximum(x, 1e-30))


def limited(value, other):
    return jnp.minimum(jnp.maximum(value, jnp.minimum(other, 0.0)), jnp.maximum(other, 0.0))


def primitive(u):
    rho, mx, my, mz, energy, bx, by, bz = u
    inv = recip(rho)
    vx, vy, vz = mx * inv, my * inv, mz * inv
    half_b2 = 0.5 * (bx * bx + by * by + bz * bz)
    kinetic = 0.5 * (mx * vx + my * vy + mz * vz)
    pressure = (GAMMA - 1.0) * (energy - kinetic - half_b2)
    return inv, vx, vy, vz, pressure, half_b2


def fast_pair(inv, pressure, half_b2, trans_x, trans_y):
    sound = GAMMA * pressure * inv
    alfven = 2.0 * half_b2 * inv
    total = sound + alfven
    diff = sound - alfven
    square = diff * diff
    four = 4.0 * sound * inv
    fast_x = root(0.5 * (total + root(square + four * trans_x)))
    fast_y = root(0.5 * (total + root(square + four * trans_y)))
    return fast_x, fast_y


def cell_state(u):
    rho, mx, my, mz, energy, bx, by, bz = u
    inv, vx, vy, vz, pressure, half_b2 = primitive(u)
    xx, yy, zz = bx * bx, by * by, bz * bz
    fast_x, fast_y = fast_pair(inv, pressure, half_b2, yy + zz, xx + zz)
    total_p = pressure + half_b2
    enthalpy = energy + total_p
    vb = vx * bx + vy * by + vz * bz
    cross = mx * vy - bx * by
    emf = by * vx - bx * vy
    flux_x = (mx * vx + total_p - xx, cross, mx * vz - bx * bz, enthalpy * vx - bx * vb, emf, bz * vx - bx * vz)
    flux_y = (cross, my * vy + total_p - yy, my * vz - by * bz, enthalpy * vy - by * vb, -emf, bz * vy - by * vz)
    return flux_x, (vx - fast_x, vx + fast_x), flux_y, (vy - fast_y, vy + fast_y)


def edge_weights(slow_l, fast_l, slow_r, fast_r):
    slow = jnp.minimum(jnp.minimum(slow_l, slow_r), 0.0)
    fast = jnp.maximum(jnp.maximum(fast_l, fast_r), 0.0)
    inv = recip(fast - slow)
    a = fast * inv
    b = -slow * inv
    return slow, fast, a, b, slow * a


def side(w, normal):
    rho, vx, vy, vz, pressure, bx, by, bz = w
    vn, vt, bn, bt = (vx, vy, bx, by) if normal == 1 else (vy, vx, by, bx)
    inv = recip(rho)
    trans = bt * bt + bz * bz
    nn = bn * bn
    b2 = trans + nn
    sound = GAMMA * pressure * inv
    alfven = b2 * inv
    diff = sound - alfven
    fast = root(0.5 * (sound + alfven + root(diff * diff + 4.0 * sound * inv * trans)))
    half_b2 = 0.5 * b2
    total_p = pressure + half_b2
    energy = 1.5 * pressure + half_b2 + 0.5 * rho * (vn * vn + vt * vt + vz * vz)
    vb = vn * bn + vt * bt + vz * bz
    return vn - fast, vn + fast, (rho, vn, vt, vz, bn, bt, bz, energy, total_p, total_p - nn, vb)


def moved(state, speed):
    rho, vn, vt, vz, bn, bt, bz, energy, total_p, stress, vb = state
    rel = vn - speed
    mass = rho * rel
    return (
        mass,
        mass * vn + stress,
        mass * vt - bn * bt,
        mass * vz - bn * bz,
        energy * rel + total_p * vn - bn * vb,
        bt * rel - bn * vt,
        bz * rel - bn * vz,
    )


def face_flux(left, right, normal):
    slow_l, fast_l, state_l = side(left, normal)
    slow_r, fast_r, state_r = side(right, normal)
    slow, fast, a, b, c = edge_weights(slow_l, fast_l, slow_r, fast_r)
    from_l = moved(state_l, slow)
    from_r = moved(state_r, fast)
    mass, mn, mt, mz, en, bt, bz = (a * p + b * q for p, q in zip(from_l, from_r))
    bn = c * (state_r[4] - state_l[4])
    if normal == 1:
        return (mass, mn, mt, mz, en, bn, bt, bz)
    return (mass, mt, mn, mz, en, bt, bn, bz)


def kernel(ngx, ngy, ref_s, ref_v, X, out, *scratch):
    (Z, G, U, ML, MR, SR, RB, SK, RK, SY, RY, VM, P1, P2, SX, GX, DY, W, RA, EA, GX2, O, send, recv) = scratch
    gx = lax.axis_index("gx")
    gy = lax.axis_index("gy")
    me = gx * ngy + gy
    def at(dx, dy):
        return lax.rem(gx + dx + ngx, ngx), lax.rem(gy + dy + ngy, ngy)

    partners = [at(0, s) for s in range(1, ngy)] + [at(s, 0) for s in range(1, ngx)]
    partners += [at(1, 1), at(1, -1), at(-1, 1), at(-1, -1)]
    barrier = pltpu.get_barrier_semaphore()
    for who in partners:
        pl.semaphore_signal(barrier, inc=1, device_id=who, device_id_type=MESH)

    sems = iter(range(64))

    def remote(src, dst, who):
        i = next(sems)
        return pltpu.make_async_remote_copy(
            src_ref=src, dst_ref=dst, send_sem=send.at[i], recv_sem=recv.at[i], device_id=who, device_id_type=MESH
        )

    def flags_of(tile):
        tx, ty = lax.div(tile, ngy), lax.rem(tile, ngy)
        return [ref_s[2 * ty + r % 2, 2 * tx + r // 2] for r in range(4)]

    mine = flags_of(me)
    lane8, lane32, lane40 = lanes(8), lanes(32), lanes(EXT)

    zero8 = jnp.zeros((8, 128), F32)
    peak = zero8
    for r in range(4):
        on = mine[r] > 0
        weight = jnp.where(lane8 < 32, jnp.where(on, 1.0, 0.5), jnp.where(on, 1.0, 0.0)).astype(F32)
        for q in range(4):
            u = [X[c, 8 * q : 8 * q + 8, 128 * r : 128 * r + 128] for c in range(8)]
            inv, vx, vy, vz, pressure, half_b2 = primitive(u)
            xx, yy, zz = (b * b for b in u[5:])
            fast_x, fast_y = fast_pair(inv, pressure, half_b2, yy + zz, xx + zz)
            rate = jnp.maximum(jnp.abs(vx) + fast_x, jnp.abs(vy) + fast_y)
            peak = jnp.maximum(peak, jnp.where(weight > 0.0, rate * weight, 0.0))
    VM[0] = peak
    round1 = [remote(VM.at[0], P1.at[s - 1], at(0, s)) for s in range(1, ngy)]
    pl.semaphore_wait(barrier, len(partners))
    for copy in round1:
        copy.start()

    def rotate(h, carry):
        for cc in range(4):
            c = 4 * h + cc
            for rx in range(2):
                for q in range(4):
                    a = X[c, 8 * q : 8 * q + 8, 256 * rx : 256 * rx + 128]
                    b = X[c, 8 * q : 8 * q + 8, 256 * rx + 128 : 256 * rx + 256]
                    a32, b32 = roll(a, -32), roll(b, 32)
                    top = jnp.where(lane8 < 32, a, jnp.where(lane8 < 64, a32, jnp.where(lane8 < 96, roll(b, 64), b32)))
                    low = jnp.where(lane8 < 32, a32, jnp.where(lane8 < 64, roll(a, -64), jnp.where(lane8 < 96, b32, b)))
                    row = FINE[0] + 4 + 64 * rx + 8 * q
                    G[c, row : row + 8, :] = top
                    G[c, row + 32 : row + 40, :] = low
                    Z[c, rx, 8 * q : 8 * q + 8, :] = jnp.where(lane8 < 32, a, b32)
        return carry

    def spread(h, carry):
        row8 = lax.broadcasted_iota(jnp.int32, (8, 128), 0)
        half = row8 % 4 * 2
        halves = lane8 * 2 % 128
        for cc in range(4):
            c = 4 * h + cc
            for rx in range(2):
                keep = jnp.where(lane8 < 64, mine[2 * rx], mine[2 * rx + 1]) > 0
                fine = []
                for q in range(4):
                    z = jnp.take_along_axis(Z[c, rx, 8 * q : 8 * q + 8, :], lane8 // 2, axis=1)
                    for i in range(2):
                        row = FINE[0] + 4 + 64 * rx + 16 * q + 8 * i
                        x = jnp.take_along_axis(z, row8 // 2 + 4 * i, axis=0)
                        x = jnp.where(keep, G[c, row : row + 8, :], x)
                        G[c, row : row + 8, :] = x
                        G[c, row + 136 : row + 144, :] = x
                        x = x + pltpu.roll(x, 7, 0)
                        fine.append(jnp.take_along_axis(x, half, axis=0))
                for q in range(4):
                    x = jnp.where(row8 < 4, fine[2 * q], fine[2 * q + 1])
                    x = 0.25 * (jnp.take_along_axis(x, halves, axis=1) + jnp.take_along_axis(x, halves + 1, axis=1))
                    for base in COARSE:
                        row = base + 4 + 32 * rx + 8 * q
                        G[c, row : row + 8, :] = x
        return carry

    lax.fori_loop(0, 2, rotate, 0)
    lax.fori_loop(0, 2, spread, 0)

    def pack_columns():
        for h in range(2):
            for q in range(4):
                acc_r, acc_l = zero8, zero8
                for cc in range(4):
                    for k in range(6):
                        s = 32 * cc + 4 * k
                        row = (FINE[0] + 4 + 32 * k if k < 4 else COARSE[0] + 4 + 32 * (k - 4)) + 8 * q
                        x = roll(G[4 * h + cc, row : row + 8, :], s + 4)
                        acc_r = jnp.where((lane8 >= s) & (lane8 < s + 4), x, acc_r)
                        acc_l = jnp.where((lane8 >= s + 4) & (lane8 < s + 8), x, acc_l)
                SY[0, h, 8 * q : 8 * q + 8, :] = acc_r
                SY[1, h, 8 * q : 8 * q + 8, :] = acc_l

    pack_columns()

    ghosts = [remote(SY.at[0], RY.at[0], at(0, 1)), remote(SY.at[1], RY.at[1], at(0, -1))]
    for copy in ghosts:
        copy.start()
    def pack_rows():
        for d in range(2):
            corner = zero8
            fine, coarse = FINE[0] + 4 + (124, 0)[d], COARSE[0] + 4 + (60, 0)[d]
            for c in range(8):
                SR[d, c, 0:4, :] = G[c, fine : fine + 4, :]
                SR[d, c, 4:8, :] = G[c, coarse : coarse + 4, :]
                corner = jnp.where(lane8 // 8 == c, roll(SR[d, c], 8 * c + 4), corner)
            SK[d] = corner

    pack_rows()

    edges = [
        remote(SR.at[0], RB.at[0], at(1, 0)),
        remote(SR.at[1], RB.at[1], at(-1, 0)),
        remote(SK.at[0], RK.at[0], at(1, 1)),
        remote(SK.at[0], RK.at[1], at(1, -1)),
        remote(SK.at[1], RK.at[2], at(-1, 1)),
        remote(SK.at[1], RK.at[3], at(-1, -1)),
    ]
    for copy in edges:
        copy.start()
    ghosts += edges

    for copy in round1:
        copy.wait_recv()
    for s in range(ngy - 1):
        peak = jnp.maximum(peak, P1[s])
    VM[1] = peak
    round2 = [remote(VM.at[1], P2.at[s - 1], at(s, 0)) for s in range(1, ngx)]
    for copy in round2:
        copy.start()

    tile_of = lax.broadcasted_iota(jnp.int32, (2 * ngy, 2 * ngx), 1) // 2 * ngy
    tile_of = tile_of + lax.broadcasted_iota(jnp.int32, (2 * ngy, 2 * ngx), 0) // 2
    before = jnp.sum(jnp.where(tile_of < me, ref_v[...], 0))
    excess = 4 * me + 3 * before - CAP * me
    prev = flags_of(lax.rem(me + ngx * ngy - 1, ngx * ngy))
    following = flags_of(lax.rem(me + 1, ngx * ngy))

    def count_of(fl):
        return 4 + 3 * (fl[0] + fl[1] + fl[2] + fl[3])

    count = count_of(mine)

    def ge(a, b):
        return jnp.where(a >= b, 1, 0)

    def find(index, fl):
        index = jnp.clip(index, 0, count_of(fl) - 1)
        p1 = 1 + 3 * fl[0]
        p2 = p1 + 1 + 3 * fl[1]
        p3 = p2 + 1 + 3 * fl[2]
        a1, a2, a3 = ge(index, p1), ge(index, p2), ge(index, p3)
        child = index - (a1 * p1 + a2 * (p2 - p1) + a3 * (p3 - p2))
        flag = fl[0] + a1 * (fl[1] - fl[0]) + a2 * (fl[2] - fl[1]) + a3 * (fl[3] - fl[2])
        rx = a2
        ry = a1 + a2 + a3 - 2 * rx
        cx, cy = child & 1, child >> 1
        row = flag * (FINE[0] + 136 * ry + 64 * rx + 32 * cx) + (1 - flag) * (COARSE[0] + 72 * ry + 32 * rx)
        lane = flag * (64 * ry + 32 * cy) + (1 - flag) * 96 * ry - 4
        return row, lane, flag

    place = {w: find(w - excess, mine) for w in range(-3, 13)}
    wide = {}
    for w in range(CAP):
        flag = place[w][2]
        index = w - excess
        if w < 3:
            flag = jnp.where(index >= 0, flag, find(index + count_of(prev), prev)[2])
        if w >= 7:
            flag = jnp.where(index < count, flag, find(index - count, following)[2])
        wide[w] = 0.5 + 0.5 * flag.astype(F32)

    for copy in ghosts:
        copy.wait_recv()
    def fill():
        left8, right8 = lane8 >= 124, lane8 < 4
        left32, right32 = lane32 >= 124, lane32 < 4
        for d in range(2):
            corner = jnp.where(lane8 % 8 < 4, RK[2 * d], RK[2 * d + 1])
            for c in range(8):
                piece = roll(corner, -8 * c - 4)
                row = RB[d, c]
                for i, mask in enumerate((left8, right8)):
                    x = jnp.where(mask, piece, row)
                    fine, coarse = FINE[i] + 132 * d, COARSE[i] + 68 * d
                    G[c, fine : fine + 4, :] = x[0:4]
                    G[c, coarse : coarse + 4, :] = x[4:8]
        for h in range(2):
            low4 = lane32 % 8 < 4
            pair = (jnp.where(low4, RY[0, h], RY[1, h]), jnp.where(low4, RY[1, h], RY[0, h]))
            for cc in range(4):
                for k in range(6):
                    x = roll(pair[k % 2], -(32 * cc + 4 * k) - 4)
                    for i, mask in enumerate((left32, right32)):
                        row = FINE[i] + 4 + 32 * k if k < 4 else COARSE[i] + 4 + 32 * (k - 4)
                        pltpu.store(G.at[4 * h + cc, pl.ds(row, 32), :], x, mask=mask)

    fill()

    def gather(dst, which):
        for c in range(8):
            parts = [roll(G[c, pl.ds(place[w][0], EXT), :], EXT * g - place[w][1]) for g, w in enumerate(which)]
            x = parts[0]
            for g, part in enumerate(parts[1:]):
                x = jnp.where(lane40 < EXT * (g + 1), x, part)
            dst[c] = x

    gather(MR, (10, 11, 12))
    gather(ML, (-3, -2, -1))
    carry_up = lax.div(gy + 1, ngy)
    carry_down = lax.div(ngy - gy, ngy)
    ahead = (lax.rem(gx + carry_up, ngx), lax.rem(gy + 1, ngy))
    behind = (lax.rem(gx + ngx - carry_down, ngx), lax.rem(gy + ngy - 1, ngy))
    moves = [remote(MR, U.at[4], ahead), remote(ML, U.at[5], behind)]
    for copy in moves:
        copy.start()

    gather(U.at[0], (3, 4, 5))
    gather(U.at[1], (6,))
    gather(U.at[2], (0, 1, 2))
    gather(U.at[3], (7, 8, 9))

    def first(t, carry, pick=lambda t: t):
        at_u = pick(t)
        for r in ROWS:
            u = [U[at_u, c, r : r + 8, :] for c in range(8)]
            flux_x, edge_x, flux_y, edge_y = cell_state(u)
            for i, v in enumerate(flux_x + edge_x):
                SX[i, r : r + 8, :] = v
            _, _, a, b, w = edge_weights(*edge_y, roll(edge_y[0], -1), roll(edge_y[1], -1))
            cell = (u[2],) + flux_y[:5] + (None,) + flux_y[5:]
            for c in range(8):
                jump = w * (roll(u[c], -1) - u[c])
                flux = jump if cell[c] is None else a * cell[c] + b * roll(cell[c], -1) + jump
                DY[t, c, r : r + 8, :] = flux - roll(flux, 1)
        for r in FACE1:
            edges = [SX[i, r + d : r + d + 8, :] for d in range(2) for i in (6, 7)]
            _, _, a, b, w = edge_weights(*edges)
            for c in range(8):
                low, high = U[at_u, c, r : r + 8, :], U[at_u, c, r + 1 : r + 9, :]
                flux = w * (high - low)
                if c == 0:
                    flux = a * U[at_u, 1, r : r + 8, :] + b * U[at_u, 1, r + 1 : r + 9, :] + flux
                elif c != 5:
                    i = c - 1 if c < 5 else c - 2
                    flux = a * SX[i, r : r + 8, :] + b * SX[i, r + 1 : r + 9, :] + flux
                GX[t, c, r : r + 8, :] = flux
        return carry

    lax.fori_loop(0, 2, first, 0)

    for copy in round2:
        copy.wait_recv()
    for s in range(ngx - 1):
        peak = jnp.maximum(peak, P2[s])
    peak = jnp.max(jnp.max(peak, axis=0, keepdims=True), axis=1, keepdims=True)
    time_step = COURANT / jnp.broadcast_to(peak, (8, 128))

    def widths(ws):
        v = jnp.full((8, 128), wide[ws[0]], F32)
        for g, w in enumerate(ws[1:]):
            v = jnp.where(lane8 < EXT * (g + 1), v, wide[w])
        return v

    VM[2] = time_step * widths((3, 4, 5))
    VM[3] = time_step * widths((6,))
    VM[4] = time_step * widths((0, 1, 2))
    VM[5] = time_step * widths((7, 8, 9))

    def second(t, carry, pick=lambda t: t):
        rate = VM[2 + t]
        at_u = pick(t)
        half = 0.5 * rate
        for r in MID:
            u = []
            for c in range(8):
                change = GX[t, c, r : r + 8, :] - GX[t, c, r - 1 : r + 7, :] + DY[t, c, r : r + 8, :]
                u.append(U[at_u, c, r : r + 8, :] - half * change)
            _, vx, vy, vz, pressure, _ = primitive(u)
            for c, v in enumerate((u[0], vx, vy, vz, pressure, u[5], u[6], u[7])):
                W[c, r : r + 8, :] = v
        for r in SLOPE:
            for c in range(8):
                w = [W[c, r + d : r + d + 8, :] for d in (-1, 0, 1, 2)]
                low, d, high = w[1] - w[0], w[2] - w[1], w[3] - w[2]
                rise = limited(0.5 * d + (low - high) * (1.0 / 12.0), d)
                RA[c, r : r + 8, :] = rise
                EA[c, r : r + 8, :] = d - rise
        for r in FACE2:
            left, right = [], []
            for c in range(8):
                rise, rise_next = RA[c, r : r + 8, :], RA[c, r + 1 : r + 9, :]
                fall, fall_next = EA[c, r - 1 : r + 7, :], EA[c, r : r + 8, :]
                left.append(W[c, r : r + 8, :] + limited(rise, 2.0 * fall))
                right.append(W[c, r + 1 : r + 9, :] - limited(fall_next, 2.0 * rise_next))
            for c, v in enumerate(face_flux(left, right, 1)):
                GX2[c, r : r + 8, :] = v
        for r in LAST:
            left, right = [], []
            for c in range(8):
                w = W[c, r : r + 8, :]
                ahead_w = roll(w, -1)
                d = ahead_w - w
                rise = limited(0.5 * d + (roll(d, 1) - roll(d, -1)) * (1.0 / 12.0), d)
                fall = d - rise
                left.append(w + limited(rise, 2.0 * roll(fall, 1)))
                right.append(ahead_w - limited(fall, 2.0 * roll(rise, -1)))
            for c, v in enumerate(face_flux(left, right, 2)):
                change = GX2[c, r : r + 8, :] - GX2[c, r - 1 : r + 7, :] + (v - roll(v, 1))
                O[t, c, r - 4 : r + 4, :] = U[at_u, c, r : r + 8, :] - rate * change
        return carry

    lax.fori_loop(0, 2, second, 0)

    for copy in moves:
        copy.wait_recv()

    def pick(t):
        from_left = jnp.where(excess > 0, 4, 2)
        from_right = jnp.where(excess + count < CAP, 5, 3)
        return jnp.where(t == 2, from_left, jnp.where(t == 3, from_right, t))

    lax.fori_loop(2, 4, functools.partial(first, pick=pick), 0)
    lax.fori_loop(2, 4, functools.partial(second, pick=pick), 0)

    def finish():
        for c in range(8):
            o = [O[t, c] for t in range(4)]
            o0 = jnp.where(lane32 < 32, roll(o[2], -4), jnp.where(lane32 < 64, roll(o[2], -12), roll(o[2], -20)))
            out[c, :, 0:128] = jnp.where(lane32 < 96, o0, roll(o[0], 92))
            o1 = jnp.where(lane32 < 32, roll(o[0], -44), roll(o[0], -52))
            out[c, :, 128:256] = jnp.where(lane32 < 64, o1, jnp.where(lane32 < 96, roll(o[1], 60), roll(o[3], 92)))
            o2 = jnp.where(lane32 < 32, roll(o[3], -44), roll(o[3], -52))
            out[c, :, 256:320] = o2[:, 0:64]

    finish()

    for copy in ghosts + moves + round1 + round2:
        copy.wait_send()


def shards(ngx, ngy, fields, refined):
    vmem = lambda *shape: pltpu.VMEM(shape, F32)
    scratch = [
        vmem(8, 2, BS, 128),
        vmem(8, PAD_ROWS, 128),
        vmem(6, 8, EXT, 128),
        vmem(8, EXT, 128),
        vmem(8, EXT, 128),
        vmem(2, 8, 8, 128),
        vmem(2, 8, 8, 128),
        vmem(2, 8, 128),
        vmem(4, 8, 128),
        vmem(2, 2, 32, 128),
        vmem(2, 2, 32, 128),
        vmem(6, 8, 128),
        vmem(ngy - 1, 8, 128),
        vmem(ngx - 1, 8, 128),
        vmem(8, EXT, 128),
        vmem(4, 8, EXT, 128),
        vmem(4, 8, EXT, 128),
        vmem(8, EXT, 128),
        vmem(8, EXT, 128),
        vmem(8, EXT, 128),
        vmem(8, EXT, 128),
        vmem(4, 8, BS, 128),
        pltpu.SemaphoreType.DMA((ngx + ngy + 8,)),
        pltpu.SemaphoreType.DMA((ngx + ngy + 8,)),
    ]
    return pl.pallas_call(
        functools.partial(kernel, ngx, ngy),
        out_shape=jax.ShapeDtypeStruct((8, BS, CAP * BS), F32),
        in_specs=[
            pl.BlockSpec(memory_space=pltpu.SMEM),
            pl.BlockSpec(memory_space=pltpu.VMEM),
            pl.BlockSpec(memory_space=pltpu.VMEM),
        ],
        out_specs=pl.BlockSpec(memory_space=pltpu.VMEM),
        scratch_shapes=scratch,
        compiler_params=pltpu.CompilerParams(
            collective_id=0, has_side_effects=True, vmem_limit_bytes=32 * 1024 * 1024
        ),
    )(refined.T, refined.T, fields)


def solution(mesh):
    ngx, ngy = mesh.shape["gx"], mesh.shape["gy"]
    return jax.shard_map(
        functools.partial(shards, ngx, ngy),
        mesh=mesh,
        in_specs=(P(None, None, ("gx", "gy")), P()),
        out_specs=P(None, None, ("gx", "gy")),
        check_vma=False,
    )
```

```python
import functools

import jax
import jax.numpy as jnp
from jax import lax
from jax.experimental import pallas as pl
from jax.experimental.pallas import tpu as pltpu
from jax.sharding import PartitionSpec as P

BS = 32
CAP = 10
EXT = BS + 8
GAMMA = 5.0 / 3.0
COURANT = 0.2
MESH = pl.DeviceIdType.MESH
F32 = jnp.float32

FINE = (4, 140)
COARSE = (276, 348)
PAD_ROWS = 424
ROWS = (0, 8, 16, 24, 32)
FACE1 = (0, 8, 16, 24, 31)
MID = (1, 9, 17, 25, 31)
SLOPE = (2, 10, 18, 26, 29)
FACE2 = (3, 11, 19, 27, 28)
LAST = (4, 12, 20, 28)


def lanes(rows):
    return lax.broadcasted_iota(jnp.int32, (rows, 128), 1)


def roll(x, by):
    if isinstance(by, int):
        by = by % 128
        return x if by == 0 else pltpu.roll(x, by, 1)
    return pltpu.roll(x, lax.rem(by + 256, 128), 1)


def recip(x):
    return pltpu.reciprocal(x, approx=True)


def root(x):
    return x * lax.rsqrt(jnp.maximum(x, 1e-30))


def limited(value, other):
    return jnp.minimum(jnp.maximum(value, jnp.minimum(other, 0.0)), jnp.maximum(other, 0.0))


def primitive(u):
    rho, mx, my, mz, energy, bx, by, bz = u
    inv = recip(rho)
    vx, vy, vz = mx * inv, my * inv, mz * inv
    half_b2 = 0.5 * (bx * bx + by * by + bz * bz)
    kinetic = 0.5 * (mx * vx + my * vy + mz * vz)
    pressure = (GAMMA - 1.0) * (energy - kinetic - half_b2)
    return inv, vx, vy, vz, pressure, half_b2


def fast_pair(inv, pressure, half_b2, trans_x, trans_y):
    sound = GAMMA * pressure * inv
    alfven = 2.0 * half_b2 * inv
    total = sound + alfven
    diff = sound - alfven
    square = diff * diff
    four = 4.0 * sound * inv
    fast_x = root(0.5 * (total + root(square + four * trans_x)))
    fast_y = root(0.5 * (total + root(square + four * trans_y)))
    return fast_x, fast_y


def cell_state(u):
    rho, mx, my, mz, energy, bx, by, bz = u
    inv, vx, vy, vz, pressure, half_b2 = primitive(u)
    xx, yy, zz = bx * bx, by * by, bz * bz
    fast_x, fast_y = fast_pair(inv, pressure, half_b2, yy + zz, xx + zz)
    total_p = pressure + half_b2
    enthalpy = energy + total_p
    vb = vx * bx + vy * by + vz * bz
    cross = mx * vy - bx * by
    emf = by * vx - bx * vy
    flux_x = (mx * vx + total_p - xx, cross, mx * vz - bx * bz, enthalpy * vx - bx * vb, emf, bz * vx - bx * vz)
    flux_y = (cross, my * vy + total_p - yy, my * vz - by * bz, enthalpy * vy - by * vb, -emf, bz * vy - by * vz)
    return flux_x, (vx - fast_x, vx + fast_x), flux_y, (vy - fast_y, vy + fast_y)


def edge_weights(slow_l, fast_l, slow_r, fast_r):
    slow = jnp.minimum(jnp.minimum(slow_l, slow_r), 0.0)
    fast = jnp.maximum(jnp.maximum(fast_l, fast_r), 0.0)
    inv = recip(fast - slow)
    a = fast * inv
    b = -slow * inv
    return slow, fast, a, b, slow * a


def side(w, normal):
    rho, vx, vy, vz, pressure, bx, by, bz = w
    vn, vt, bn, bt = (vx, vy, bx, by) if normal == 1 else (vy, vx, by, bx)
    inv = recip(rho)
    trans = bt * bt + bz * bz
    nn = bn * bn
    b2 = trans + nn
    sound = GAMMA * pressure * inv
    alfven = b2 * inv
    diff = sound - alfven
    fast = root(0.5 * (sound + alfven + root(diff * diff + 4.0 * sound * inv * trans)))
    half_b2 = 0.5 * b2
    total_p = pressure + half_b2
    energy = 1.5 * pressure + half_b2 + 0.5 * rho * (vn * vn + vt * vt + vz * vz)
    vb = vn * bn + vt * bt + vz * bz
    return vn - fast, vn + fast, (rho, vn, vt, vz, bn, bt, bz, energy, total_p, total_p - nn, vb)


def moved(state, speed):
    rho, vn, vt, vz, bn, bt, bz, energy, total_p, stress, vb = state
    rel = vn - speed
    mass = rho * rel
    return (
        mass,
        mass * vn + stress,
        mass * vt - bn * bt,
        mass * vz - bn * bz,
        energy * rel + total_p * vn - bn * vb,
        bt * rel - bn * vt,
        bz * rel - bn * vz,
    )


def face_flux(left, right, normal):
    slow_l, fast_l, state_l = side(left, normal)
    slow_r, fast_r, state_r = side(right, normal)
    slow, fast, a, b, c = edge_weights(slow_l, fast_l, slow_r, fast_r)
    from_l = moved(state_l, slow)
    from_r = moved(state_r, fast)
    mass, mn, mt, mz, en, bt, bz = (a * p + b * q for p, q in zip(from_l, from_r))
    bn = c * (state_r[4] - state_l[4])
    if normal == 1:
        return (mass, mn, mt, mz, en, bn, bt, bz)
    return (mass, mt, mn, mz, en, bt, bn, bz)


def kernel(ngx, ngy, refined, fields, out, *scratch):
    (ref_s, ref_v, X, Z, G, U, ML, MR, SR, RB, SK, RK, SY, RY, VM, VS, P1, P2, SX, GX, DY, W, RA, EA, GX2, O, in_sem, send, recv) = scratch
    gx = lax.axis_index("gx")
    gy = lax.axis_index("gy")
    me = gx * ngy + gy
    load = pltpu.make_async_copy(fields, X, in_sem.at[0])
    load.start()
    load_s = pltpu.make_async_copy(refined, ref_s, in_sem.at[1])
    load_s.start()
    load_v = pltpu.make_async_copy(refined, ref_v, in_sem.at[2])
    load_v.start()

    def at(dx, dy):
        return lax.rem(gx + dx + ngx, ngx), lax.rem(gy + dy + ngy, ngy)

    partners = [at(0, s) for s in range(1, ngy)] + [at(s, 0) for s in range(1, ngx)]
    partners += [at(1, 1), at(1, -1), at(-1, 1), at(-1, -1)]
    barrier = pltpu.get_barrier_semaphore()
    for who in partners:
        pl.semaphore_signal(barrier, inc=1, device_id=who, device_id_type=MESH)

    sems = iter(range(64))

    def remote(src, dst, who):
        i = next(sems)
        return pltpu.make_async_remote_copy(
            src_ref=src, dst_ref=dst, send_sem=send.at[i], recv_sem=recv.at[i], device_id=who, device_id_type=MESH
        )

    def flags_of(tile):
        tx, ty = lax.div(tile, ngy), lax.rem(tile, ngy)
        return [ref_s[2 * ty + r % 2, 2 * tx + r // 2] for r in range(4)]

    load_s.wait()
    mine = flags_of(me)
    lane8, lane32, lane40 = lanes(8), lanes(32), lanes(EXT)
    load.wait()

    zero8 = jnp.zeros((8, 128), F32)
    peak = zero8
    for r in range(4):
        on = mine[r] > 0
        weight = jnp.where(lane8 < 32, jnp.where(on, 1.0, 0.5), jnp.where(on, 1.0, 0.0)).astype(F32)
        for q in range(4):
            u = [X[c, 8 * q : 8 * q + 8, 128 * r : 128 * r + 128] for c in range(8)]
            inv, vx, vy, vz, pressure, half_b2 = primitive(u)
            xx, yy, zz = (b * b for b in u[5:])
            fast_x, fast_y = fast_pair(inv, pressure, half_b2, yy + zz, xx + zz)
            rate = jnp.maximum(jnp.abs(vx) + fast_x, jnp.abs(vy) + fast_y)
            peak = jnp.maximum(peak, jnp.where(weight > 0.0, rate * weight, 0.0))
    VS[0] = jnp.max(peak, axis=0, keepdims=True)

    def rotate(h, carry):
        for cc in range(4):
            c = 4 * h + cc
            for rx in range(2):
                for q in range(4):
                    a = X[c, 8 * q : 8 * q + 8, 256 * rx : 256 * rx + 128]
                    b = X[c, 8 * q : 8 * q + 8, 256 * rx + 128 : 256 * rx + 256]
                    a32, b32 = roll(a, -32), roll(b, 32)
                    top = jnp.where(lane8 < 32, a, jnp.where(lane8 < 64, a32, jnp.where(lane8 < 96, roll(b, 64), b32)))
                    low = jnp.where(lane8 < 32, a32, jnp.where(lane8 < 64, roll(a, -64), jnp.where(lane8 < 96, b32, b)))
                    row = FINE[0] + 4 + 64 * rx + 8 * q
                    G[c, row : row + 8, :] = top
                    G[c, row + 32 : row + 40, :] = low
                    Z[c, rx, 8 * q : 8 * q + 8, :] = jnp.where(lane8 < 32, a, b32)
        return carry

    def spread(h, carry):
        row8 = lax.broadcasted_iota(jnp.int32, (8, 128), 0)
        half = row8 % 4 * 2
        halves = lane8 * 2 % 128
        for cc in range(4):
            c = 4 * h + cc
            for rx in range(2):
                keep = jnp.where(lane8 < 64, mine[2 * rx], mine[2 * rx + 1]) > 0
                fine = []
                for q in range(4):
                    z = jnp.take_along_axis(Z[c, rx, 8 * q : 8 * q + 8, :], lane8 // 2, axis=1)
                    for i in range(2):
                        row = FINE[0] + 4 + 64 * rx + 16 * q + 8 * i
                        x = jnp.take_along_axis(z, row8 // 2 + 4 * i, axis=0)
                        x = jnp.where(keep, G[c, row : row + 8, :], x)
                        G[c, row : row + 8, :] = x
                        G[c, row + 136 : row + 144, :] = x
                        x = x + pltpu.roll(x, 7, 0)
                        fine.append(jnp.take_along_axis(x, half, axis=0))
                for q in range(4):
                    x = jnp.where(row8 < 4, fine[2 * q], fine[2 * q + 1])
                    x = 0.25 * (jnp.take_along_axis(x, halves, axis=1) + jnp.take_along_axis(x, halves + 1, axis=1))
                    for base in COARSE:
                        row = base + 4 + 32 * rx + 8 * q
                        G[c, row : row + 8, :] = x
        return carry

    lax.fori_loop(0, 2, rotate, 0)
    lax.fori_loop(0, 2, spread, 0)

    def pack_columns():
        for h in range(2):
            for q in range(4):
                acc_r, acc_l = zero8, zero8
                for cc in range(4):
                    for k in range(6):
                        s = 32 * cc + 4 * k
                        row = (FINE[0] + 4 + 32 * k if k < 4 else COARSE[0] + 4 + 32 * (k - 4)) + 8 * q
                        x = roll(G[4 * h + cc, row : row + 8, :], s + 4)
                        acc_r = jnp.where((lane8 >= s) & (lane8 < s + 4), x, acc_r)
                        acc_l = jnp.where((lane8 >= s + 4) & (lane8 < s + 8), x, acc_l)
                SY[0, h, 8 * q : 8 * q + 8, :] = acc_r
                SY[1, h, 8 * q : 8 * q + 8, :] = acc_l

    pack_columns()

    def pack_rows():
        for d in range(2):
            corner = zero8
            fine, coarse = FINE[0] + 4 + (124, 0)[d], COARSE[0] + 4 + (60, 0)[d]
            for c in range(8):
                SR[d, c, 0:4, :] = G[c, fine : fine + 4, :]
                SR[d, c, 4:8, :] = G[c, coarse : coarse + 4, :]
                corner = jnp.where(lane8 // 8 == c, roll(SR[d, c], 8 * c + 4), corner)
            SK[d] = corner

    pack_rows()

    ghosts = [
        remote(SY.at[0], RY.at[0], at(0, 1)),
        remote(SY.at[1], RY.at[1], at(0, -1)),
        remote(SR.at[0], RB.at[0], at(1, 0)),
        remote(SR.at[1], RB.at[1], at(-1, 0)),
        remote(SK.at[0], RK.at[0], at(1, 1)),
        remote(SK.at[0], RK.at[1], at(1, -1)),
        remote(SK.at[1], RK.at[2], at(-1, 1)),
        remote(SK.at[1], RK.at[3], at(-1, -1)),
    ]
    round1 = [remote(VS.at[0], P1.at[s - 1], at(0, s)) for s in range(1, ngy)]
    pl.semaphore_wait(barrier, len(partners))
    for copy in ghosts + round1:
        copy.start()

    load_v.wait()
    tile_of = lax.broadcasted_iota(jnp.int32, (2 * ngy, 2 * ngx), 1) // 2 * ngy
    tile_of = tile_of + lax.broadcasted_iota(jnp.int32, (2 * ngy, 2 * ngx), 0) // 2
    before = jnp.sum(jnp.where(tile_of < me, ref_v[...], 0))
    excess = 4 * me + 3 * before - CAP * me
    prev = flags_of(lax.rem(me + ngx * ngy - 1, ngx * ngy))
    following = flags_of(lax.rem(me + 1, ngx * ngy))

    def count_of(fl):
        return 4 + 3 * (fl[0] + fl[1] + fl[2] + fl[3])

    count = count_of(mine)

    def ge(a, b):
        return jnp.where(a >= b, 1, 0)

    def find(index, fl):
        index = jnp.clip(index, 0, count_of(fl) - 1)
        p1 = 1 + 3 * fl[0]
        p2 = p1 + 1 + 3 * fl[1]
        p3 = p2 + 1 + 3 * fl[2]
        a1, a2, a3 = ge(index, p1), ge(index, p2), ge(index, p3)
        child = index - (a1 * p1 + a2 * (p2 - p1) + a3 * (p3 - p2))
        flag = fl[0] + a1 * (fl[1] - fl[0]) + a2 * (fl[2] - fl[1]) + a3 * (fl[3] - fl[2])
        rx = a2
        ry = a1 + a2 + a3 - 2 * rx
        cx, cy = child & 1, child >> 1
        row = flag * (FINE[0] + 136 * ry + 64 * rx + 32 * cx) + (1 - flag) * (COARSE[0] + 72 * ry + 32 * rx)
        lane = flag * (64 * ry + 32 * cy) + (1 - flag) * 96 * ry - 4
        return row, lane, flag

    place = {w: find(w - excess, mine) for w in range(-3, 13)}
    wide = {}
    for w in range(CAP):
        flag = place[w][2]
        index = w - excess
        if w < 3:
            flag = jnp.where(index >= 0, flag, find(index + count_of(prev), prev)[2])
        if w >= 7:
            flag = jnp.where(index < count, flag, find(index - count, following)[2])
        wide[w] = 0.5 + 0.5 * flag.astype(F32)

    for copy in round1:
        copy.wait_recv()
    top = VS[0]
    for s in range(ngy - 1):
        top = jnp.maximum(top, P1[s])
    VS[1] = top
    round2 = [remote(VS.at[1], P2.at[s - 1], at(s, 0)) for s in range(1, ngx)]
    for copy in round2:
        copy.start()

    for copy in ghosts:
        copy.wait_recv()
    def fill():
        left8, right8 = lane8 >= 124, lane8 < 4
        left32, right32 = lane32 >= 124, lane32 < 4
        for d in range(2):
            corner = jnp.where(lane8 % 8 < 4, RK[2 * d], RK[2 * d + 1])
            for c in range(8):
                piece = roll(corner, -8 * c - 4)
                row = RB[d, c]
                for i, mask in enumerate((left8, right8)):
                    x = jnp.where(mask, piece, row)
                    fine, coarse = FINE[i] + 132 * d, COARSE[i] + 68 * d
                    G[c, fine : fine + 4, :] = x[0:4]
                    G[c, coarse : coarse + 4, :] = x[4:8]
        for h in range(2):
            low4 = lane32 % 8 < 4
            pair = (jnp.where(low4, RY[0, h], RY[1, h]), jnp.where(low4, RY[1, h], RY[0, h]))
            for cc in range(4):
                for k in range(6):
                    x = roll(pair[k % 2], -(32 * cc + 4 * k) - 4)
                    for i, mask in enumerate((left32, right32)):
                        row = FINE[i] + 4 + 32 * k if k < 4 else COARSE[i] + 4 + 32 * (k - 4)
                        pltpu.store(G.at[4 * h + cc, pl.ds(row, 32), :], x, mask=mask)

    fill()

    def gather(dst, which):
        for c in range(8):
            parts = [roll(G[c, pl.ds(place[w][0], EXT), :], EXT * g - place[w][1]) for g, w in enumerate(which)]
            x = parts[0]
            for g, part in enumerate(parts[1:]):
                x = jnp.where(lane40 < EXT * (g + 1), x, part)
            dst[c] = x

    gather(MR, (10, 11, 12))
    gather(ML, (-3, -2, -1))
    carry_up = lax.div(gy + 1, ngy)
    carry_down = lax.div(ngy - gy, ngy)
    ahead = (lax.rem(gx + carry_up, ngx), lax.rem(gy + 1, ngy))
    behind = (lax.rem(gx + ngx - carry_down, ngx), lax.rem(gy + ngy - 1, ngy))
    moves = [remote(MR, U.at[4], ahead), remote(ML, U.at[5], behind)]
    for copy in moves:
        copy.start()

    gather(U.at[0], (3, 4, 5))
    gather(U.at[1], (6,))
    gather(U.at[2], (0, 1, 2))
    gather(U.at[3], (7, 8, 9))

    def first(t, carry, pick=lambda t: t):
        at_u = pick(t)
        for r in ROWS:
            u = [U[at_u, c, r : r + 8, :] for c in range(8)]
            flux_x, edge_x, flux_y, edge_y = cell_state(u)
            for i, v in enumerate(flux_x + edge_x):
                SX[i, r : r + 8, :] = v
            _, _, a, b, w = edge_weights(*edge_y, roll(edge_y[0], -1), roll(edge_y[1], -1))
            cell = (u[2],) + flux_y[:5] + (None,) + flux_y[5:]
            for c in range(8):
                jump = w * (roll(u[c], -1) - u[c])
                flux = jump if cell[c] is None else a * cell[c] + b * roll(cell[c], -1) + jump
                DY[t, c, r : r + 8, :] = flux - roll(flux, 1)
        for r in FACE1:
            edges = [SX[i, r + d : r + d + 8, :] for d in range(2) for i in (6, 7)]
            _, _, a, b, w = edge_weights(*edges)
            for c in range(8):
                low, high = U[at_u, c, r : r + 8, :], U[at_u, c, r + 1 : r + 9, :]
                flux = w * (high - low)
                if c == 0:
                    flux = a * U[at_u, 1, r : r + 8, :] + b * U[at_u, 1, r + 1 : r + 9, :] + flux
                elif c != 5:
                    i = c - 1 if c < 5 else c - 2
                    flux = a * SX[i, r : r + 8, :] + b * SX[i, r + 1 : r + 9, :] + flux
                GX[t, c, r : r + 8, :] = flux
        return carry

    lax.fori_loop(0, 2, first, 0)

    for copy in round2:
        copy.wait_recv()
    for s in range(ngx - 1):
        top = jnp.maximum(top, P2[s])
    top = jnp.max(top, axis=1, keepdims=True)
    time_step = COURANT / jnp.broadcast_to(top, (8, 128))

    def widths(ws):
        v = jnp.full((8, 128), wide[ws[0]], F32)
        for g, w in enumerate(ws[1:]):
            v = jnp.where(lane8 < EXT * (g + 1), v, wide[w])
        return v

    VM[0] = time_step * widths((3, 4, 5))
    VM[1] = time_step * widths((6,))
    VM[2] = time_step * widths((0, 1, 2))
    VM[3] = time_step * widths((7, 8, 9))

    def second(t, carry, pick=lambda t: t):
        rate = VM[t]
        at_u = pick(t)
        half = 0.5 * rate
        for r in MID:
            u = []
            for c in range(8):
                change = GX[t, c, r : r + 8, :] - GX[t, c, r - 1 : r + 7, :] + DY[t, c, r : r + 8, :]
                u.append(U[at_u, c, r : r + 8, :] - half * change)
            _, vx, vy, vz, pressure, _ = primitive(u)
            for c, v in enumerate((u[0], vx, vy, vz, pressure, u[5], u[6], u[7])):
                W[c, r : r + 8, :] = v
        for r in SLOPE:
            for c in range(8):
                w = [W[c, r + d : r + d + 8, :] for d in (-1, 0, 1, 2)]
                low, d, high = w[1] - w[0], w[2] - w[1], w[3] - w[2]
                rise = limited(0.5 * d + (low - high) * (1.0 / 12.0), d)
                RA[c, r : r + 8, :] = rise
                EA[c, r : r + 8, :] = d - rise
        for r in FACE2:
            left, right = [], []
            for c in range(8):
                rise, rise_next = RA[c, r : r + 8, :], RA[c, r + 1 : r + 9, :]
                fall, fall_next = EA[c, r - 1 : r + 7, :], EA[c, r : r + 8, :]
                left.append(W[c, r : r + 8, :] + limited(rise, 2.0 * fall))
                right.append(W[c, r + 1 : r + 9, :] - limited(fall_next, 2.0 * rise_next))
            for c, v in enumerate(face_flux(left, right, 1)):
                GX2[c, r : r + 8, :] = v
        for r in LAST:
            left, right = [], []
            for c in range(8):
                w = W[c, r : r + 8, :]
                ahead_w = roll(w, -1)
                d = ahead_w - w
                rise = limited(0.5 * d + (roll(d, 1) - roll(d, -1)) * (1.0 / 12.0), d)
                fall = d - rise
                left.append(w + limited(rise, 2.0 * roll(fall, 1)))
                right.append(ahead_w - limited(fall, 2.0 * roll(rise, -1)))
            for c, v in enumerate(face_flux(left, right, 2)):
                change = GX2[c, r : r + 8, :] - GX2[c, r - 1 : r + 7, :] + (v - roll(v, 1))
                O[t, c, r - 4 : r + 4, :] = U[at_u, c, r : r + 8, :] - rate * change
        return carry

    lax.fori_loop(0, 2, second, 0)

    def finish_local():
        for c in range(8):
            o0, o1 = O[0, c], O[1, c]
            out[c, :, 0:128] = roll(o0, 92)
            x = jnp.where(lane32 < 64, roll(o0, -52), roll(o1, 60))
            out[c, :, 128:256] = jnp.where(lane32 < 32, roll(o0, -44), x)

    finish_local()

    for copy in moves:
        copy.wait_recv()

    def pick(t):
        from_left = jnp.where(excess > 0, 4, 2)
        from_right = jnp.where(excess + count < CAP, 5, 3)
        return jnp.where(t == 2, from_left, jnp.where(t == 3, from_right, t))

    lax.fori_loop(2, 4, functools.partial(first, pick=pick), 0)
    lax.fori_loop(2, 4, functools.partial(second, pick=pick), 0)

    def finish():
        for c in range(8):
            o2, o3 = O[2, c], O[3, c]
            x = jnp.where(lane32 < 32, roll(o2, -4), jnp.where(lane32 < 64, roll(o2, -12), roll(o2, -20)))
            pltpu.store(out.at[c, :, pl.ds(0, 128)], x, mask=lane32 < 96)
            pltpu.store(out.at[c, :, pl.ds(128, 128)], roll(o3, 92), mask=lane32 >= 96)
            x = jnp.where(lane32 < 32, roll(o3, -44), roll(o3, -52))
            out[c, :, 256:320] = x[:, 0:64]

    finish()

    for copy in ghosts + moves + round1 + round2:
        copy.wait_send()


def shards(ngx, ngy, fields, refined):
    vmem = lambda *shape: pltpu.VMEM(shape, F32)
    scratch = [
        pltpu.SMEM((2 * ngy, 2 * ngx), jnp.int32),
        pltpu.VMEM((2 * ngy, 2 * ngx), jnp.int32),
        vmem(8, 32, 512),
        vmem(8, 2, BS, 128),
        vmem(8, PAD_ROWS, 128),
        vmem(6, 8, EXT, 128),
        vmem(8, EXT, 128),
        vmem(8, EXT, 128),
        vmem(2, 8, 8, 128),
        vmem(2, 8, 8, 128),
        vmem(2, 8, 128),
        vmem(4, 8, 128),
        vmem(2, 2, 32, 128),
        vmem(2, 2, 32, 128),
        vmem(4, 8, 128),
        vmem(2, 1, 128),
        vmem(ngy - 1, 1, 128),
        vmem(ngx - 1, 1, 128),
        vmem(8, EXT, 128),
        vmem(4, 8, EXT, 128),
        vmem(4, 8, EXT, 128),
        vmem(8, EXT, 128),
        vmem(8, EXT, 128),
        vmem(8, EXT, 128),
        vmem(8, EXT, 128),
        vmem(4, 8, BS, 128),
        pltpu.SemaphoreType.DMA((3,)),
        pltpu.SemaphoreType.DMA((ngx + ngy + 8,)),
        pltpu.SemaphoreType.DMA((ngx + ngy + 8,)),
    ]
    return pl.pallas_call(
        functools.partial(kernel, ngx, ngy),
        out_shape=jax.ShapeDtypeStruct((8, BS, CAP * BS), F32),
        in_specs=[
            pl.BlockSpec(memory_space=pltpu.HBM),
            pl.BlockSpec(memory_space=pltpu.HBM),
        ],
        out_specs=pl.BlockSpec(memory_space=pltpu.VMEM),
        scratch_shapes=scratch,
        compiler_params=pltpu.CompilerParams(
            collective_id=0, has_side_effects=True, vmem_limit_bytes=56_000_000
        ),
    )(refined.T, fields)


def solution(mesh):
    ngx, ngy = mesh.shape["gx"], mesh.shape["gy"]
    return jax.shard_map(
        functools.partial(shards, ngx, ngy),
        mesh=mesh,
        in_specs=(P(None, None, ("gx", "gy")), P()),
        out_specs=P(None, None, ("gx", "gy")),
        check_vma=False,
    )
```

```python
import functools

import jax
import jax.numpy as jnp
from jax import lax
from jax.experimental import pallas as pl
from jax.experimental.pallas import tpu as pltpu
from jax.sharding import PartitionSpec as P

BS = 32
CAP = 10
EXT = BS + 8
GAMMA = 5.0 / 3.0
COURANT = 0.2
MESH = pl.DeviceIdType.MESH
F32 = jnp.float32

FINE = (4, 140)
COARSE = (276, 348)
PAD_ROWS = 424
ROWS = (0, 8, 16, 24, 32)
FACE1 = (0, 8, 16, 24, 31)
MID = (1, 9, 17, 25, 31)
SLOPE = (2, 10, 18, 26, 29)
FACE2 = (3, 11, 19, 27, 28)
LAST = (4, 12, 20, 28)


def lanes(rows):
    return lax.broadcasted_iota(jnp.int32, (rows, 128), 1)


def roll(x, by):
    if isinstance(by, int):
        by = by % 128
        return x if by == 0 else pltpu.roll(x, by, 1)
    return pltpu.roll(x, lax.rem(by + 256, 128), 1)


def recip(x):
    return pltpu.reciprocal(x, approx=True)


def root(x):
    return x * lax.rsqrt(jnp.maximum(x, 1e-30))


def limited(value, other):
    return jnp.minimum(jnp.maximum(value, jnp.minimum(other, 0.0)), jnp.maximum(other, 0.0))


def primitive(u):
    rho, mx, my, mz, energy, bx, by, bz = u
    inv = recip(rho)
    vx, vy, vz = mx * inv, my * inv, mz * inv
    half_b2 = 0.5 * (bx * bx + by * by + bz * bz)
    kinetic = 0.5 * (mx * vx + my * vy + mz * vz)
    pressure = (GAMMA - 1.0) * (energy - kinetic - half_b2)
    return inv, vx, vy, vz, pressure, half_b2


def fast_pair(inv, pressure, half_b2, trans_x, trans_y):
    sound = GAMMA * pressure * inv
    alfven = 2.0 * half_b2 * inv
    total = sound + alfven
    diff = sound - alfven
    square = diff * diff
    four = 4.0 * sound * inv
    fast_x = root(0.5 * (total + root(square + four * trans_x)))
    fast_y = root(0.5 * (total + root(square + four * trans_y)))
    return fast_x, fast_y


def cell_state(u):
    rho, mx, my, mz, energy, bx, by, bz = u
    inv, vx, vy, vz, pressure, half_b2 = primitive(u)
    xx, yy, zz = bx * bx, by * by, bz * bz
    fast_x, fast_y = fast_pair(inv, pressure, half_b2, yy + zz, xx + zz)
    total_p = pressure + half_b2
    enthalpy = energy + total_p
    vb = vx * bx + vy * by + vz * bz
    cross = mx * vy - bx * by
    emf = by * vx - bx * vy
    flux_x = (mx * vx + total_p - xx, cross, mx * vz - bx * bz, enthalpy * vx - bx * vb, emf, bz * vx - bx * vz)
    flux_y = (cross, my * vy + total_p - yy, my * vz - by * bz, enthalpy * vy - by * vb, -emf, bz * vy - by * vz)
    return flux_x, (vx - fast_x, vx + fast_x), flux_y, (vy - fast_y, vy + fast_y)


def edge_weights(slow_l, fast_l, slow_r, fast_r):
    slow = jnp.minimum(jnp.minimum(slow_l, slow_r), 0.0)
    fast = jnp.maximum(jnp.maximum(fast_l, fast_r), 0.0)
    inv = recip(fast - slow)
    a = fast * inv
    b = -slow * inv
    return slow, fast, a, b, slow * a


def side(w, normal):
    rho, vx, vy, vz, pressure, bx, by, bz = w
    vn, vt, bn, bt = (vx, vy, bx, by) if normal == 1 else (vy, vx, by, bx)
    inv = recip(rho)
    trans = bt * bt + bz * bz
    nn = bn * bn
    b2 = trans + nn
    sound = GAMMA * pressure * inv
    alfven = b2 * inv
    diff = sound - alfven
    fast = root(0.5 * (sound + alfven + root(diff * diff + 4.0 * sound * inv * trans)))
    half_b2 = 0.5 * b2
    total_p = pressure + half_b2
    energy = 1.5 * pressure + half_b2 + 0.5 * rho * (vn * vn + vt * vt + vz * vz)
    vb = vn * bn + vt * bt + vz * bz
    return vn - fast, vn + fast, (rho, vn, vt, vz, bn, bt, bz, energy, total_p, total_p - nn, vb)


def moved(state, speed):
    rho, vn, vt, vz, bn, bt, bz, energy, total_p, stress, vb = state
    rel = vn - speed
    mass = rho * rel
    return (
        mass,
        mass * vn + stress,
        mass * vt - bn * bt,
        mass * vz - bn * bz,
        energy * rel + total_p * vn - bn * vb,
        bt * rel - bn * vt,
        bz * rel - bn * vz,
    )


def face_flux(left, right, normal):
    slow_l, fast_l, state_l = side(left, normal)
    slow_r, fast_r, state_r = side(right, normal)
    slow, fast, a, b, c = edge_weights(slow_l, fast_l, slow_r, fast_r)
    from_l = moved(state_l, slow)
    from_r = moved(state_r, fast)
    mass, mn, mt, mz, en, bt, bz = (a * p + b * q for p, q in zip(from_l, from_r))
    bn = c * (state_r[4] - state_l[4])
    if normal == 1:
        return (mass, mn, mt, mz, en, bn, bt, bz)
    return (mass, mt, mn, mz, en, bt, bn, bz)


def kernel(ngx, ngy, refined, fields, out, *scratch):
    (ref_s, ref_v, X, Z, G, U, ML, MR, SR, RB, SK, RK, SY, RY, VM, VS, P1, P2, SX, GX, DY, W, RA, EA, GX2, O, in_sem, send, recv) = scratch
    gx = lax.axis_index("gx")
    gy = lax.axis_index("gy")
    me = gx * ngy + gy
    load = pltpu.make_async_copy(fields, X, in_sem.at[0])
    load.start()
    load_s = pltpu.make_async_copy(refined, ref_s, in_sem.at[1])
    load_s.start()
    load_v = pltpu.make_async_copy(refined, ref_v, in_sem.at[2])
    load_v.start()

    def at(dx, dy):
        return lax.rem(gx + dx + ngx, ngx), lax.rem(gy + dy + ngy, ngy)

    partners = [at(0, s) for s in range(1, ngy)] + [at(s, 0) for s in range(1, ngx)]
    partners += [at(1, 1), at(1, -1), at(-1, 1), at(-1, -1)]
    barrier = pltpu.get_barrier_semaphore()
    for who in partners:
        pl.semaphore_signal(barrier, inc=1, device_id=who, device_id_type=MESH)

    sems = iter(range(64))

    def remote(src, dst, who):
        i = next(sems)
        return pltpu.make_async_remote_copy(
            src_ref=src, dst_ref=dst, send_sem=send.at[i], recv_sem=recv.at[i], device_id=who, device_id_type=MESH
        )

    def flags_of(tile):
        tx, ty = lax.div(tile, ngy), lax.rem(tile, ngy)
        return [ref_s[2 * ty + r % 2, 2 * tx + r // 2] for r in range(4)]

    load_s.wait()
    mine = flags_of(me)
    lane8, lane32, lane40 = lanes(8), lanes(32), lanes(EXT)
    load.wait()

    zero8 = jnp.zeros((8, 128), F32)
    peak = zero8
    for r in range(4):
        on = mine[r] > 0
        weight = jnp.where(lane8 < 32, jnp.where(on, 1.0, 0.5), jnp.where(on, 1.0, 0.0)).astype(F32)
        for q in range(4):
            u = [X[c, 8 * q : 8 * q + 8, 128 * r : 128 * r + 128] for c in range(8)]
            inv, vx, vy, vz, pressure, half_b2 = primitive(u)
            xx, yy, zz = (b * b for b in u[5:])
            fast_x, fast_y = fast_pair(inv, pressure, half_b2, yy + zz, xx + zz)
            rate = jnp.maximum(jnp.abs(vx) + fast_x, jnp.abs(vy) + fast_y)
            peak = jnp.maximum(peak, jnp.where(weight > 0.0, rate * weight, 0.0))
    VS[0] = jnp.max(peak, axis=0, keepdims=True)

    def rotate(h, carry):
        for cc in range(4):
            c = 4 * h + cc
            for rx in range(2):
                for q in range(4):
                    a = X[c, 8 * q : 8 * q + 8, 256 * rx : 256 * rx + 128]
                    b = X[c, 8 * q : 8 * q + 8, 256 * rx + 128 : 256 * rx + 256]
                    a32, b32 = roll(a, -32), roll(b, 32)
                    top = jnp.where(lane8 < 32, a, jnp.where(lane8 < 64, a32, jnp.where(lane8 < 96, roll(b, 64), b32)))
                    low = jnp.where(lane8 < 32, a32, jnp.where(lane8 < 64, roll(a, -64), jnp.where(lane8 < 96, b32, b)))
                    row = FINE[0] + 4 + 64 * rx + 8 * q
                    G[c, row : row + 8, :] = top
                    G[c, row + 32 : row + 40, :] = low
                    Z[c, rx, 8 * q : 8 * q + 8, :] = jnp.where(lane8 < 32, a, b32)
        return carry

    def spread(h, carry):
        row8 = lax.broadcasted_iota(jnp.int32, (8, 128), 0)
        half = row8 % 4 * 2
        halves = lane8 * 2 % 128
        for cc in range(4):
            c = 4 * h + cc
            for rx in range(2):
                keep = jnp.where(lane8 < 64, mine[2 * rx], mine[2 * rx + 1]) > 0
                fine = []
                for q in range(4):
                    z = jnp.take_along_axis(Z[c, rx, 8 * q : 8 * q + 8, :], lane8 // 2, axis=1)
                    for i in range(2):
                        row = FINE[0] + 4 + 64 * rx + 16 * q + 8 * i
                        x = jnp.take_along_axis(z, row8 // 2 + 4 * i, axis=0)
                        x = jnp.where(keep, G[c, row : row + 8, :], x)
                        G[c, row : row + 8, :] = x
                        G[c, row + 136 : row + 144, :] = x
                        x = x + pltpu.roll(x, 7, 0)
                        fine.append(jnp.take_along_axis(x, half, axis=0))
                for q in range(4):
                    x = jnp.where(row8 < 4, fine[2 * q], fine[2 * q + 1])
                    x = 0.25 * (jnp.take_along_axis(x, halves, axis=1) + jnp.take_along_axis(x, halves + 1, axis=1))
                    for base in COARSE:
                        row = base + 4 + 32 * rx + 8 * q
                        G[c, row : row + 8, :] = x
        return carry

    lax.fori_loop(0, 2, rotate, 0)
    lax.fori_loop(0, 2, spread, 0)

    def pack_columns():
        for h in range(2):
            for q in range(4):
                acc_r, acc_l = zero8, zero8
                for cc in range(4):
                    for k in range(6):
                        s = 32 * cc + 4 * k
                        row = (FINE[0] + 4 + 32 * k if k < 4 else COARSE[0] + 4 + 32 * (k - 4)) + 8 * q
                        x = roll(G[4 * h + cc, row : row + 8, :], s + 4)
                        acc_r = jnp.where((lane8 >= s) & (lane8 < s + 4), x, acc_r)
                        acc_l = jnp.where((lane8 >= s + 4) & (lane8 < s + 8), x, acc_l)
                SY[0, h, 8 * q : 8 * q + 8, :] = acc_r
                SY[1, h, 8 * q : 8 * q + 8, :] = acc_l

    pack_columns()

    def pack_rows():
        for d in range(2):
            corner = zero8
            fine, coarse = FINE[0] + 4 + (124, 0)[d], COARSE[0] + 4 + (60, 0)[d]
            for c in range(8):
                SR[d, c, 0:4, :] = G[c, fine : fine + 4, :]
                SR[d, c, 4:8, :] = G[c, coarse : coarse + 4, :]
                corner = jnp.where(lane8 // 8 == c, roll(SR[d, c], 8 * c + 4), corner)
            SK[d] = corner

    pack_rows()

    ghosts = [
        remote(SY.at[0], RY.at[0], at(0, 1)),
        remote(SY.at[1], RY.at[1], at(0, -1)),
        remote(SR.at[0], RB.at[0], at(1, 0)),
        remote(SR.at[1], RB.at[1], at(-1, 0)),
        remote(SK.at[0], RK.at[0], at(1, 1)),
        remote(SK.at[0], RK.at[1], at(1, -1)),
        remote(SK.at[1], RK.at[2], at(-1, 1)),
        remote(SK.at[1], RK.at[3], at(-1, -1)),
    ]
    round1 = [remote(VS.at[0], P1.at[s - 1], at(0, s)) for s in range(1, ngy)]
    pl.semaphore_wait(barrier, len(partners))
    for copy in ghosts[2:] + ghosts[:2] + round1:
        copy.start()

    load_v.wait()
    tile_of = lax.broadcasted_iota(jnp.int32, (2 * ngy, 2 * ngx), 1) // 2 * ngy
    tile_of = tile_of + lax.broadcasted_iota(jnp.int32, (2 * ngy, 2 * ngx), 0) // 2
    before = jnp.sum(jnp.where(tile_of < me, ref_v[...], 0))
    excess = 4 * me + 3 * before - CAP * me
    prev = flags_of(lax.rem(me + ngx * ngy - 1, ngx * ngy))
    following = flags_of(lax.rem(me + 1, ngx * ngy))

    def count_of(fl):
        return 4 + 3 * (fl[0] + fl[1] + fl[2] + fl[3])

    count = count_of(mine)

    def ge(a, b):
        return jnp.where(a >= b, 1, 0)

    def find(index, fl):
        index = jnp.clip(index, 0, count_of(fl) - 1)
        p1 = 1 + 3 * fl[0]
        p2 = p1 + 1 + 3 * fl[1]
        p3 = p2 + 1 + 3 * fl[2]
        a1, a2, a3 = ge(index, p1), ge(index, p2), ge(index, p3)
        child = index - (a1 * p1 + a2 * (p2 - p1) + a3 * (p3 - p2))
        flag = fl[0] + a1 * (fl[1] - fl[0]) + a2 * (fl[2] - fl[1]) + a3 * (fl[3] - fl[2])
        rx = a2
        ry = a1 + a2 + a3 - 2 * rx
        cx, cy = child & 1, child >> 1
        row = flag * (FINE[0] + 136 * ry + 64 * rx + 32 * cx) + (1 - flag) * (COARSE[0] + 72 * ry + 32 * rx)
        lane = flag * (64 * ry + 32 * cy) + (1 - flag) * 96 * ry - 4
        return row, lane, flag

    place = {w: find(w - excess, mine) for w in range(-3, 13)}
    wide = {}
    for w in range(CAP):
        flag = place[w][2]
        index = w - excess
        if w < 3:
            flag = jnp.where(index >= 0, flag, find(index + count_of(prev), prev)[2])
        if w >= 7:
            flag = jnp.where(index < count, flag, find(index - count, following)[2])
        wide[w] = 0.5 + 0.5 * flag.astype(F32)

    left8, right8 = lane8 >= 124, lane8 < 4
    left32, right32 = lane32 >= 124, lane32 < 4

    def fill_lanes():
        for h in range(2):
            low4 = lane32 % 8 < 4
            pair = (jnp.where(low4, RY[0, h], RY[1, h]), jnp.where(low4, RY[1, h], RY[0, h]))
            for cc in range(4):
                for k in range(6):
                    x = roll(pair[k % 2], -(32 * cc + 4 * k) - 4)
                    for i, mask in enumerate((left32, right32)):
                        row = FINE[i] + 4 + 32 * k if k < 4 else COARSE[i] + 4 + 32 * (k - 4)
                        pltpu.store(G.at[4 * h + cc, pl.ds(row, 32), :], x, mask=mask)

    for copy in ghosts[:2]:
        copy.wait_recv()
    fill_lanes()

    for copy in round1:
        copy.wait_recv()
    top = VS[0]
    for s in range(ngy - 1):
        top = jnp.maximum(top, P1[s])
    VS[1] = top
    round2 = [remote(VS.at[1], P2.at[s - 1], at(s, 0)) for s in range(1, ngx)]
    for copy in round2:
        copy.start()

    def fill_rows():
        for d in range(2):
            corner = jnp.where(lane8 % 8 < 4, RK[2 * d], RK[2 * d + 1])
            for c in range(8):
                piece = roll(corner, -8 * c - 4)
                row = RB[d, c]
                for i, mask in enumerate((left8, right8)):
                    x = jnp.where(mask, piece, row)
                    fine, coarse = FINE[i] + 132 * d, COARSE[i] + 68 * d
                    G[c, fine : fine + 4, :] = x[0:4]
                    G[c, coarse : coarse + 4, :] = x[4:8]

    for copy in ghosts[2:]:
        copy.wait_recv()
    fill_rows()

    def gather(dst, which, some=range(8)):
        for c in some:
            parts = [roll(G[c, pl.ds(place[w][0], EXT), :], EXT * g - place[w][1]) for g, w in enumerate(which)]
            x = parts[0]
            for g, part in enumerate(parts[1:]):
                x = jnp.where(lane40 < EXT * (g + 1), x, part)
            dst[c] = x

    carry_up = lax.div(gy + 1, ngy)
    carry_down = lax.div(ngy - gy, ngy)
    ahead = (lax.rem(gx + carry_up, ngx), lax.rem(gy + 1, ngy))
    behind = (lax.rem(gx + ngx - carry_down, ngx), lax.rem(gy + ngy - 1, ngy))
    moves = []
    for part in range(2):
        gather(MR, (10, 11, 12), range(4 * part, 4 * part + 4))
        gather(ML, (-3, -2, -1), range(4 * part, 4 * part + 4))
        some = pl.ds(4 * part, 4)
        moves.append(remote(MR.at[some], U.at[4, some], ahead))
        moves.append(remote(ML.at[some], U.at[5, some], behind))
        for copy in moves[-2:]:
            copy.start()

    gather(U.at[0], (3, 4, 5))
    gather(U.at[1], (6,))
    gather(U.at[2], (0, 1, 2))
    gather(U.at[3], (7, 8, 9))

    def first(t, carry, pick=lambda t: t):
        at_u = pick(t)
        for r in ROWS:
            u = [U[at_u, c, r : r + 8, :] for c in range(8)]
            flux_x, edge_x, flux_y, edge_y = cell_state(u)
            for i, v in enumerate(flux_x + edge_x):
                SX[i, r : r + 8, :] = v
            _, _, a, b, w = edge_weights(*edge_y, roll(edge_y[0], -1), roll(edge_y[1], -1))
            cell = (u[2],) + flux_y[:5] + (None,) + flux_y[5:]
            for c in range(8):
                jump = w * (roll(u[c], -1) - u[c])
                flux = jump if cell[c] is None else a * cell[c] + b * roll(cell[c], -1) + jump
                DY[t, c, r : r + 8, :] = flux - roll(flux, 1)
        for r in FACE1:
            edges = [SX[i, r + d : r + d + 8, :] for d in range(2) for i in (6, 7)]
            _, _, a, b, w = edge_weights(*edges)
            for c in range(8):
                low, high = U[at_u, c, r : r + 8, :], U[at_u, c, r + 1 : r + 9, :]
                flux = w * (high - low)
                if c == 0:
                    flux = a * U[at_u, 1, r : r + 8, :] + b * U[at_u, 1, r + 1 : r + 9, :] + flux
                elif c != 5:
                    i = c - 1 if c < 5 else c - 2
                    flux = a * SX[i, r : r + 8, :] + b * SX[i, r + 1 : r + 9, :] + flux
                GX[t, c, r : r + 8, :] = flux
        return carry

    lax.fori_loop(0, 2, first, 0)

    for copy in round2:
        copy.wait_recv()
    for s in range(ngx - 1):
        top = jnp.maximum(top, P2[s])
    top = jnp.max(top, axis=1, keepdims=True)
    time_step = COURANT / jnp.broadcast_to(top, (8, 128))

    def widths(ws):
        v = jnp.full((8, 128), wide[ws[0]], F32)
        for g, w in enumerate(ws[1:]):
            v = jnp.where(lane8 < EXT * (g + 1), v, wide[w])
        return v

    VM[0] = time_step * widths((3, 4, 5))
    VM[1] = time_step * widths((6,))
    VM[2] = time_step * widths((0, 1, 2))
    VM[3] = time_step * widths((7, 8, 9))

    def second(t, carry, pick=lambda t: t):
        rate = VM[t]
        at_u = pick(t)
        half = 0.5 * rate
        for r in MID:
            u = []
            for c in range(8):
                change = GX[t, c, r : r + 8, :] - GX[t, c, r - 1 : r + 7, :] + DY[t, c, r : r + 8, :]
                u.append(U[at_u, c, r : r + 8, :] - half * change)
            _, vx, vy, vz, pressure, _ = primitive(u)
            for c, v in enumerate((u[0], vx, vy, vz, pressure, u[5], u[6], u[7])):
                W[c, r : r + 8, :] = v
        for r in SLOPE:
            for c in range(8):
                w = [W[c, r + d : r + d + 8, :] for d in (-1, 0, 1, 2)]
                low, d, high = w[1] - w[0], w[2] - w[1], w[3] - w[2]
                rise = limited(0.5 * d + (low - high) * (1.0 / 12.0), d)
                RA[c, r : r + 8, :] = rise
                EA[c, r : r + 8, :] = d - rise
        for r in FACE2:
            left, right = [], []
            for c in range(8):
                rise, rise_next = RA[c, r : r + 8, :], RA[c, r + 1 : r + 9, :]
                fall, fall_next = EA[c, r - 1 : r + 7, :], EA[c, r : r + 8, :]
                left.append(W[c, r : r + 8, :] + limited(rise, 2.0 * fall))
                right.append(W[c, r + 1 : r + 9, :] - limited(fall_next, 2.0 * rise_next))
            for c, v in enumerate(face_flux(left, right, 1)):
                GX2[c, r : r + 8, :] = v
        for r in LAST:
            left, right = [], []
            for c in range(8):
                w = W[c, r : r + 8, :]
                ahead_w = roll(w, -1)
                d = ahead_w - w
                rise = limited(0.5 * d + (roll(d, 1) - roll(d, -1)) * (1.0 / 12.0), d)
                fall = d - rise
                left.append(w + limited(rise, 2.0 * roll(fall, 1)))
                right.append(ahead_w - limited(fall, 2.0 * roll(rise, -1)))
            for c, v in enumerate(face_flux(left, right, 2)):
                change = GX2[c, r : r + 8, :] - GX2[c, r - 1 : r + 7, :] + (v - roll(v, 1))
                O[t, c, r - 4 : r + 4, :] = U[at_u, c, r : r + 8, :] - rate * change
        return carry

    lax.fori_loop(0, 2, second, 0)

    def finish_local():
        for c in range(8):
            o0, o1 = O[0, c], O[1, c]
            out[c, :, 0:128] = roll(o0, 92)
            x = jnp.where(lane32 < 64, roll(o0, -52), roll(o1, 60))
            out[c, :, 128:256] = jnp.where(lane32 < 32, roll(o0, -44), x)

    finish_local()

    for copy in moves:
        copy.wait_recv()

    def pick(t):
        from_left = jnp.where(excess > 0, 4, 2)
        from_right = jnp.where(excess + count < CAP, 5, 3)
        return jnp.where(t == 2, from_left, jnp.where(t == 3, from_right, t))

    lax.fori_loop(2, 4, functools.partial(first, pick=pick), 0)
    lax.fori_loop(2, 4, functools.partial(second, pick=pick), 0)

    def finish():
        for c in range(8):
            o2, o3 = O[2, c], O[3, c]
            x = jnp.where(lane32 < 32, roll(o2, -4), jnp.where(lane32 < 64, roll(o2, -12), roll(o2, -20)))
            pltpu.store(out.at[c, :, pl.ds(0, 128)], x, mask=lane32 < 96)
            pltpu.store(out.at[c, :, pl.ds(128, 128)], roll(o3, 92), mask=lane32 >= 96)
            x = jnp.where(lane32 < 32, roll(o3, -44), roll(o3, -52))
            out[c, :, 256:320] = x[:, 0:64]

    finish()

    for copy in ghosts + moves + round1 + round2:
        copy.wait_send()


def shards(ngx, ngy, fields, refined):
    vmem = lambda *shape: pltpu.VMEM(shape, F32)
    scratch = [
        pltpu.SMEM((2 * ngy, 2 * ngx), jnp.int32),
        pltpu.VMEM((2 * ngy, 2 * ngx), jnp.int32),
        vmem(8, 32, 512),
        vmem(8, 2, BS, 128),
        vmem(8, PAD_ROWS, 128),
        vmem(6, 8, EXT, 128),
        vmem(8, EXT, 128),
        vmem(8, EXT, 128),
        vmem(2, 8, 8, 128),
        vmem(2, 8, 8, 128),
        vmem(2, 8, 128),
        vmem(4, 8, 128),
        vmem(2, 2, 32, 128),
        vmem(2, 2, 32, 128),
        vmem(4, 8, 128),
        vmem(2, 1, 128),
        vmem(ngy - 1, 1, 128),
        vmem(ngx - 1, 1, 128),
        vmem(8, EXT, 128),
        vmem(4, 8, EXT, 128),
        vmem(4, 8, EXT, 128),
        vmem(8, EXT, 128),
        vmem(8, EXT, 128),
        vmem(8, EXT, 128),
        vmem(8, EXT, 128),
        vmem(4, 8, BS, 128),
        pltpu.SemaphoreType.DMA((3,)),
        pltpu.SemaphoreType.DMA((ngx + ngy + 10,)),
        pltpu.SemaphoreType.DMA((ngx + ngy + 10,)),
    ]
    return pl.pallas_call(
        functools.partial(kernel, ngx, ngy),
        out_shape=jax.ShapeDtypeStruct((8, BS, CAP * BS), F32),
        in_specs=[
            pl.BlockSpec(memory_space=pltpu.HBM),
            pl.BlockSpec(memory_space=pltpu.HBM),
        ],
        out_specs=pl.BlockSpec(memory_space=pltpu.VMEM),
        scratch_shapes=scratch,
        compiler_params=pltpu.CompilerParams(
            collective_id=0, has_side_effects=True, vmem_limit_bytes=56_000_000
        ),
    )(refined.T, fields)


def solution(mesh):
    ngx, ngy = mesh.shape["gx"], mesh.shape["gy"]
    return jax.shard_map(
        functools.partial(shards, ngx, ngy),
        mesh=mesh,
        in_specs=(P(None, None, ("gx", "gy")), P()),
        out_specs=P(None, None, ("gx", "gy")),
        check_vma=False,
    )
```

```python
import functools

import jax
import jax.numpy as jnp
from jax import lax
from jax.experimental import pallas as pl
from jax.experimental.pallas import tpu as pltpu
from jax.sharding import PartitionSpec as P

BS = 32
CAP = 10
EXT = BS + 8
GAMMA = 5.0 / 3.0
COURANT = 0.2
MESH = pl.DeviceIdType.MESH
F32 = jnp.float32

FINE = (4, 140)
COARSE = (276, 348)
PAD_ROWS = 424
ROWS = (0, 8, 16, 24, 32)
FACE1 = (0, 8, 16, 24, 31)
MID = (1, 9, 17, 25, 31)
SLOPE = (2, 10, 18, 26, 29)
FACE2 = (3, 11, 19, 27, 28)
LAST = (4, 12, 20, 28)


def lanes(rows):
    return lax.broadcasted_iota(jnp.int32, (rows, 128), 1)


def roll(x, by):
    if isinstance(by, int):
        by = by % 128
        return x if by == 0 else pltpu.roll(x, by, 1)
    return pltpu.roll(x, lax.rem(by + 256, 128), 1)


def recip(x):
    return pltpu.reciprocal(x, approx=True)


def root(x):
    return x * lax.rsqrt(jnp.maximum(x, 1e-30))


def farthest(count, minor):
    major = max(count // minor, 1)

    def hops(step):
        outer, inner = step // minor, step % minor
        return min(outer, major - outer) + min(inner, minor - inner)

    return sorted(range(1, count), key=lambda step: -hops(step))


def limited(value, other):
    return jnp.minimum(jnp.maximum(value, jnp.minimum(other, 0.0)), jnp.maximum(other, 0.0))


def primitive(u):
    rho, mx, my, mz, energy, bx, by, bz = u
    inv = recip(rho)
    vx, vy, vz = mx * inv, my * inv, mz * inv
    half_b2 = 0.5 * (bx * bx + by * by + bz * bz)
    kinetic = 0.5 * (mx * vx + my * vy + mz * vz)
    pressure = (GAMMA - 1.0) * (energy - kinetic - half_b2)
    return inv, vx, vy, vz, pressure, half_b2


def fast_pair(inv, pressure, half_b2, trans_x, trans_y):
    sound = GAMMA * pressure * inv
    alfven = 2.0 * half_b2 * inv
    total = sound + alfven
    diff = sound - alfven
    square = diff * diff
    four = 4.0 * sound * inv
    fast_x = root(0.5 * (total + root(square + four * trans_x)))
    fast_y = root(0.5 * (total + root(square + four * trans_y)))
    return fast_x, fast_y


def cell_state(u):
    rho, mx, my, mz, energy, bx, by, bz = u
    inv, vx, vy, vz, pressure, half_b2 = primitive(u)
    xx, yy, zz = bx * bx, by * by, bz * bz
    fast_x, fast_y = fast_pair(inv, pressure, half_b2, yy + zz, xx + zz)
    total_p = pressure + half_b2
    enthalpy = energy + total_p
    vb = vx * bx + vy * by + vz * bz
    cross = mx * vy - bx * by
    emf = by * vx - bx * vy
    flux_x = (mx * vx + total_p - xx, cross, mx * vz - bx * bz, enthalpy * vx - bx * vb, emf, bz * vx - bx * vz)
    flux_y = (cross, my * vy + total_p - yy, my * vz - by * bz, enthalpy * vy - by * vb, -emf, bz * vy - by * vz)
    return flux_x, (vx - fast_x, vx + fast_x), flux_y, (vy - fast_y, vy + fast_y)


def edge_weights(slow_l, fast_l, slow_r, fast_r):
    slow = jnp.minimum(jnp.minimum(slow_l, slow_r), 0.0)
    fast = jnp.maximum(jnp.maximum(fast_l, fast_r), 0.0)
    inv = recip(fast - slow)
    a = fast * inv
    b = -slow * inv
    return slow, fast, a, b, slow * a


def side(w, normal):
    rho, vx, vy, vz, pressure, bx, by, bz = w
    vn, vt, bn, bt = (vx, vy, bx, by) if normal == 1 else (vy, vx, by, bx)
    inv = recip(rho)
    trans = bt * bt + bz * bz
    nn = bn * bn
    b2 = trans + nn
    sound = GAMMA * pressure * inv
    alfven = b2 * inv
    diff = sound - alfven
    fast = root(0.5 * (sound + alfven + root(diff * diff + 4.0 * sound * inv * trans)))
    half_b2 = 0.5 * b2
    total_p = pressure + half_b2
    energy = 1.5 * pressure + half_b2 + 0.5 * rho * (vn * vn + vt * vt + vz * vz)
    vb = vn * bn + vt * bt + vz * bz
    return vn - fast, vn + fast, (rho, vn, vt, vz, bn, bt, bz, energy, total_p, total_p - nn, vb)


def moved(state, speed):
    rho, vn, vt, vz, bn, bt, bz, energy, total_p, stress, vb = state
    rel = vn - speed
    mass = rho * rel
    return (
        mass,
        mass * vn + stress,
        mass * vt - bn * bt,
        mass * vz - bn * bz,
        energy * rel + total_p * vn - bn * vb,
        bt * rel - bn * vt,
        bz * rel - bn * vz,
    )


def face_flux(left, right, normal):
    slow_l, fast_l, state_l = side(left, normal)
    slow_r, fast_r, state_r = side(right, normal)
    slow, fast, a, b, c = edge_weights(slow_l, fast_l, slow_r, fast_r)
    from_l = moved(state_l, slow)
    from_r = moved(state_r, fast)
    mass, mn, mt, mz, en, bt, bz = (a * p + b * q for p, q in zip(from_l, from_r))
    bn = c * (state_r[4] - state_l[4])
    if normal == 1:
        return (mass, mn, mt, mz, en, bn, bt, bz)
    return (mass, mt, mn, mz, en, bt, bn, bz)


def kernel(ngx, ngy, refined, fields, out, *scratch):
    (ref_s, ref_v, X, Z, G, U, ML, MR, SR, RB, SK, RK, SY, RY, VM, VS, P1, P2, SX, GX, DY, W, RA, EA, GX2, O, in_sem, send, recv) = scratch
    gx = lax.axis_index("gx")
    gy = lax.axis_index("gy")
    me = gx * ngy + gy
    load = pltpu.make_async_copy(fields, X, in_sem.at[0])
    load.start()
    load_s = pltpu.make_async_copy(refined, ref_s, in_sem.at[1])
    load_s.start()
    load_v = pltpu.make_async_copy(refined, ref_v, in_sem.at[2])
    load_v.start()

    def at(dx, dy):
        return lax.rem(gx + dx + ngx, ngx), lax.rem(gy + dy + ngy, ngy)

    partners = [at(0, s) for s in range(1, ngy)] + [at(s, 0) for s in range(1, ngx)]
    partners += [at(1, 1), at(1, -1), at(-1, 1), at(-1, -1)]
    barrier = pltpu.get_barrier_semaphore()
    for who in partners:
        pl.semaphore_signal(barrier, inc=1, device_id=who, device_id_type=MESH)

    sems = iter(range(64))

    def remote(src, dst, who):
        i = next(sems)
        return pltpu.make_async_remote_copy(
            src_ref=src, dst_ref=dst, send_sem=send.at[i], recv_sem=recv.at[i], device_id=who, device_id_type=MESH
        )

    def flags_of(tile):
        tx, ty = lax.div(tile, ngy), lax.rem(tile, ngy)
        return [ref_s[2 * ty + r % 2, 2 * tx + r // 2] for r in range(4)]

    load_s.wait()
    mine = flags_of(me)
    lane8, lane32, lane40 = lanes(8), lanes(32), lanes(EXT)
    load.wait()

    zero8 = jnp.zeros((8, 128), F32)
    peak = zero8
    for r in range(4):
        on = mine[r] > 0
        weight = jnp.where(lane8 < 32, jnp.where(on, 1.0, 0.5), jnp.where(on, 1.0, 0.0)).astype(F32)
        for q in range(4):
            u = [X[c, 8 * q : 8 * q + 8, 128 * r : 128 * r + 128] for c in range(8)]
            inv, vx, vy, vz, pressure, half_b2 = primitive(u)
            xx, yy, zz = (b * b for b in u[5:])
            fast_x, fast_y = fast_pair(inv, pressure, half_b2, yy + zz, xx + zz)
            rate = jnp.maximum(jnp.abs(vx) + fast_x, jnp.abs(vy) + fast_y)
            peak = jnp.maximum(peak, jnp.where(weight > 0.0, rate * weight, 0.0))
    VS[0] = jnp.max(peak, axis=0, keepdims=True)

    def rotate(h, carry):
        for cc in range(4):
            c = 4 * h + cc
            for rx in range(2):
                for q in range(4):
                    a = X[c, 8 * q : 8 * q + 8, 256 * rx : 256 * rx + 128]
                    b = X[c, 8 * q : 8 * q + 8, 256 * rx + 128 : 256 * rx + 256]
                    a32, b32 = roll(a, -32), roll(b, 32)
                    top = jnp.where(lane8 < 32, a, jnp.where(lane8 < 64, a32, jnp.where(lane8 < 96, roll(b, 64), b32)))
                    low = jnp.where(lane8 < 32, a32, jnp.where(lane8 < 64, roll(a, -64), jnp.where(lane8 < 96, b32, b)))
                    row = FINE[0] + 4 + 64 * rx + 8 * q
                    G[c, row : row + 8, :] = top
                    G[c, row + 32 : row + 40, :] = low
                    Z[c, rx, 8 * q : 8 * q + 8, :] = jnp.where(lane8 < 32, a, b32)
        return carry

    def spread(h, carry):
        row8 = lax.broadcasted_iota(jnp.int32, (8, 128), 0)
        half = row8 % 4 * 2
        halves = lane8 * 2 % 128
        for cc in range(4):
            c = 4 * h + cc
            for rx in range(2):
                keep = jnp.where(lane8 < 64, mine[2 * rx], mine[2 * rx + 1]) > 0
                fine = []
                for q in range(4):
                    z = jnp.take_along_axis(Z[c, rx, 8 * q : 8 * q + 8, :], lane8 // 2, axis=1)
                    for i in range(2):
                        row = FINE[0] + 4 + 64 * rx + 16 * q + 8 * i
                        x = jnp.take_along_axis(z, row8 // 2 + 4 * i, axis=0)
                        x = jnp.where(keep, G[c, row : row + 8, :], x)
                        G[c, row : row + 8, :] = x
                        G[c, row + 136 : row + 144, :] = x
                        x = x + pltpu.roll(x, 7, 0)
                        fine.append(jnp.take_along_axis(x, half, axis=0))
                for q in range(4):
                    x = jnp.where(row8 < 4, fine[2 * q], fine[2 * q + 1])
                    x = 0.25 * (jnp.take_along_axis(x, halves, axis=1) + jnp.take_along_axis(x, halves + 1, axis=1))
                    for base in COARSE:
                        row = base + 4 + 32 * rx + 8 * q
                        G[c, row : row + 8, :] = x
        return carry

    lax.fori_loop(0, 2, rotate, 0)
    lax.fori_loop(0, 2, spread, 0)

    def pack_columns():
        for h in range(2):
            for q in range(4):
                acc_r, acc_l = zero8, zero8
                for cc in range(4):
                    for k in range(6):
                        s = 32 * cc + 4 * k
                        row = (FINE[0] + 4 + 32 * k if k < 4 else COARSE[0] + 4 + 32 * (k - 4)) + 8 * q
                        x = roll(G[4 * h + cc, row : row + 8, :], s + 4)
                        acc_r = jnp.where((lane8 >= s) & (lane8 < s + 4), x, acc_r)
                        acc_l = jnp.where((lane8 >= s + 4) & (lane8 < s + 8), x, acc_l)
                SY[0, h, 8 * q : 8 * q + 8, :] = acc_r
                SY[1, h, 8 * q : 8 * q + 8, :] = acc_l

    pack_columns()

    def pack_rows():
        for d in range(2):
            corner = zero8
            fine, coarse = FINE[0] + 4 + (124, 0)[d], COARSE[0] + 4 + (60, 0)[d]
            for c in range(8):
                SR[d, c, 0:4, :] = G[c, fine : fine + 4, :]
                SR[d, c, 4:8, :] = G[c, coarse : coarse + 4, :]
                corner = jnp.where(lane8 // 8 == c, roll(SR[d, c], 8 * c + 4), corner)
            SK[d] = corner

    pack_rows()

    ghosts = [
        remote(SY.at[0], RY.at[0], at(0, 1)),
        remote(SY.at[1], RY.at[1], at(0, -1)),
        remote(SR.at[0], RB.at[0], at(1, 0)),
        remote(SR.at[1], RB.at[1], at(-1, 0)),
        remote(SK.at[0], RK.at[0], at(1, 1)),
        remote(SK.at[0], RK.at[1], at(1, -1)),
        remote(SK.at[1], RK.at[2], at(-1, 1)),
        remote(SK.at[1], RK.at[3], at(-1, -1)),
    ]
    round1 = [remote(VS.at[0], P1.at[s - 1], at(0, s)) for s in farthest(ngy, 2)]
    pl.semaphore_wait(barrier, len(partners))
    for copy in ghosts[2:] + ghosts[:2] + round1:
        copy.start()

    load_v.wait()
    tile_of = lax.broadcasted_iota(jnp.int32, (2 * ngy, 2 * ngx), 1) // 2 * ngy
    tile_of = tile_of + lax.broadcasted_iota(jnp.int32, (2 * ngy, 2 * ngx), 0) // 2
    before = jnp.sum(jnp.where(tile_of < me, ref_v[...], 0))
    excess = 4 * me + 3 * before - CAP * me
    prev = flags_of(lax.rem(me + ngx * ngy - 1, ngx * ngy))
    following = flags_of(lax.rem(me + 1, ngx * ngy))

    def count_of(fl):
        return 4 + 3 * (fl[0] + fl[1] + fl[2] + fl[3])

    count = count_of(mine)

    def ge(a, b):
        return jnp.where(a >= b, 1, 0)

    def find(index, fl):
        index = jnp.clip(index, 0, count_of(fl) - 1)
        p1 = 1 + 3 * fl[0]
        p2 = p1 + 1 + 3 * fl[1]
        p3 = p2 + 1 + 3 * fl[2]
        a1, a2, a3 = ge(index, p1), ge(index, p2), ge(index, p3)
        child = index - (a1 * p1 + a2 * (p2 - p1) + a3 * (p3 - p2))
        flag = fl[0] + a1 * (fl[1] - fl[0]) + a2 * (fl[2] - fl[1]) + a3 * (fl[3] - fl[2])
        rx = a2
        ry = a1 + a2 + a3 - 2 * rx
        cx, cy = child & 1, child >> 1
        row = flag * (FINE[0] + 136 * ry + 64 * rx + 32 * cx) + (1 - flag) * (COARSE[0] + 72 * ry + 32 * rx)
        lane = flag * (64 * ry + 32 * cy) + (1 - flag) * 96 * ry - 4
        return row, lane, flag

    place = {w: find(w - excess, mine) for w in range(-3, 13)}
    wide = {}
    for w in range(CAP):
        flag = place[w][2]
        index = w - excess
        if w < 3:
            flag = jnp.where(index >= 0, flag, find(index + count_of(prev), prev)[2])
        if w >= 7:
            flag = jnp.where(index < count, flag, find(index - count, following)[2])
        wide[w] = 0.5 + 0.5 * flag.astype(F32)

    left8, right8 = lane8 >= 124, lane8 < 4
    left32, right32 = lane32 >= 124, lane32 < 4

    def fill_lanes():
        for h in range(2):
            low4 = lane32 % 8 < 4
            pair = (jnp.where(low4, RY[0, h], RY[1, h]), jnp.where(low4, RY[1, h], RY[0, h]))
            for cc in range(4):
                for k in range(6):
                    x = roll(pair[k % 2], -(32 * cc + 4 * k) - 4)
                    for i, mask in enumerate((left32, right32)):
                        row = FINE[i] + 4 + 32 * k if k < 4 else COARSE[i] + 4 + 32 * (k - 4)
                        pltpu.store(G.at[4 * h + cc, pl.ds(row, 32), :], x, mask=mask)

    for copy in ghosts[:2]:
        copy.wait_recv()
    fill_lanes()

    for copy in round1:
        copy.wait_recv()
    top = VS[0]
    for s in range(ngy - 1):
        top = jnp.maximum(top, P1[s])
    VS[1] = top
    round2 = [remote(VS.at[1], P2.at[s - 1], at(s, 0)) for s in farthest(ngx, 4)]
    for copy in round2:
        copy.start()

    def fill_rows():
        for d in range(2):
            corner = jnp.where(lane8 % 8 < 4, RK[2 * d], RK[2 * d + 1])
            for c in range(8):
                piece = roll(corner, -8 * c - 4)
                row = RB[d, c]
                for i, mask in enumerate((left8, right8)):
                    x = jnp.where(mask, piece, row)
                    fine, coarse = FINE[i] + 132 * d, COARSE[i] + 68 * d
                    G[c, fine : fine + 4, :] = x[0:4]
                    G[c, coarse : coarse + 4, :] = x[4:8]

    for copy in ghosts[2:]:
        copy.wait_recv()
    fill_rows()

    def gather(dst, which, some=range(8)):
        for c in some:
            parts = [roll(G[c, pl.ds(place[w][0], EXT), :], EXT * g - place[w][1]) for g, w in enumerate(which)]
            x = parts[0]
            for g, part in enumerate(parts[1:]):
                x = jnp.where(lane40 < EXT * (g + 1), x, part)
            dst[c] = x

    carry_up = lax.div(gy + 1, ngy)
    carry_down = lax.div(ngy - gy, ngy)
    ahead = (lax.rem(gx + carry_up, ngx), lax.rem(gy + 1, ngy))
    behind = (lax.rem(gx + ngx - carry_down, ngx), lax.rem(gy + ngy - 1, ngy))
    moves = []
    for part in range(2):
        gather(MR, (10, 11, 12), range(4 * part, 4 * part + 4))
        gather(ML, (-3, -2, -1), range(4 * part, 4 * part + 4))
        some = pl.ds(4 * part, 4)
        moves.append(remote(MR.at[some], U.at[4, some], ahead))
        moves.append(remote(ML.at[some], U.at[5, some], behind))
        for copy in moves[-2:]:
            copy.start()

    gather(U.at[0], (3, 4, 5))
    gather(U.at[1], (6,))
    gather(U.at[2], (0, 1, 2))
    gather(U.at[3], (7, 8, 9))

    def first(t, carry, pick=lambda t: t):
        at_u = pick(t)
        for r in ROWS:
            u = [U[at_u, c, r : r + 8, :] for c in range(8)]
            flux_x, edge_x, flux_y, edge_y = cell_state(u)
            for i, v in enumerate(flux_x + edge_x):
                SX[i, r : r + 8, :] = v
            _, _, a, b, w = edge_weights(*edge_y, roll(edge_y[0], -1), roll(edge_y[1], -1))
            cell = (u[2],) + flux_y[:5] + (None,) + flux_y[5:]
            for c in range(8):
                jump = w * (roll(u[c], -1) - u[c])
                flux = jump if cell[c] is None else a * cell[c] + b * roll(cell[c], -1) + jump
                DY[t, c, r : r + 8, :] = flux - roll(flux, 1)
        for r in FACE1:
            edges = [SX[i, r + d : r + d + 8, :] for d in range(2) for i in (6, 7)]
            _, _, a, b, w = edge_weights(*edges)
            for c in range(8):
                low, high = U[at_u, c, r : r + 8, :], U[at_u, c, r + 1 : r + 9, :]
                flux = w * (high - low)
                if c == 0:
                    flux = a * U[at_u, 1, r : r + 8, :] + b * U[at_u, 1, r + 1 : r + 9, :] + flux
                elif c != 5:
                    i = c - 1 if c < 5 else c - 2
                    flux = a * SX[i, r : r + 8, :] + b * SX[i, r + 1 : r + 9, :] + flux
                GX[t, c, r : r + 8, :] = flux
        return carry

    lax.fori_loop(0, 2, first, 0)

    def widths(ws):
        v = jnp.full((8, 128), wide[ws[0]], F32)
        for g, w in enumerate(ws[1:]):
            v = jnp.where(lane8 < EXT * (g + 1), v, wide[w])
        return v

    VM[0] = widths((3, 4, 5))
    VM[1] = widths((6,))
    VM[2] = widths((0, 1, 2))
    VM[3] = widths((7, 8, 9))

    for copy in ghosts + round1 + moves + round2:
        copy.wait_send()
    for copy in round2:
        copy.wait_recv()
    for s in range(ngx - 1):
        top = jnp.maximum(top, P2[s])
    top = jnp.max(top, axis=1, keepdims=True)
    time_step = COURANT / jnp.broadcast_to(top, (8, 128))

    def second(t, carry, pick=lambda t: t):
        rate = time_step * VM[t]
        at_u = pick(t)
        half = 0.5 * rate
        for r in MID:
            u = []
            for c in range(8):
                change = GX[t, c, r : r + 8, :] - GX[t, c, r - 1 : r + 7, :] + DY[t, c, r : r + 8, :]
                u.append(U[at_u, c, r : r + 8, :] - half * change)
            _, vx, vy, vz, pressure, _ = primitive(u)
            for c, v in enumerate((u[0], vx, vy, vz, pressure, u[5], u[6], u[7])):
                W[c, r : r + 8, :] = v
        for r in SLOPE:
            for c in range(8):
                w = [W[c, r + d : r + d + 8, :] for d in (-1, 0, 1, 2)]
                low, d, high = w[1] - w[0], w[2] - w[1], w[3] - w[2]
                rise = limited(0.5 * d + (low - high) * (1.0 / 12.0), d)
                RA[c, r : r + 8, :] = rise
                EA[c, r : r + 8, :] = d - rise
        for r in FACE2:
            left, right = [], []
            for c in range(8):
                rise, rise_next = RA[c, r : r + 8, :], RA[c, r + 1 : r + 9, :]
                fall, fall_next = EA[c, r - 1 : r + 7, :], EA[c, r : r + 8, :]
                left.append(W[c, r : r + 8, :] + limited(rise, 2.0 * fall))
                right.append(W[c, r + 1 : r + 9, :] - limited(fall_next, 2.0 * rise_next))
            for c, v in enumerate(face_flux(left, right, 1)):
                GX2[c, r : r + 8, :] = v
        for r in LAST:
            left, right = [], []
            for c in range(8):
                w = W[c, r : r + 8, :]
                ahead_w = roll(w, -1)
                d = ahead_w - w
                rise = limited(0.5 * d + (roll(d, 1) - roll(d, -1)) * (1.0 / 12.0), d)
                fall = d - rise
                left.append(w + limited(rise, 2.0 * roll(fall, 1)))
                right.append(ahead_w - limited(fall, 2.0 * roll(rise, -1)))
            for c, v in enumerate(face_flux(left, right, 2)):
                change = GX2[c, r : r + 8, :] - GX2[c, r - 1 : r + 7, :] + (v - roll(v, 1))
                O[t, c, r - 4 : r + 4, :] = U[at_u, c, r : r + 8, :] - rate * change
        return carry

    lax.fori_loop(0, 2, second, 0)

    def finish_local():
        for c in range(8):
            o0, o1 = O[0, c], O[1, c]
            out[c, :, 0:128] = roll(o0, 92)
            x = jnp.where(lane32 < 64, roll(o0, -52), roll(o1, 60))
            out[c, :, 128:256] = jnp.where(lane32 < 32, roll(o0, -44), x)

    finish_local()

    for copy in moves:
        copy.wait_recv()

    def pick(t):
        from_left = jnp.where(excess > 0, 4, 2)
        from_right = jnp.where(excess + count < CAP, 5, 3)
        return jnp.where(t == 2, from_left, jnp.where(t == 3, from_right, t))

    lax.fori_loop(2, 4, functools.partial(first, pick=pick), 0)
    lax.fori_loop(2, 4, functools.partial(second, pick=pick), 0)

    def finish():
        for c in range(8):
            o2, o3 = O[2, c], O[3, c]
            x = jnp.where(lane32 < 32, roll(o2, -4), jnp.where(lane32 < 64, roll(o2, -12), roll(o2, -20)))
            pltpu.store(out.at[c, :, pl.ds(0, 128)], x, mask=lane32 < 96)
            pltpu.store(out.at[c, :, pl.ds(128, 128)], roll(o3, 92), mask=lane32 >= 96)
            x = jnp.where(lane32 < 32, roll(o3, -44), roll(o3, -52))
            out[c, :, 256:320] = x[:, 0:64]

    finish()


def shards(ngx, ngy, fields, refined):
    vmem = lambda *shape: pltpu.VMEM(shape, F32)
    scratch = [
        pltpu.SMEM((2 * ngy, 2 * ngx), jnp.int32),
        pltpu.VMEM((2 * ngy, 2 * ngx), jnp.int32),
        vmem(8, 32, 512),
        vmem(8, 2, BS, 128),
        vmem(8, PAD_ROWS, 128),
        vmem(6, 8, EXT, 128),
        vmem(8, EXT, 128),
        vmem(8, EXT, 128),
        vmem(2, 8, 8, 128),
        vmem(2, 8, 8, 128),
        vmem(2, 8, 128),
        vmem(4, 8, 128),
        vmem(2, 2, 32, 128),
        vmem(2, 2, 32, 128),
        vmem(4, 8, 128),
        vmem(2, 1, 128),
        vmem(ngy - 1, 1, 128),
        vmem(ngx - 1, 1, 128),
        vmem(8, EXT, 128),
        vmem(4, 8, EXT, 128),
        vmem(4, 8, EXT, 128),
        vmem(8, EXT, 128),
        vmem(8, EXT, 128),
        vmem(8, EXT, 128),
        vmem(8, EXT, 128),
        vmem(4, 8, BS, 128),
        pltpu.SemaphoreType.DMA((3,)),
        pltpu.SemaphoreType.DMA((ngx + ngy + 10,)),
        pltpu.SemaphoreType.DMA((ngx + ngy + 10,)),
    ]
    return pl.pallas_call(
        functools.partial(kernel, ngx, ngy),
        out_shape=jax.ShapeDtypeStruct((8, BS, CAP * BS), F32),
        in_specs=[
            pl.BlockSpec(memory_space=pltpu.HBM),
            pl.BlockSpec(memory_space=pltpu.HBM),
        ],
        out_specs=pl.BlockSpec(memory_space=pltpu.VMEM),
        scratch_shapes=scratch,
        compiler_params=pltpu.CompilerParams(
            collective_id=0, has_side_effects=True, vmem_limit_bytes=56_000_000
        ),
    )(refined.T, fields)


def solution(mesh):
    ngx, ngy = mesh.shape["gx"], mesh.shape["gy"]
    return jax.shard_map(
        functools.partial(shards, ngx, ngy),
        mesh=mesh,
        in_specs=(P(None, None, ("gx", "gy")), P()),
        out_specs=P(None, None, ("gx", "gy")),
        check_vma=False,
    )
```

```python
import functools

import jax
import jax.numpy as jnp
from jax import lax
from jax.experimental import pallas as pl
from jax.experimental.pallas import tpu as pltpu
from jax.sharding import PartitionSpec as P

BS = 32
CAP = 10
EXT = BS + 8
GAMMA = 5.0 / 3.0
COURANT = 0.2
MESH = pl.DeviceIdType.MESH
F32 = jnp.float32

FINE = (4, 140)
COARSE = (276, 348)
PAD_ROWS = 424
ROWS = (0, 8, 16, 24, 32)
FACE1 = (0, 8, 16, 24, 31)
MID = (1, 9, 17, 25, 31)
SLOPE = (2, 10, 18, 26, 29)
FACE2 = (3, 11, 19, 27, 28)
LAST = (4, 12, 20, 28)


def lanes(rows):
    return lax.broadcasted_iota(jnp.int32, (rows, 128), 1)


def roll(x, by):
    if isinstance(by, int):
        by = by % 128
        return x if by == 0 else pltpu.roll(x, by, 1)
    return pltpu.roll(x, lax.rem(by + 256, 128), 1)


def recip(x):
    return pltpu.reciprocal(x, approx=True)


def root(x):
    return x * lax.rsqrt(jnp.maximum(x, 1e-30))


def farthest(count, minor):
    major = max(count // minor, 1)

    def hops(step):
        outer, inner = step // minor, step % minor
        return min(outer, major - outer) + min(inner, minor - inner)

    return sorted(range(1, count), key=lambda step: -hops(step))


def limited(value, other):
    return jnp.minimum(jnp.maximum(value, jnp.minimum(other, 0.0)), jnp.maximum(other, 0.0))


def primitive(u):
    rho, mx, my, mz, energy, bx, by, bz = u
    inv = recip(rho)
    vx, vy, vz = mx * inv, my * inv, mz * inv
    half_b2 = 0.5 * (bx * bx + by * by + bz * bz)
    kinetic = 0.5 * (mx * vx + my * vy + mz * vz)
    pressure = (GAMMA - 1.0) * (energy - kinetic - half_b2)
    return inv, vx, vy, vz, pressure, half_b2


def fast_pair(inv, pressure, half_b2, trans_x, trans_y):
    sound = GAMMA * pressure * inv
    alfven = 2.0 * half_b2 * inv
    total = sound + alfven
    diff = sound - alfven
    square = diff * diff
    four = 4.0 * sound * inv
    fast_x = root(0.5 * (total + root(square + four * trans_x)))
    fast_y = root(0.5 * (total + root(square + four * trans_y)))
    return fast_x, fast_y


def cell_state(u):
    rho, mx, my, mz, energy, bx, by, bz = u
    inv, vx, vy, vz, pressure, half_b2 = primitive(u)
    xx, yy, zz = bx * bx, by * by, bz * bz
    fast_x, fast_y = fast_pair(inv, pressure, half_b2, yy + zz, xx + zz)
    total_p = pressure + half_b2
    enthalpy = energy + total_p
    vb = vx * bx + vy * by + vz * bz
    cross = mx * vy - bx * by
    emf = by * vx - bx * vy
    flux_x = (mx * vx + total_p - xx, cross, mx * vz - bx * bz, enthalpy * vx - bx * vb, emf, bz * vx - bx * vz)
    flux_y = (cross, my * vy + total_p - yy, my * vz - by * bz, enthalpy * vy - by * vb, -emf, bz * vy - by * vz)
    return flux_x, (vx - fast_x, vx + fast_x), flux_y, (vy - fast_y, vy + fast_y)


def edge_weights(slow_l, fast_l, slow_r, fast_r):
    slow = jnp.minimum(jnp.minimum(slow_l, slow_r), 0.0)
    fast = jnp.maximum(jnp.maximum(fast_l, fast_r), 0.0)
    inv = recip(fast - slow)
    a = fast * inv
    b = -slow * inv
    return slow, fast, a, b, slow * a


def side(w, normal):
    rho, vx, vy, vz, pressure, bx, by, bz = w
    vn, vt, bn, bt = (vx, vy, bx, by) if normal == 1 else (vy, vx, by, bx)
    inv = recip(rho)
    trans = bt * bt + bz * bz
    nn = bn * bn
    b2 = trans + nn
    sound = GAMMA * pressure * inv
    alfven = b2 * inv
    diff = sound - alfven
    fast = root(0.5 * (sound + alfven + root(diff * diff + 4.0 * sound * inv * trans)))
    half_b2 = 0.5 * b2
    total_p = pressure + half_b2
    energy = 1.5 * pressure + half_b2 + 0.5 * rho * (vn * vn + vt * vt + vz * vz)
    vb = vn * bn + vt * bt + vz * bz
    return vn - fast, vn + fast, (rho, vn, vt, vz, bn, bt, bz, energy, total_p, total_p - nn, vb)


def moved(state, speed):
    rho, vn, vt, vz, bn, bt, bz, energy, total_p, stress, vb = state
    rel = vn - speed
    mass = rho * rel
    return (
        mass,
        mass * vn + stress,
        mass * vt - bn * bt,
        mass * vz - bn * bz,
        energy * rel + total_p * vn - bn * vb,
        bt * rel - bn * vt,
        bz * rel - bn * vz,
    )


def face_flux(left, right, normal):
    slow_l, fast_l, state_l = side(left, normal)
    slow_r, fast_r, state_r = side(right, normal)
    slow, fast, a, b, c = edge_weights(slow_l, fast_l, slow_r, fast_r)
    from_l = moved(state_l, slow)
    from_r = moved(state_r, fast)
    mass, mn, mt, mz, en, bt, bz = (a * p + b * q for p, q in zip(from_l, from_r))
    bn = c * (state_r[4] - state_l[4])
    if normal == 1:
        return (mass, mn, mt, mz, en, bn, bt, bz)
    return (mass, mt, mn, mz, en, bt, bn, bz)


def kernel(ngx, ngy, refined, fields, out, *scratch):
    (ref_s, ref_v, X, Z, G, U, ML, MR, SR, RB, SK, RK, SY, RY, VM, VS, P1, P2, SX, GX, DY, W, RA, EA, GX2, O, in_sem, send, recv) = scratch
    gx = lax.axis_index("gx")
    gy = lax.axis_index("gy")
    me = gx * ngy + gy
    load = pltpu.make_async_copy(fields, X, in_sem.at[0])
    load.start()
    load_s = pltpu.make_async_copy(refined, ref_s, in_sem.at[1])
    load_s.start()
    load_v = pltpu.make_async_copy(refined, ref_v, in_sem.at[2])
    load_v.start()

    def at(dx, dy):
        return lax.rem(gx + dx + ngx, ngx), lax.rem(gy + dy + ngy, ngy)

    partners = [at(0, s) for s in range(1, ngy)] + [at(s, 0) for s in range(1, ngx)]
    partners += [at(1, 1), at(1, -1), at(-1, 1), at(-1, -1)]
    barrier = pltpu.get_barrier_semaphore()
    for who in partners:
        pl.semaphore_signal(barrier, inc=1, device_id=who, device_id_type=MESH)

    sems = iter(range(64))

    def remote(src, dst, who):
        i = next(sems)
        return pltpu.make_async_remote_copy(
            src_ref=src, dst_ref=dst, send_sem=send.at[i], recv_sem=recv.at[i], device_id=who, device_id_type=MESH
        )

    def flags_of(tile):
        tx, ty = lax.div(tile, ngy), lax.rem(tile, ngy)
        return [ref_s[2 * ty + r % 2, 2 * tx + r // 2] for r in range(4)]

    load_s.wait()
    mine = flags_of(me)
    lane8, lane32, lane40 = lanes(8), lanes(32), lanes(EXT)
    load.wait()

    zero8 = jnp.zeros((8, 128), F32)
    peak = zero8
    for r in range(4):
        on = mine[r] > 0
        weight = jnp.where(lane8 < 32, jnp.where(on, 1.0, 0.5), jnp.where(on, 1.0, 0.0)).astype(F32)
        for q in range(4):
            u = [X[c, 8 * q : 8 * q + 8, 128 * r : 128 * r + 128] for c in range(8)]
            inv, vx, vy, vz, pressure, half_b2 = primitive(u)
            xx, yy, zz = (b * b for b in u[5:])
            fast_x, fast_y = fast_pair(inv, pressure, half_b2, yy + zz, xx + zz)
            rate = jnp.maximum(jnp.abs(vx) + fast_x, jnp.abs(vy) + fast_y)
            peak = jnp.maximum(peak, jnp.where(weight > 0.0, rate * weight, 0.0))
    VS[0] = jnp.max(peak, axis=0, keepdims=True)

    def rotate(h, carry):
        for cc in range(4):
            c = 4 * h + cc
            for rx in range(2):
                for q in range(4):
                    a = X[c, 8 * q : 8 * q + 8, 256 * rx : 256 * rx + 128]
                    b = X[c, 8 * q : 8 * q + 8, 256 * rx + 128 : 256 * rx + 256]
                    a32, b32 = roll(a, -32), roll(b, 32)
                    top = jnp.where(lane8 < 32, a, jnp.where(lane8 < 64, a32, jnp.where(lane8 < 96, roll(b, 64), b32)))
                    low = jnp.where(lane8 < 32, a32, jnp.where(lane8 < 64, roll(a, -64), jnp.where(lane8 < 96, b32, b)))
                    row = FINE[0] + 4 + 64 * rx + 8 * q
                    G[c, row : row + 8, :] = top
                    G[c, row + 32 : row + 40, :] = low
                    Z[c, rx, 8 * q : 8 * q + 8, :] = jnp.where(lane8 < 32, a, b32)
        return carry

    def spread(h, carry):
        row8 = lax.broadcasted_iota(jnp.int32, (8, 128), 0)
        half = row8 % 4 * 2
        halves = lane8 * 2 % 128
        for cc in range(4):
            c = 4 * h + cc
            for rx in range(2):
                keep = jnp.where(lane8 < 64, mine[2 * rx], mine[2 * rx + 1]) > 0
                fine = []
                for q in range(4):
                    z = jnp.take_along_axis(Z[c, rx, 8 * q : 8 * q + 8, :], lane8 // 2, axis=1)
                    for i in range(2):
                        row = FINE[0] + 4 + 64 * rx + 16 * q + 8 * i
                        x = jnp.take_along_axis(z, row8 // 2 + 4 * i, axis=0)
                        x = jnp.where(keep, G[c, row : row + 8, :], x)
                        G[c, row : row + 8, :] = x
                        G[c, row + 136 : row + 144, :] = x
                        x = x + pltpu.roll(x, 7, 0)
                        fine.append(jnp.take_along_axis(x, half, axis=0))
                for q in range(4):
                    x = jnp.where(row8 < 4, fine[2 * q], fine[2 * q + 1])
                    x = 0.25 * (jnp.take_along_axis(x, halves, axis=1) + jnp.take_along_axis(x, halves + 1, axis=1))
                    for base in COARSE:
                        row = base + 4 + 32 * rx + 8 * q
                        G[c, row : row + 8, :] = x
        return carry

    lax.fori_loop(0, 2, rotate, 0)
    lax.fori_loop(0, 2, spread, 0)

    def pack_columns():
        for h in range(2):
            for q in range(4):
                acc_r, acc_l = zero8, zero8
                for cc in range(4):
                    for k in range(6):
                        s = 32 * cc + 4 * k
                        row = (FINE[0] + 4 + 32 * k if k < 4 else COARSE[0] + 4 + 32 * (k - 4)) + 8 * q
                        x = roll(G[4 * h + cc, row : row + 8, :], s + 4)
                        acc_r = jnp.where((lane8 >= s) & (lane8 < s + 4), x, acc_r)
                        acc_l = jnp.where((lane8 >= s + 4) & (lane8 < s + 8), x, acc_l)
                SY[0, h, 8 * q : 8 * q + 8, :] = acc_r
                SY[1, h, 8 * q : 8 * q + 8, :] = acc_l

    pack_columns()

    def pack_rows():
        for d in range(2):
            corner = zero8
            fine, coarse = FINE[0] + 4 + (124, 0)[d], COARSE[0] + 4 + (60, 0)[d]
            for c in range(8):
                SR[d, c, 0:4, :] = G[c, fine : fine + 4, :]
                SR[d, c, 4:8, :] = G[c, coarse : coarse + 4, :]
                corner = jnp.where(lane8 // 8 == c, roll(SR[d, c], 8 * c + 4), corner)
            SK[d] = corner

    pack_rows()

    ghosts = [
        remote(SY.at[0], RY.at[0], at(0, 1)),
        remote(SY.at[1], RY.at[1], at(0, -1)),
        remote(SR.at[0], RB.at[0], at(1, 0)),
        remote(SR.at[1], RB.at[1], at(-1, 0)),
        remote(SK.at[0], RK.at[0], at(1, 1)),
        remote(SK.at[0], RK.at[1], at(1, -1)),
        remote(SK.at[1], RK.at[2], at(-1, 1)),
        remote(SK.at[1], RK.at[3], at(-1, -1)),
    ]
    round1 = [remote(VS.at[0], P1.at[s - 1], at(0, s)) for s in farthest(ngy, 2)]
    pl.semaphore_wait(barrier, len(partners))
    for copy in ghosts[2:] + ghosts[:2] + round1:
        copy.start()

    load_v.wait()
    tile_of = lax.broadcasted_iota(jnp.int32, (2 * ngy, 2 * ngx), 1) // 2 * ngy
    tile_of = tile_of + lax.broadcasted_iota(jnp.int32, (2 * ngy, 2 * ngx), 0) // 2
    before = jnp.sum(jnp.where(tile_of < me, ref_v[...], 0))
    excess = 4 * me + 3 * before - CAP * me
    prev = flags_of(lax.rem(me + ngx * ngy - 1, ngx * ngy))
    following = flags_of(lax.rem(me + 1, ngx * ngy))

    def count_of(fl):
        return 4 + 3 * (fl[0] + fl[1] + fl[2] + fl[3])

    count = count_of(mine)

    def ge(a, b):
        return jnp.where(a >= b, 1, 0)

    def find(index, fl):
        index = jnp.clip(index, 0, count_of(fl) - 1)
        p1 = 1 + 3 * fl[0]
        p2 = p1 + 1 + 3 * fl[1]
        p3 = p2 + 1 + 3 * fl[2]
        a1, a2, a3 = ge(index, p1), ge(index, p2), ge(index, p3)
        child = index - (a1 * p1 + a2 * (p2 - p1) + a3 * (p3 - p2))
        flag = fl[0] + a1 * (fl[1] - fl[0]) + a2 * (fl[2] - fl[1]) + a3 * (fl[3] - fl[2])
        rx = a2
        ry = a1 + a2 + a3 - 2 * rx
        cx, cy = child & 1, child >> 1
        row = flag * (FINE[0] + 136 * ry + 64 * rx + 32 * cx) + (1 - flag) * (COARSE[0] + 72 * ry + 32 * rx)
        lane = flag * (64 * ry + 32 * cy) + (1 - flag) * 96 * ry - 4
        return row, lane, flag

    place = {w: find(w - excess, mine) for w in range(-3, 13)}
    wide = {}
    for w in range(CAP):
        flag = place[w][2]
        index = w - excess
        if w < 3:
            flag = jnp.where(index >= 0, flag, find(index + count_of(prev), prev)[2])
        if w >= 7:
            flag = jnp.where(index < count, flag, find(index - count, following)[2])
        wide[w] = 0.5 + 0.5 * flag.astype(F32)

    left8, right8 = lane8 >= 124, lane8 < 4
    left32, right32 = lane32 >= 124, lane32 < 4

    def fill_lanes():
        for h in range(2):
            low4 = lane32 % 8 < 4
            pair = (jnp.where(low4, RY[0, h], RY[1, h]), jnp.where(low4, RY[1, h], RY[0, h]))
            for cc in range(4):
                for k in range(6):
                    x = roll(pair[k % 2], -(32 * cc + 4 * k) - 4)
                    for i, mask in enumerate((left32, right32)):
                        row = FINE[i] + 4 + 32 * k if k < 4 else COARSE[i] + 4 + 32 * (k - 4)
                        pltpu.store(G.at[4 * h + cc, pl.ds(row, 32), :], x, mask=mask)

    for copy in ghosts[:2]:
        copy.wait_recv()
    fill_lanes()

    for copy in round1:
        copy.wait_recv()
    top = VS[0]
    for s in range(ngy - 1):
        top = jnp.maximum(top, P1[s])
    VS[1] = top
    round2 = [remote(VS.at[1], P2.at[s - 1], at(s, 0)) for s in farthest(ngx, 4)]
    for copy in round2:
        copy.start()

    def fill_rows():
        for d in range(2):
            corner = jnp.where(lane8 % 8 < 4, RK[2 * d], RK[2 * d + 1])
            for c in range(8):
                piece = roll(corner, -8 * c - 4)
                row = RB[d, c]
                for i, mask in enumerate((left8, right8)):
                    x = jnp.where(mask, piece, row)
                    fine, coarse = FINE[i] + 132 * d, COARSE[i] + 68 * d
                    G[c, fine : fine + 4, :] = x[0:4]
                    G[c, coarse : coarse + 4, :] = x[4:8]

    for copy in ghosts[2:]:
        copy.wait_recv()
    fill_rows()

    def gather(dst, which, some=range(8)):
        for c in some:
            parts = [roll(G[c, pl.ds(place[w][0], EXT), :], EXT * g - place[w][1]) for g, w in enumerate(which)]
            x = parts[0]
            for g, part in enumerate(parts[1:]):
                x = jnp.where(lane40 < EXT * (g + 1), x, part)
            dst[c] = x

    carry_up = lax.div(gy + 1, ngy)
    carry_down = lax.div(ngy - gy, ngy)
    ahead = (lax.rem(gx + carry_up, ngx), lax.rem(gy + 1, ngy))
    behind = (lax.rem(gx + ngx - carry_down, ngx), lax.rem(gy + ngy - 1, ngy))
    moves = []
    for part in range(2):
        gather(MR, (10, 11, 12), range(4 * part, 4 * part + 4))
        gather(ML, (-3, -2, -1), range(4 * part, 4 * part + 4))
        some = pl.ds(4 * part, 4)
        moves.append(remote(MR.at[some], U.at[4, some], ahead))
        moves.append(remote(ML.at[some], U.at[5, some], behind))
        for copy in moves[-2:]:
            copy.start()

    gather(U.at[0], (3, 4, 5))
    gather(U.at[1], (6,))
    gather(U.at[2], (0, 1, 2))
    gather(U.at[3], (7, 8, 9))

    def first(t, carry, pick=lambda t: t):
        at_u = pick(t)
        for r in ROWS:
            u = [U[at_u, c, r : r + 8, :] for c in range(8)]
            flux_x, edge_x, flux_y, edge_y = cell_state(u)
            for i, v in enumerate(flux_x + edge_x):
                SX[i, r : r + 8, :] = v
            _, _, a, b, w = edge_weights(*edge_y, roll(edge_y[0], -1), roll(edge_y[1], -1))
            cell = (u[2],) + flux_y[:5] + (None,) + flux_y[5:]
            for c in range(8):
                jump = w * (roll(u[c], -1) - u[c])
                flux = jump if cell[c] is None else a * cell[c] + b * roll(cell[c], -1) + jump
                DY[t, c, r : r + 8, :] = flux - roll(flux, 1)
        for r in FACE1:
            edges = [SX[i, r + d : r + d + 8, :] for d in range(2) for i in (6, 7)]
            _, _, a, b, w = edge_weights(*edges)
            for c in range(8):
                low, high = U[at_u, c, r : r + 8, :], U[at_u, c, r + 1 : r + 9, :]
                flux = w * (high - low)
                if c == 0:
                    flux = a * U[at_u, 1, r : r + 8, :] + b * U[at_u, 1, r + 1 : r + 9, :] + flux
                elif c != 5:
                    i = c - 1 if c < 5 else c - 2
                    flux = a * SX[i, r : r + 8, :] + b * SX[i, r + 1 : r + 9, :] + flux
                GX[t, c, r : r + 8, :] = flux
        return carry

    lax.fori_loop(0, 2, first, 0)

    for copy in moves:
        copy.wait_recv()

    def pick(t):
        from_left = jnp.where(excess > 0, 4, 2)
        from_right = jnp.where(excess + count < CAP, 5, 3)
        return jnp.where(t == 2, from_left, jnp.where(t == 3, from_right, t))

    lax.fori_loop(2, 4, functools.partial(first, pick=pick), 0)

    def widths(ws):
        v = jnp.full((8, 128), wide[ws[0]], F32)
        for g, w in enumerate(ws[1:]):
            v = jnp.where(lane8 < EXT * (g + 1), v, wide[w])
        return v

    VM[0] = widths((3, 4, 5))
    VM[1] = widths((6,))
    VM[2] = widths((0, 1, 2))
    VM[3] = widths((7, 8, 9))

    for copy in ghosts + round1 + moves + round2:
        copy.wait_send()
    for copy in round2:
        copy.wait_recv()
    for s in range(ngx - 1):
        top = jnp.maximum(top, P2[s])
    top = jnp.max(top, axis=1, keepdims=True)
    time_step = COURANT / jnp.broadcast_to(top, (8, 128))

    def second(t, carry):
        rate = time_step * VM[t]
        at_u = pick(t)
        half = 0.5 * rate
        for r in MID:
            u = []
            for c in range(8):
                change = GX[t, c, r : r + 8, :] - GX[t, c, r - 1 : r + 7, :] + DY[t, c, r : r + 8, :]
                u.append(U[at_u, c, r : r + 8, :] - half * change)
            _, vx, vy, vz, pressure, _ = primitive(u)
            for c, v in enumerate((u[0], vx, vy, vz, pressure, u[5], u[6], u[7])):
                W[c, r : r + 8, :] = v
        for r in SLOPE:
            for c in range(8):
                w = [W[c, r + d : r + d + 8, :] for d in (-1, 0, 1, 2)]
                low, d, high = w[1] - w[0], w[2] - w[1], w[3] - w[2]
                rise = limited(0.5 * d + (low - high) * (1.0 / 12.0), d)
                RA[c, r : r + 8, :] = rise
                EA[c, r : r + 8, :] = d - rise
        for r in FACE2:
            left, right = [], []
            for c in range(8):
                rise, rise_next = RA[c, r : r + 8, :], RA[c, r + 1 : r + 9, :]
                fall, fall_next = EA[c, r - 1 : r + 7, :], EA[c, r : r + 8, :]
                left.append(W[c, r : r + 8, :] + limited(rise, 2.0 * fall))
                right.append(W[c, r + 1 : r + 9, :] - limited(fall_next, 2.0 * rise_next))
            for c, v in enumerate(face_flux(left, right, 1)):
                GX2[c, r : r + 8, :] = v
        for r in LAST:
            left, right = [], []
            for c in range(8):
                w = W[c, r : r + 8, :]
                ahead_w = roll(w, -1)
                d = ahead_w - w
                rise = limited(0.5 * d + (roll(d, 1) - roll(d, -1)) * (1.0 / 12.0), d)
                fall = d - rise
                left.append(w + limited(rise, 2.0 * roll(fall, 1)))
                right.append(ahead_w - limited(fall, 2.0 * roll(rise, -1)))
            for c, v in enumerate(face_flux(left, right, 2)):
                change = GX2[c, r : r + 8, :] - GX2[c, r - 1 : r + 7, :] + (v - roll(v, 1))
                O[t, c, r - 4 : r + 4, :] = U[at_u, c, r : r + 8, :] - rate * change
        return carry

    lax.fori_loop(0, 4, second, 0)

    def finish_local():
        for c in range(8):
            o0, o1 = O[0, c], O[1, c]
            out[c, :, 0:128] = roll(o0, 92)
            x = jnp.where(lane32 < 64, roll(o0, -52), roll(o1, 60))
            out[c, :, 128:256] = jnp.where(lane32 < 32, roll(o0, -44), x)

    finish_local()


    def finish():
        for c in range(8):
            o2, o3 = O[2, c], O[3, c]
            x = jnp.where(lane32 < 32, roll(o2, -4), jnp.where(lane32 < 64, roll(o2, -12), roll(o2, -20)))
            pltpu.store(out.at[c, :, pl.ds(0, 128)], x, mask=lane32 < 96)
            pltpu.store(out.at[c, :, pl.ds(128, 128)], roll(o3, 92), mask=lane32 >= 96)
            x = jnp.where(lane32 < 32, roll(o3, -44), roll(o3, -52))
            out[c, :, 256:320] = x[:, 0:64]

    finish()


def shards(ngx, ngy, fields, refined):
    vmem = lambda *shape: pltpu.VMEM(shape, F32)
    scratch = [
        pltpu.SMEM((2 * ngy, 2 * ngx), jnp.int32),
        pltpu.VMEM((2 * ngy, 2 * ngx), jnp.int32),
        vmem(8, 32, 512),
        vmem(8, 2, BS, 128),
        vmem(8, PAD_ROWS, 128),
        vmem(6, 8, EXT, 128),
        vmem(8, EXT, 128),
        vmem(8, EXT, 128),
        vmem(2, 8, 8, 128),
        vmem(2, 8, 8, 128),
        vmem(2, 8, 128),
        vmem(4, 8, 128),
        vmem(2, 2, 32, 128),
        vmem(2, 2, 32, 128),
        vmem(4, 8, 128),
        vmem(2, 1, 128),
        vmem(ngy - 1, 1, 128),
        vmem(ngx - 1, 1, 128),
        vmem(8, EXT, 128),
        vmem(4, 8, EXT, 128),
        vmem(4, 8, EXT, 128),
        vmem(8, EXT, 128),
        vmem(8, EXT, 128),
        vmem(8, EXT, 128),
        vmem(8, EXT, 128),
        vmem(4, 8, BS, 128),
        pltpu.SemaphoreType.DMA((3,)),
        pltpu.SemaphoreType.DMA((ngx + ngy + 10,)),
        pltpu.SemaphoreType.DMA((ngx + ngy + 10,)),
    ]
    return pl.pallas_call(
        functools.partial(kernel, ngx, ngy),
        out_shape=jax.ShapeDtypeStruct((8, BS, CAP * BS), F32),
        in_specs=[
            pl.BlockSpec(memory_space=pltpu.HBM),
            pl.BlockSpec(memory_space=pltpu.HBM),
        ],
        out_specs=pl.BlockSpec(memory_space=pltpu.VMEM),
        scratch_shapes=scratch,
        compiler_params=pltpu.CompilerParams(
            collective_id=0, has_side_effects=True, vmem_limit_bytes=56_000_000
        ),
    )(refined.T, fields)


def solution(mesh):
    ngx, ngy = mesh.shape["gx"], mesh.shape["gy"]
    return jax.shard_map(
        functools.partial(shards, ngx, ngy),
        mesh=mesh,
        in_specs=(P(None, None, ("gx", "gy")), P()),
        out_specs=P(None, None, ("gx", "gy")),
        check_vma=False,
    )
```

```python
import functools

import jax
import jax.numpy as jnp
from jax import lax
from jax.experimental import pallas as pl
from jax.experimental.pallas import tpu as pltpu
from jax.sharding import PartitionSpec as P

BS = 32
CAP = 10
EXT = BS + 8
GAMMA = 5.0 / 3.0
COURANT = 0.2
MESH = pl.DeviceIdType.MESH
F32 = jnp.float32

FINE = (4, 140)
COARSE = (276, 348)
PAD_ROWS = 424
ROWS = (0, 8, 16, 24, 32)
FACE1 = (0, 8, 16, 24, 31)
MID = (1, 9, 17, 25, 31)
SLOPE = (2, 10, 18, 26, 29)
FACE2 = (3, 11, 19, 27, 28)
LAST = (4, 12, 20, 28)


def lanes(rows):
    return lax.broadcasted_iota(jnp.int32, (rows, 128), 1)


def roll(x, by):
    if isinstance(by, int):
        by = by % 128
        return x if by == 0 else pltpu.roll(x, by, 1)
    return pltpu.roll(x, lax.rem(by + 256, 128), 1)


def recip(x):
    return pltpu.reciprocal(x, approx=True)


def root(x):
    return x * lax.rsqrt(jnp.maximum(x, 1e-30))


def farthest(count, minor):
    major = max(count // minor, 1)

    def hops(step):
        outer, inner = step // minor, step % minor
        return min(outer, major - outer) + min(inner, minor - inner)

    return sorted(range(1, count), key=lambda step: -hops(step))


def limited(value, other):
    return jnp.minimum(jnp.maximum(value, jnp.minimum(other, 0.0)), jnp.maximum(other, 0.0))


def primitive(u):
    rho, mx, my, mz, energy, bx, by, bz = u
    inv = recip(rho)
    vx, vy, vz = mx * inv, my * inv, mz * inv
    half_b2 = 0.5 * (bx * bx + by * by + bz * bz)
    kinetic = 0.5 * (mx * vx + my * vy + mz * vz)
    pressure = (GAMMA - 1.0) * (energy - kinetic - half_b2)
    return inv, vx, vy, vz, pressure, half_b2


def fast_pair(inv, pressure, half_b2, trans_x, trans_y):
    sound = GAMMA * pressure * inv
    alfven = 2.0 * half_b2 * inv
    total = sound + alfven
    diff = sound - alfven
    square = diff * diff
    four = 4.0 * sound * inv
    fast_x = root(0.5 * (total + root(square + four * trans_x)))
    fast_y = root(0.5 * (total + root(square + four * trans_y)))
    return fast_x, fast_y


def cell_state(u):
    rho, mx, my, mz, energy, bx, by, bz = u
    inv, vx, vy, vz, pressure, half_b2 = primitive(u)
    xx, yy, zz = bx * bx, by * by, bz * bz
    fast_x, fast_y = fast_pair(inv, pressure, half_b2, yy + zz, xx + zz)
    total_p = pressure + half_b2
    enthalpy = energy + total_p
    vb = vx * bx + vy * by + vz * bz
    cross = mx * vy - bx * by
    emf = by * vx - bx * vy
    flux_x = (mx * vx + total_p - xx, cross, mx * vz - bx * bz, enthalpy * vx - bx * vb, emf, bz * vx - bx * vz)
    flux_y = (cross, my * vy + total_p - yy, my * vz - by * bz, enthalpy * vy - by * vb, -emf, bz * vy - by * vz)
    return flux_x, (vx - fast_x, vx + fast_x), flux_y, (vy - fast_y, vy + fast_y)


def edge_weights(slow_l, fast_l, slow_r, fast_r):
    slow = jnp.minimum(jnp.minimum(slow_l, slow_r), 0.0)
    fast = jnp.maximum(jnp.maximum(fast_l, fast_r), 0.0)
    inv = recip(fast - slow)
    a = fast * inv
    b = -slow * inv
    return slow, fast, a, b, slow * a


def side(w, normal):
    rho, vx, vy, vz, pressure, bx, by, bz = w
    vn, vt, bn, bt = (vx, vy, bx, by) if normal == 1 else (vy, vx, by, bx)
    inv = recip(rho)
    trans = bt * bt + bz * bz
    nn = bn * bn
    b2 = trans + nn
    sound = GAMMA * pressure * inv
    alfven = b2 * inv
    diff = sound - alfven
    fast = root(0.5 * (sound + alfven + root(diff * diff + 4.0 * sound * inv * trans)))
    half_b2 = 0.5 * b2
    total_p = pressure + half_b2
    energy = 1.5 * pressure + half_b2 + 0.5 * rho * (vn * vn + vt * vt + vz * vz)
    vb = vn * bn + vt * bt + vz * bz
    return vn - fast, vn + fast, (rho, vn, vt, vz, bn, bt, bz, energy, total_p, total_p - nn, vb)


def moved(state, speed):
    rho, vn, vt, vz, bn, bt, bz, energy, total_p, stress, vb = state
    rel = vn - speed
    mass = rho * rel
    return (
        mass,
        mass * vn + stress,
        mass * vt - bn * bt,
        mass * vz - bn * bz,
        energy * rel + total_p * vn - bn * vb,
        bt * rel - bn * vt,
        bz * rel - bn * vz,
    )


def face_flux(left, right, normal):
    slow_l, fast_l, state_l = side(left, normal)
    slow_r, fast_r, state_r = side(right, normal)
    slow, fast, a, b, c = edge_weights(slow_l, fast_l, slow_r, fast_r)
    from_l = moved(state_l, slow)
    from_r = moved(state_r, fast)
    mass, mn, mt, mz, en, bt, bz = (a * p + b * q for p, q in zip(from_l, from_r))
    bn = c * (state_r[4] - state_l[4])
    if normal == 1:
        return (mass, mn, mt, mz, en, bn, bt, bz)
    return (mass, mt, mn, mz, en, bt, bn, bz)


def kernel(ngx, ngy, refined, fields, out, *scratch):
    (ref_s, ref_v, X, Z, G, U, ML, MR, SR, RB, SK, RK, SY, RY, VM, VS, P1, P2, SX, GX, DY, W, RA, EA, GX2, O, in_sem, send, recv) = scratch
    gx = lax.axis_index("gx")
    gy = lax.axis_index("gy")
    me = gx * ngy + gy
    load = pltpu.make_async_copy(fields, X, in_sem.at[0])
    load.start()
    load_s = pltpu.make_async_copy(refined, ref_s, in_sem.at[1])
    load_s.start()
    load_v = pltpu.make_async_copy(refined, ref_v, in_sem.at[2])
    load_v.start()

    def at(dx, dy):
        return lax.rem(gx + dx + ngx, ngx), lax.rem(gy + dy + ngy, ngy)

    partners = [at(0, s) for s in range(1, ngy)] + [at(s, 0) for s in range(1, ngx)]
    partners += [at(1, 1), at(1, -1), at(-1, 1), at(-1, -1)]
    barrier = pltpu.get_barrier_semaphore()
    for who in partners:
        pl.semaphore_signal(barrier, inc=1, device_id=who, device_id_type=MESH)

    sems = iter(range(64))

    def remote(src, dst, who):
        i = next(sems)
        return pltpu.make_async_remote_copy(
            src_ref=src, dst_ref=dst, send_sem=send.at[i], recv_sem=recv.at[i], device_id=who, device_id_type=MESH
        )

    def flags_of(tile):
        tx, ty = lax.div(tile, ngy), lax.rem(tile, ngy)
        return [ref_s[2 * ty + r % 2, 2 * tx + r // 2] for r in range(4)]

    load_s.wait()
    mine = flags_of(me)
    lane8, lane32, lane40 = lanes(8), lanes(32), lanes(EXT)
    load.wait()

    zero8 = jnp.zeros((8, 128), F32)
    peak = zero8
    for r in range(4):
        on = mine[r] > 0
        weight = jnp.where(lane8 < 32, jnp.where(on, 1.0, 0.5), jnp.where(on, 1.0, 0.0)).astype(F32)
        for q in range(4):
            u = [X[c, 8 * q : 8 * q + 8, 128 * r : 128 * r + 128] for c in range(8)]
            inv, vx, vy, vz, pressure, half_b2 = primitive(u)
            xx, yy, zz = (b * b for b in u[5:])
            fast_x, fast_y = fast_pair(inv, pressure, half_b2, yy + zz, xx + zz)
            rate = jnp.maximum(jnp.abs(vx) + fast_x, jnp.abs(vy) + fast_y)
            peak = jnp.maximum(peak, jnp.where(weight > 0.0, rate * weight, 0.0))
    VS[0] = jnp.max(peak, axis=0, keepdims=True)

    def rotate(h, carry):
        for cc in range(4):
            c = 4 * h + cc
            for rx in range(2):
                for q in range(4):
                    a = X[c, 8 * q : 8 * q + 8, 256 * rx : 256 * rx + 128]
                    b = X[c, 8 * q : 8 * q + 8, 256 * rx + 128 : 256 * rx + 256]
                    a32, b32 = roll(a, -32), roll(b, 32)
                    top = jnp.where(lane8 < 32, a, jnp.where(lane8 < 64, a32, jnp.where(lane8 < 96, roll(b, 64), b32)))
                    low = jnp.where(lane8 < 32, a32, jnp.where(lane8 < 64, roll(a, -64), jnp.where(lane8 < 96, b32, b)))
                    row = FINE[0] + 4 + 64 * rx + 8 * q
                    G[c, row : row + 8, :] = top
                    G[c, row + 32 : row + 40, :] = low
                    Z[c, rx, 8 * q : 8 * q + 8, :] = jnp.where(lane8 < 32, a, b32)
        return carry

    def spread(h, carry):
        row8 = lax.broadcasted_iota(jnp.int32, (8, 128), 0)
        half = row8 % 4 * 2
        halves = lane8 * 2 % 128
        for cc in range(4):
            c = 4 * h + cc
            for rx in range(2):
                keep = jnp.where(lane8 < 64, mine[2 * rx], mine[2 * rx + 1]) > 0
                fine = []
                for q in range(4):
                    z = jnp.take_along_axis(Z[c, rx, 8 * q : 8 * q + 8, :], lane8 // 2, axis=1)
                    for i in range(2):
                        row = FINE[0] + 4 + 64 * rx + 16 * q + 8 * i
                        x = jnp.take_along_axis(z, row8 // 2 + 4 * i, axis=0)
                        x = jnp.where(keep, G[c, row : row + 8, :], x)
                        G[c, row : row + 8, :] = x
                        G[c, row + 136 : row + 144, :] = x
                        x = x + pltpu.roll(x, 7, 0)
                        fine.append(jnp.take_along_axis(x, half, axis=0))
                for q in range(4):
                    x = jnp.where(row8 < 4, fine[2 * q], fine[2 * q + 1])
                    x = 0.25 * (jnp.take_along_axis(x, halves, axis=1) + jnp.take_along_axis(x, halves + 1, axis=1))
                    for base in COARSE:
                        row = base + 4 + 32 * rx + 8 * q
                        G[c, row : row + 8, :] = x
        return carry

    lax.fori_loop(0, 2, rotate, 0)
    lax.fori_loop(0, 2, spread, 0)

    def pack_columns():
        for h in range(2):
            for q in range(4):
                acc_r, acc_l = zero8, zero8
                for cc in range(4):
                    for k in range(6):
                        s = 32 * cc + 4 * k
                        row = (FINE[0] + 4 + 32 * k if k < 4 else COARSE[0] + 4 + 32 * (k - 4)) + 8 * q
                        x = roll(G[4 * h + cc, row : row + 8, :], s + 4)
                        acc_r = jnp.where((lane8 >= s) & (lane8 < s + 4), x, acc_r)
                        acc_l = jnp.where((lane8 >= s + 4) & (lane8 < s + 8), x, acc_l)
                SY[0, h, 8 * q : 8 * q + 8, :] = acc_r
                SY[1, h, 8 * q : 8 * q + 8, :] = acc_l

    pack_columns()

    def pack_rows():
        for d in range(2):
            corner = zero8
            fine, coarse = FINE[0] + 4 + (124, 0)[d], COARSE[0] + 4 + (60, 0)[d]
            for c in range(8):
                SR[d, c, 0:4, :] = G[c, fine : fine + 4, :]
                SR[d, c, 4:8, :] = G[c, coarse : coarse + 4, :]
                corner = jnp.where(lane8 // 8 == c, roll(SR[d, c], 8 * c + 4), corner)
            SK[d] = corner

    pack_rows()

    ghosts = [
        remote(SY.at[0], RY.at[0], at(0, 1)),
        remote(SY.at[1], RY.at[1], at(0, -1)),
        remote(SR.at[0], RB.at[0], at(1, 0)),
        remote(SR.at[1], RB.at[1], at(-1, 0)),
        remote(SK.at[0], RK.at[0], at(1, 1)),
        remote(SK.at[0], RK.at[1], at(1, -1)),
        remote(SK.at[1], RK.at[2], at(-1, 1)),
        remote(SK.at[1], RK.at[3], at(-1, -1)),
    ]
    round1 = [remote(VS.at[0], P1.at[s - 1], at(0, s)) for s in farthest(ngy, 2)]
    pl.semaphore_wait(barrier, len(partners))
    for copy in ghosts[2:] + ghosts[:2] + round1:
        copy.start()

    load_v.wait()
    tile_of = lax.broadcasted_iota(jnp.int32, (2 * ngy, 2 * ngx), 1) // 2 * ngy
    tile_of = tile_of + lax.broadcasted_iota(jnp.int32, (2 * ngy, 2 * ngx), 0) // 2
    before = jnp.sum(jnp.where(tile_of < me, ref_v[...], 0))
    excess = 4 * me + 3 * before - CAP * me
    prev = flags_of(lax.rem(me + ngx * ngy - 1, ngx * ngy))
    following = flags_of(lax.rem(me + 1, ngx * ngy))

    def count_of(fl):
        return 4 + 3 * (fl[0] + fl[1] + fl[2] + fl[3])

    count = count_of(mine)

    def ge(a, b):
        return jnp.where(a >= b, 1, 0)

    def find(index, fl):
        index = jnp.clip(index, 0, count_of(fl) - 1)
        p1 = 1 + 3 * fl[0]
        p2 = p1 + 1 + 3 * fl[1]
        p3 = p2 + 1 + 3 * fl[2]
        a1, a2, a3 = ge(index, p1), ge(index, p2), ge(index, p3)
        child = index - (a1 * p1 + a2 * (p2 - p1) + a3 * (p3 - p2))
        flag = fl[0] + a1 * (fl[1] - fl[0]) + a2 * (fl[2] - fl[1]) + a3 * (fl[3] - fl[2])
        rx = a2
        ry = a1 + a2 + a3 - 2 * rx
        cx, cy = child & 1, child >> 1
        row = flag * (FINE[0] + 136 * ry + 64 * rx + 32 * cx) + (1 - flag) * (COARSE[0] + 72 * ry + 32 * rx)
        lane = flag * (64 * ry + 32 * cy) + (1 - flag) * 96 * ry - 4
        return row, lane, flag

    place = {w: find(w - excess, mine) for w in range(-3, 13)}
    wide = {}
    for w in range(CAP):
        flag = place[w][2]
        index = w - excess
        if w < 3:
            flag = jnp.where(index >= 0, flag, find(index + count_of(prev), prev)[2])
        if w >= 7:
            flag = jnp.where(index < count, flag, find(index - count, following)[2])
        wide[w] = 0.5 + 0.5 * flag.astype(F32)

    left8, right8 = lane8 >= 124, lane8 < 4
    left32, right32 = lane32 >= 124, lane32 < 4

    def fill_lanes():
        for h in range(2):
            low4 = lane32 % 8 < 4
            pair = (jnp.where(low4, RY[0, h], RY[1, h]), jnp.where(low4, RY[1, h], RY[0, h]))
            for cc in range(4):
                for k in range(6):
                    x = roll(pair[k % 2], -(32 * cc + 4 * k) - 4)
                    for i, mask in enumerate((left32, right32)):
                        row = FINE[i] + 4 + 32 * k if k < 4 else COARSE[i] + 4 + 32 * (k - 4)
                        pltpu.store(G.at[4 * h + cc, pl.ds(row, 32), :], x, mask=mask)

    for copy in ghosts[:2]:
        copy.wait_recv()
    fill_lanes()

    def fill_rows():
        for d in range(2):
            corner = jnp.where(lane8 % 8 < 4, RK[2 * d], RK[2 * d + 1])
            for c in range(8):
                piece = roll(corner, -8 * c - 4)
                row = RB[d, c]
                for i, mask in enumerate((left8, right8)):
                    x = jnp.where(mask, piece, row)
                    fine, coarse = FINE[i] + 132 * d, COARSE[i] + 68 * d
                    G[c, fine : fine + 4, :] = x[0:4]
                    G[c, coarse : coarse + 4, :] = x[4:8]

    for copy in ghosts[2:]:
        copy.wait_recv()
    fill_rows()

    def gather(dst, which, some=range(8)):
        for c in some:
            parts = [roll(G[c, pl.ds(place[w][0], EXT), :], EXT * g - place[w][1]) for g, w in enumerate(which)]
            x = parts[0]
            for g, part in enumerate(parts[1:]):
                x = jnp.where(lane40 < EXT * (g + 1), x, part)
            dst[c] = x

    carry_up = lax.div(gy + 1, ngy)
    carry_down = lax.div(ngy - gy, ngy)
    ahead = (lax.rem(gx + carry_up, ngx), lax.rem(gy + 1, ngy))
    behind = (lax.rem(gx + ngx - carry_down, ngx), lax.rem(gy + ngy - 1, ngy))
    moves = []
    for part in range(2):
        gather(MR, (10, 11, 12), range(4 * part, 4 * part + 4))
        gather(ML, (-3, -2, -1), range(4 * part, 4 * part + 4))
        some = pl.ds(4 * part, 4)
        moves.append(remote(MR.at[some], U.at[4, some], ahead))
        moves.append(remote(ML.at[some], U.at[5, some], behind))
        for copy in moves[-2:]:
            copy.start()

    for copy in round1:
        copy.wait_recv()
    top = VS[0]
    for s in range(ngy - 1):
        top = jnp.maximum(top, P1[s])
    VS[1] = top
    round2 = [remote(VS.at[1], P2.at[s - 1], at(s, 0)) for s in farthest(ngx, 4)]
    for copy in round2:
        copy.start()

    gather(U.at[0], (3, 4, 5))
    gather(U.at[1], (6,))
    gather(U.at[2], (0, 1, 2))
    gather(U.at[3], (7, 8, 9))

    def first(t, carry, pick=lambda t: t):
        at_u = pick(t)
        for r in ROWS:
            u = [U[at_u, c, r : r + 8, :] for c in range(8)]
            flux_x, edge_x, flux_y, edge_y = cell_state(u)
            for i, v in enumerate(flux_x + edge_x):
                SX[i, r : r + 8, :] = v
            _, _, a, b, w = edge_weights(*edge_y, roll(edge_y[0], -1), roll(edge_y[1], -1))
            cell = (u[2],) + flux_y[:5] + (None,) + flux_y[5:]
            for c in range(8):
                jump = w * (roll(u[c], -1) - u[c])
                flux = jump if cell[c] is None else a * cell[c] + b * roll(cell[c], -1) + jump
                DY[t, c, r : r + 8, :] = flux - roll(flux, 1)
        for r in FACE1:
            edges = [SX[i, r + d : r + d + 8, :] for d in range(2) for i in (6, 7)]
            _, _, a, b, w = edge_weights(*edges)
            for c in range(8):
                low, high = U[at_u, c, r : r + 8, :], U[at_u, c, r + 1 : r + 9, :]
                flux = w * (high - low)
                if c == 0:
                    flux = a * U[at_u, 1, r : r + 8, :] + b * U[at_u, 1, r + 1 : r + 9, :] + flux
                elif c != 5:
                    i = c - 1 if c < 5 else c - 2
                    flux = a * SX[i, r : r + 8, :] + b * SX[i, r + 1 : r + 9, :] + flux
                GX[t, c, r : r + 8, :] = flux
        return carry

    lax.fori_loop(0, 2, first, 0)

    def widths(ws):
        v = jnp.full((8, 128), wide[ws[0]], F32)
        for g, w in enumerate(ws[1:]):
            v = jnp.where(lane8 < EXT * (g + 1), v, wide[w])
        return v

    VM[0] = widths((3, 4, 5))
    VM[1] = widths((6,))
    VM[2] = widths((0, 1, 2))
    VM[3] = widths((7, 8, 9))

    for copy in ghosts + round1 + moves + round2:
        copy.wait_send()
    for copy in round2:
        copy.wait_recv()
    for s in range(ngx - 1):
        top = jnp.maximum(top, P2[s])
    top = jnp.max(top, axis=1, keepdims=True)
    time_step = COURANT / jnp.broadcast_to(top, (8, 128))

    def second(t, carry, pick=lambda t: t):
        rate = time_step * VM[t]
        at_u = pick(t)
        half = 0.5 * rate
        for r in MID:
            u = []
            for c in range(8):
                change = GX[t, c, r : r + 8, :] - GX[t, c, r - 1 : r + 7, :] + DY[t, c, r : r + 8, :]
                u.append(U[at_u, c, r : r + 8, :] - half * change)
            _, vx, vy, vz, pressure, _ = primitive(u)
            for c, v in enumerate((u[0], vx, vy, vz, pressure, u[5], u[6], u[7])):
                W[c, r : r + 8, :] = v
        for r in SLOPE:
            for c in range(8):
                w = [W[c, r + d : r + d + 8, :] for d in (-1, 0, 1, 2)]
                low, d, high = w[1] - w[0], w[2] - w[1], w[3] - w[2]
                rise = limited(0.5 * d + (low - high) * (1.0 / 12.0), d)
                RA[c, r : r + 8, :] = rise
                EA[c, r : r + 8, :] = d - rise
        for r in FACE2:
            left, right = [], []
            for c in range(8):
                rise, rise_next = RA[c, r : r + 8, :], RA[c, r + 1 : r + 9, :]
                fall, fall_next = EA[c, r - 1 : r + 7, :], EA[c, r : r + 8, :]
                left.append(W[c, r : r + 8, :] + limited(rise, 2.0 * fall))
                right.append(W[c, r + 1 : r + 9, :] - limited(fall_next, 2.0 * rise_next))
            for c, v in enumerate(face_flux(left, right, 1)):
                GX2[c, r : r + 8, :] = v
        for r in LAST:
            left, right = [], []
            for c in range(8):
                w = W[c, r : r + 8, :]
                ahead_w = roll(w, -1)
                d = ahead_w - w
                rise = limited(0.5 * d + (roll(d, 1) - roll(d, -1)) * (1.0 / 12.0), d)
                fall = d - rise
                left.append(w + limited(rise, 2.0 * roll(fall, 1)))
                right.append(ahead_w - limited(fall, 2.0 * roll(rise, -1)))
            for c, v in enumerate(face_flux(left, right, 2)):
                change = GX2[c, r : r + 8, :] - GX2[c, r - 1 : r + 7, :] + (v - roll(v, 1))
                O[t, c, r - 4 : r + 4, :] = U[at_u, c, r : r + 8, :] - rate * change
        return carry

    lax.fori_loop(0, 2, second, 0)

    def finish_local():
        for c in range(8):
            o0, o1 = O[0, c], O[1, c]
            out[c, :, 0:128] = roll(o0, 92)
            x = jnp.where(lane32 < 64, roll(o0, -52), roll(o1, 60))
            out[c, :, 128:256] = jnp.where(lane32 < 32, roll(o0, -44), x)

    finish_local()

    for copy in moves:
        copy.wait_recv()

    def pick(t):
        from_left = jnp.where(excess > 0, 4, 2)
        from_right = jnp.where(excess + count < CAP, 5, 3)
        return jnp.where(t == 2, from_left, jnp.where(t == 3, from_right, t))

    lax.fori_loop(2, 4, functools.partial(first, pick=pick), 0)
    lax.fori_loop(2, 4, functools.partial(second, pick=pick), 0)

    def finish():
        for c in range(8):
            o2, o3 = O[2, c], O[3, c]
            x = jnp.where(lane32 < 32, roll(o2, -4), jnp.where(lane32 < 64, roll(o2, -12), roll(o2, -20)))
            pltpu.store(out.at[c, :, pl.ds(0, 128)], x, mask=lane32 < 96)
            pltpu.store(out.at[c, :, pl.ds(128, 128)], roll(o3, 92), mask=lane32 >= 96)
            x = jnp.where(lane32 < 32, roll(o3, -44), roll(o3, -52))
            out[c, :, 256:320] = x[:, 0:64]

    finish()


def shards(ngx, ngy, fields, refined):
    vmem = lambda *shape: pltpu.VMEM(shape, F32)
    scratch = [
        pltpu.SMEM((2 * ngy, 2 * ngx), jnp.int32),
        pltpu.VMEM((2 * ngy, 2 * ngx), jnp.int32),
        vmem(8, 32, 512),
        vmem(8, 2, BS, 128),
        vmem(8, PAD_ROWS, 128),
        vmem(6, 8, EXT, 128),
        vmem(8, EXT, 128),
        vmem(8, EXT, 128),
        vmem(2, 8, 8, 128),
        vmem(2, 8, 8, 128),
        vmem(2, 8, 128),
        vmem(4, 8, 128),
        vmem(2, 2, 32, 128),
        vmem(2, 2, 32, 128),
        vmem(4, 8, 128),
        vmem(2, 1, 128),
        vmem(ngy - 1, 1, 128),
        vmem(ngx - 1, 1, 128),
        vmem(8, EXT, 128),
        vmem(4, 8, EXT, 128),
        vmem(4, 8, EXT, 128),
        vmem(8, EXT, 128),
        vmem(8, EXT, 128),
        vmem(8, EXT, 128),
        vmem(8, EXT, 128),
        vmem(4, 8, BS, 128),
        pltpu.SemaphoreType.DMA((3,)),
        pltpu.SemaphoreType.DMA((ngx + ngy + 10,)),
        pltpu.SemaphoreType.DMA((ngx + ngy + 10,)),
    ]
    return pl.pallas_call(
        functools.partial(kernel, ngx, ngy),
        out_shape=jax.ShapeDtypeStruct((8, BS, CAP * BS), F32),
        in_specs=[
            pl.BlockSpec(memory_space=pltpu.HBM),
            pl.BlockSpec(memory_space=pltpu.HBM),
        ],
        out_specs=pl.BlockSpec(memory_space=pltpu.VMEM),
        scratch_shapes=scratch,
        compiler_params=pltpu.CompilerParams(
            collective_id=0, has_side_effects=True, vmem_limit_bytes=56_000_000
        ),
    )(refined.T, fields)


def solution(mesh):
    ngx, ngy = mesh.shape["gx"], mesh.shape["gy"]
    return jax.shard_map(
        functools.partial(shards, ngx, ngy),
        mesh=mesh,
        in_specs=(P(None, None, ("gx", "gy")), P()),
        out_specs=P(None, None, ("gx", "gy")),
        check_vma=False,
    )
```

```python
import functools

import jax
import jax.numpy as jnp
from jax import lax
from jax.experimental import pallas as pl
from jax.experimental.pallas import tpu as pltpu
from jax.sharding import PartitionSpec as P

BS = 32
CAP = 10
EXT = BS + 8
GAMMA = 5.0 / 3.0
COURANT = 0.2
MESH = pl.DeviceIdType.MESH
F32 = jnp.float32

FINE = (4, 140)
COARSE = (276, 348)
PAD_ROWS = 424
ROWS = (0, 8, 16, 24, 32)
FACE1 = (0, 8, 16, 24, 31)
MID = (1, 9, 17, 25, 31)
SLOPE = (2, 10, 18, 26, 29)
FACE2 = (3, 11, 19, 27, 28)
LAST = (4, 12, 20, 28)


def lanes(rows):
    return lax.broadcasted_iota(jnp.int32, (rows, 128), 1)


def roll(x, by):
    if isinstance(by, int):
        by = by % 128
        return x if by == 0 else pltpu.roll(x, by, 1)
    return pltpu.roll(x, lax.rem(by + 256, 128), 1)


def recip(x):
    return pltpu.reciprocal(x, approx=True)


def root(x):
    return x * lax.rsqrt(jnp.maximum(x, 1e-30))


def farthest(count, minor):
    major = max(count // minor, 1)

    def hops(step):
        outer, inner = step // minor, step % minor
        return min(outer, major - outer) + min(inner, minor - inner)

    return sorted(range(1, count), key=lambda step: -hops(step))


def limited(value, other):
    return jnp.minimum(jnp.maximum(value, jnp.minimum(other, 0.0)), jnp.maximum(other, 0.0))


def primitive(u):
    rho, mx, my, mz, energy, bx, by, bz = u
    inv = recip(rho)
    vx, vy, vz = mx * inv, my * inv, mz * inv
    half_b2 = 0.5 * (bx * bx + by * by + bz * bz)
    kinetic = 0.5 * (mx * vx + my * vy + mz * vz)
    pressure = (GAMMA - 1.0) * (energy - kinetic - half_b2)
    return inv, vx, vy, vz, pressure, half_b2


def fast_pair(inv, pressure, half_b2, trans_x, trans_y):
    sound = GAMMA * pressure * inv
    alfven = 2.0 * half_b2 * inv
    total = sound + alfven
    diff = sound - alfven
    square = diff * diff
    four = 4.0 * sound * inv
    fast_x = root(0.5 * (total + root(square + four * trans_x)))
    fast_y = root(0.5 * (total + root(square + four * trans_y)))
    return fast_x, fast_y


def cell_state(u):
    rho, mx, my, mz, energy, bx, by, bz = u
    inv, vx, vy, vz, pressure, half_b2 = primitive(u)
    xx, yy, zz = bx * bx, by * by, bz * bz
    fast_x, fast_y = fast_pair(inv, pressure, half_b2, yy + zz, xx + zz)
    total_p = pressure + half_b2
    enthalpy = energy + total_p
    vb = vx * bx + vy * by + vz * bz
    cross = mx * vy - bx * by
    emf = by * vx - bx * vy
    flux_x = (mx * vx + total_p - xx, cross, mx * vz - bx * bz, enthalpy * vx - bx * vb, emf, bz * vx - bx * vz)
    flux_y = (cross, my * vy + total_p - yy, my * vz - by * bz, enthalpy * vy - by * vb, -emf, bz * vy - by * vz)
    return flux_x, (vx - fast_x, vx + fast_x), flux_y, (vy - fast_y, vy + fast_y)


def edge_weights(slow_l, fast_l, slow_r, fast_r):
    slow = jnp.minimum(jnp.minimum(slow_l, slow_r), 0.0)
    fast = jnp.maximum(jnp.maximum(fast_l, fast_r), 0.0)
    inv = recip(fast - slow)
    a = fast * inv
    b = -slow * inv
    return slow, fast, a, b, slow * a


def side(w, normal):
    rho, vx, vy, vz, pressure, bx, by, bz = w
    vn, vt, bn, bt = (vx, vy, bx, by) if normal == 1 else (vy, vx, by, bx)
    inv = recip(rho)
    trans = bt * bt + bz * bz
    nn = bn * bn
    b2 = trans + nn
    sound = GAMMA * pressure * inv
    alfven = b2 * inv
    diff = sound - alfven
    fast = root(0.5 * (sound + alfven + root(diff * diff + 4.0 * sound * inv * trans)))
    half_b2 = 0.5 * b2
    total_p = pressure + half_b2
    energy = 1.5 * pressure + half_b2 + 0.5 * rho * (vn * vn + vt * vt + vz * vz)
    vb = vn * bn + vt * bt + vz * bz
    return vn - fast, vn + fast, (rho, vn, vt, vz, bn, bt, bz, energy, total_p, total_p - nn, vb)


def moved(state, speed):
    rho, vn, vt, vz, bn, bt, bz, energy, total_p, stress, vb = state
    rel = vn - speed
    mass = rho * rel
    return (
        mass,
        mass * vn + stress,
        mass * vt - bn * bt,
        mass * vz - bn * bz,
        energy * rel + total_p * vn - bn * vb,
        bt * rel - bn * vt,
        bz * rel - bn * vz,
    )


def face_flux(left, right, normal):
    slow_l, fast_l, state_l = side(left, normal)
    slow_r, fast_r, state_r = side(right, normal)
    slow, fast, a, b, c = edge_weights(slow_l, fast_l, slow_r, fast_r)
    from_l = moved(state_l, slow)
    from_r = moved(state_r, fast)
    mass, mn, mt, mz, en, bt, bz = (a * p + b * q for p, q in zip(from_l, from_r))
    bn = c * (state_r[4] - state_l[4])
    if normal == 1:
        return (mass, mn, mt, mz, en, bn, bt, bz)
    return (mass, mt, mn, mz, en, bt, bn, bz)


def kernel(ngx, ngy, refined, fields, out, *scratch):
    (ref_s, ref_v, X, Z, G, U, ML, MR, SR, RB, SK, RK, SY, RY, VM, VS, P1, P2, SX, GX, DY, W, RA, EA, GX2, O, in_sem, send, recv) = scratch
    gx = lax.axis_index("gx")
    gy = lax.axis_index("gy")
    me = gx * ngy + gy
    load = pltpu.make_async_copy(fields, X, in_sem.at[0])
    load.start()
    load_s = pltpu.make_async_copy(refined, ref_s, in_sem.at[1])
    load_s.start()
    load_v = pltpu.make_async_copy(refined, ref_v, in_sem.at[2])
    load_v.start()

    def at(dx, dy):
        return lax.rem(gx + dx + ngx, ngx), lax.rem(gy + dy + ngy, ngy)

    partners = [at(0, s) for s in range(1, ngy)] + [at(s, 0) for s in range(1, ngx)]
    partners += [at(1, 1), at(1, -1), at(-1, 1), at(-1, -1)]
    barrier = pltpu.get_barrier_semaphore()
    for who in partners:
        pl.semaphore_signal(barrier, inc=1, device_id=who, device_id_type=MESH)

    sems = iter(range(64))

    def remote(src, dst, who):
        i = next(sems)
        return pltpu.make_async_remote_copy(
            src_ref=src, dst_ref=dst, send_sem=send.at[i], recv_sem=recv.at[i], device_id=who, device_id_type=MESH
        )

    def flags_of(tile):
        tx, ty = lax.div(tile, ngy), lax.rem(tile, ngy)
        return [ref_s[2 * ty + r % 2, 2 * tx + r // 2] for r in range(4)]

    load_s.wait()
    mine = flags_of(me)
    lane8, lane32, lane40 = lanes(8), lanes(32), lanes(EXT)
    load.wait()

    zero8 = jnp.zeros((8, 128), F32)
    peak = zero8
    for r in range(4):
        on = mine[r] > 0
        weight = jnp.where(lane8 < 32, jnp.where(on, 1.0, 0.5), jnp.where(on, 1.0, 0.0)).astype(F32)
        for q in range(4):
            u = [X[c, 8 * q : 8 * q + 8, 128 * r : 128 * r + 128] for c in range(8)]
            inv, vx, vy, vz, pressure, half_b2 = primitive(u)
            xx, yy, zz = (b * b for b in u[5:])
            fast_x, fast_y = fast_pair(inv, pressure, half_b2, yy + zz, xx + zz)
            rate = jnp.maximum(jnp.abs(vx) + fast_x, jnp.abs(vy) + fast_y)
            peak = jnp.maximum(peak, jnp.where(weight > 0.0, rate * weight, 0.0))
    VS[0] = jnp.max(peak, axis=0, keepdims=True)

    def rotate(h, carry):
        for cc in range(4):
            c = 4 * h + cc
            for rx in range(2):
                for q in range(4):
                    a = X[c, 8 * q : 8 * q + 8, 256 * rx : 256 * rx + 128]
                    b = X[c, 8 * q : 8 * q + 8, 256 * rx + 128 : 256 * rx + 256]
                    a32, b32 = roll(a, -32), roll(b, 32)
                    top = jnp.where(lane8 < 32, a, jnp.where(lane8 < 64, a32, jnp.where(lane8 < 96, roll(b, 64), b32)))
                    low = jnp.where(lane8 < 32, a32, jnp.where(lane8 < 64, roll(a, -64), jnp.where(lane8 < 96, b32, b)))
                    row = FINE[0] + 4 + 64 * rx + 8 * q
                    G[c, row : row + 8, :] = top
                    G[c, row + 32 : row + 40, :] = low
                    Z[c, rx, 8 * q : 8 * q + 8, :] = jnp.where(lane8 < 32, a, b32)
        return carry

    def spread(h, carry):
        row8 = lax.broadcasted_iota(jnp.int32, (8, 128), 0)
        half = row8 % 4 * 2
        halves = lane8 * 2 % 128
        for cc in range(4):
            c = 4 * h + cc
            for rx in range(2):
                keep = jnp.where(lane8 < 64, mine[2 * rx], mine[2 * rx + 1]) > 0
                fine = []
                for q in range(4):
                    z = jnp.take_along_axis(Z[c, rx, 8 * q : 8 * q + 8, :], lane8 // 2, axis=1)
                    for i in range(2):
                        row = FINE[0] + 4 + 64 * rx + 16 * q + 8 * i
                        x = jnp.take_along_axis(z, row8 // 2 + 4 * i, axis=0)
                        x = jnp.where(keep, G[c, row : row + 8, :], x)
                        G[c, row : row + 8, :] = x
                        G[c, row + 136 : row + 144, :] = x
                        x = x + pltpu.roll(x, 7, 0)
                        fine.append(jnp.take_along_axis(x, half, axis=0))
                for q in range(4):
                    x = jnp.where(row8 < 4, fine[2 * q], fine[2 * q + 1])
                    x = 0.25 * (jnp.take_along_axis(x, halves, axis=1) + jnp.take_along_axis(x, halves + 1, axis=1))
                    for base in COARSE:
                        row = base + 4 + 32 * rx + 8 * q
                        G[c, row : row + 8, :] = x
        return carry

    lax.fori_loop(0, 2, rotate, 0)
    lax.fori_loop(0, 2, spread, 0)

    def pack_columns():
        for h in range(2):
            for q in range(4):
                acc_r, acc_l = zero8, zero8
                for cc in range(4):
                    for k in range(6):
                        s = 32 * cc + 4 * k
                        row = (FINE[0] + 4 + 32 * k if k < 4 else COARSE[0] + 4 + 32 * (k - 4)) + 8 * q
                        x = roll(G[4 * h + cc, row : row + 8, :], s + 4)
                        acc_r = jnp.where((lane8 >= s) & (lane8 < s + 4), x, acc_r)
                        acc_l = jnp.where((lane8 >= s + 4) & (lane8 < s + 8), x, acc_l)
                SY[0, h, 8 * q : 8 * q + 8, :] = acc_r
                SY[1, h, 8 * q : 8 * q + 8, :] = acc_l

    pack_columns()

    def pack_rows():
        for d in range(2):
            corner = zero8
            fine, coarse = FINE[0] + 4 + (124, 0)[d], COARSE[0] + 4 + (60, 0)[d]
            for c in range(8):
                SR[d, c, 0:4, :] = G[c, fine : fine + 4, :]
                SR[d, c, 4:8, :] = G[c, coarse : coarse + 4, :]
                corner = jnp.where(lane8 // 8 == c, roll(SR[d, c], 8 * c + 4), corner)
            SK[d] = corner

    pack_rows()

    ghosts = [
        remote(SY.at[0], RY.at[0], at(0, 1)),
        remote(SY.at[1], RY.at[1], at(0, -1)),
        remote(SR.at[0], RB.at[0], at(1, 0)),
        remote(SR.at[1], RB.at[1], at(-1, 0)),
        remote(SK.at[0], RK.at[0], at(1, 1)),
        remote(SK.at[0], RK.at[1], at(1, -1)),
        remote(SK.at[1], RK.at[2], at(-1, 1)),
        remote(SK.at[1], RK.at[3], at(-1, -1)),
    ]
    round1 = [remote(VS.at[0], P1.at[s - 1], at(0, s)) for s in farthest(ngy, 2)]
    pl.semaphore_wait(barrier, len(partners))
    for copy in ghosts[2:] + ghosts[:2] + round1:
        copy.start()

    load_v.wait()
    tile_of = lax.broadcasted_iota(jnp.int32, (2 * ngy, 2 * ngx), 1) // 2 * ngy
    tile_of = tile_of + lax.broadcasted_iota(jnp.int32, (2 * ngy, 2 * ngx), 0) // 2
    before = jnp.sum(jnp.where(tile_of < me, ref_v[...], 0))
    excess = 4 * me + 3 * before - CAP * me
    prev = flags_of(lax.rem(me + ngx * ngy - 1, ngx * ngy))
    following = flags_of(lax.rem(me + 1, ngx * ngy))

    def count_of(fl):
        return 4 + 3 * (fl[0] + fl[1] + fl[2] + fl[3])

    count = count_of(mine)

    def ge(a, b):
        return jnp.where(a >= b, 1, 0)

    def find(index, fl):
        index = jnp.clip(index, 0, count_of(fl) - 1)
        p1 = 1 + 3 * fl[0]
        p2 = p1 + 1 + 3 * fl[1]
        p3 = p2 + 1 + 3 * fl[2]
        a1, a2, a3 = ge(index, p1), ge(index, p2), ge(index, p3)
        child = index - (a1 * p1 + a2 * (p2 - p1) + a3 * (p3 - p2))
        flag = fl[0] + a1 * (fl[1] - fl[0]) + a2 * (fl[2] - fl[1]) + a3 * (fl[3] - fl[2])
        rx = a2
        ry = a1 + a2 + a3 - 2 * rx
        cx, cy = child & 1, child >> 1
        row = flag * (FINE[0] + 136 * ry + 64 * rx + 32 * cx) + (1 - flag) * (COARSE[0] + 72 * ry + 32 * rx)
        lane = flag * (64 * ry + 32 * cy) + (1 - flag) * 96 * ry - 4
        return row, lane, flag

    place = {w: find(w - excess, mine) for w in range(-3, 13)}
    wide = {}
    for w in range(CAP):
        flag = place[w][2]
        index = w - excess
        if w < 3:
            flag = jnp.where(index >= 0, flag, find(index + count_of(prev), prev)[2])
        if w >= 7:
            flag = jnp.where(index < count, flag, find(index - count, following)[2])
        wide[w] = 0.5 + 0.5 * flag.astype(F32)

    left8, right8 = lane8 >= 124, lane8 < 4
    left32, right32 = lane32 >= 124, lane32 < 4

    def fill_lanes():
        for h in range(2):
            low4 = lane32 % 8 < 4
            pair = (jnp.where(low4, RY[0, h], RY[1, h]), jnp.where(low4, RY[1, h], RY[0, h]))
            for cc in range(4):
                for k in range(6):
                    x = roll(pair[k % 2], -(32 * cc + 4 * k) - 4)
                    for i, mask in enumerate((left32, right32)):
                        row = FINE[i] + 4 + 32 * k if k < 4 else COARSE[i] + 4 + 32 * (k - 4)
                        pltpu.store(G.at[4 * h + cc, pl.ds(row, 32), :], x, mask=mask)

    for copy in ghosts[:2]:
        copy.wait_recv()
    fill_lanes()

    def fill_rows():
        for d in range(2):
            corner = jnp.where(lane8 % 8 < 4, RK[2 * d], RK[2 * d + 1])
            for c in range(8):
                piece = roll(corner, -8 * c - 4)
                row = RB[d, c]
                for i, mask in enumerate((left8, right8)):
                    x = jnp.where(mask, piece, row)
                    fine, coarse = FINE[i] + 132 * d, COARSE[i] + 68 * d
                    G[c, fine : fine + 4, :] = x[0:4]
                    G[c, coarse : coarse + 4, :] = x[4:8]

    for copy in ghosts[2:]:
        copy.wait_recv()
    fill_rows()

    def gather(dst, which, some=range(8)):
        for c in some:
            parts = [roll(G[c, pl.ds(place[w][0], EXT), :], EXT * g - place[w][1]) for g, w in enumerate(which)]
            x = parts[0]
            for g, part in enumerate(parts[1:]):
                x = jnp.where(lane40 < EXT * (g + 1), x, part)
            dst[c] = x

    carry_up = lax.div(gy + 1, ngy)
    carry_down = lax.div(ngy - gy, ngy)
    ahead = (lax.rem(gx + carry_up, ngx), lax.rem(gy + 1, ngy))
    behind = (lax.rem(gx + ngx - carry_down, ngx), lax.rem(gy + ngy - 1, ngy))
    moves = []

    def migrate(part):
        gather(MR, (10, 11, 12), range(4 * part, 4 * part + 4))
        gather(ML, (-3, -2, -1), range(4 * part, 4 * part + 4))
        some = pl.ds(4 * part, 4)
        moves.append(remote(MR.at[some], U.at[4, some], ahead))
        moves.append(remote(ML.at[some], U.at[5, some], behind))
        for copy in moves[-2:]:
            copy.start()

    migrate(0)
    for copy in round1:
        copy.wait_recv()
    top = VS[0]
    for s in range(ngy - 1):
        top = jnp.maximum(top, P1[s])
    VS[1] = top
    round2 = [remote(VS.at[1], P2.at[s - 1], at(s, 0)) for s in farthest(ngx, 4)]
    for copy in round2:
        copy.start()
    migrate(1)

    gather(U.at[0], (3, 4, 5))
    gather(U.at[1], (6,))
    gather(U.at[2], (0, 1, 2))
    gather(U.at[3], (7, 8, 9))

    def first(t, carry, pick=lambda t: t):
        at_u = pick(t)
        for r in ROWS:
            u = [U[at_u, c, r : r + 8, :] for c in range(8)]
            flux_x, edge_x, flux_y, edge_y = cell_state(u)
            for i, v in enumerate(flux_x + edge_x):
                SX[i, r : r + 8, :] = v
            _, _, a, b, w = edge_weights(*edge_y, roll(edge_y[0], -1), roll(edge_y[1], -1))
            cell = (u[2],) + flux_y[:5] + (None,) + flux_y[5:]
            for c in range(8):
                jump = w * (roll(u[c], -1) - u[c])
                flux = jump if cell[c] is None else a * cell[c] + b * roll(cell[c], -1) + jump
                DY[t, c, r : r + 8, :] = flux - roll(flux, 1)
        for r in FACE1:
            edges = [SX[i, r + d : r + d + 8, :] for d in range(2) for i in (6, 7)]
            _, _, a, b, w = edge_weights(*edges)
            for c in range(8):
                low, high = U[at_u, c, r : r + 8, :], U[at_u, c, r + 1 : r + 9, :]
                flux = w * (high - low)
                if c == 0:
                    flux = a * U[at_u, 1, r : r + 8, :] + b * U[at_u, 1, r + 1 : r + 9, :] + flux
                elif c != 5:
                    i = c - 1 if c < 5 else c - 2
                    flux = a * SX[i, r : r + 8, :] + b * SX[i, r + 1 : r + 9, :] + flux
                GX[t, c, r : r + 8, :] = flux
        return carry

    lax.fori_loop(0, 2, first, 0)

    def widths(ws):
        v = jnp.full((8, 128), wide[ws[0]], F32)
        for g, w in enumerate(ws[1:]):
            v = jnp.where(lane8 < EXT * (g + 1), v, wide[w])
        return v

    VM[0] = widths((3, 4, 5))
    VM[1] = widths((6,))
    VM[2] = widths((0, 1, 2))
    VM[3] = widths((7, 8, 9))

    for copy in ghosts + round1 + moves + round2:
        copy.wait_send()
    for copy in round2:
        copy.wait_recv()
    for s in range(ngx - 1):
        top = jnp.maximum(top, P2[s])
    top = jnp.max(top, axis=1, keepdims=True)
    time_step = COURANT / jnp.broadcast_to(top, (8, 128))

    def second(t, carry, pick=lambda t: t):
        rate = time_step * VM[t]
        at_u = pick(t)
        half = 0.5 * rate
        for r in MID:
            u = []
            for c in range(8):
                change = GX[t, c, r : r + 8, :] - GX[t, c, r - 1 : r + 7, :] + DY[t, c, r : r + 8, :]
                u.append(U[at_u, c, r : r + 8, :] - half * change)
            _, vx, vy, vz, pressure, _ = primitive(u)
            for c, v in enumerate((u[0], vx, vy, vz, pressure, u[5], u[6], u[7])):
                W[c, r : r + 8, :] = v
        for r in SLOPE:
            for c in range(8):
                w = [W[c, r + d : r + d + 8, :] for d in (-1, 0, 1, 2)]
                low, d, high = w[1] - w[0], w[2] - w[1], w[3] - w[2]
                rise = limited(0.5 * d + (low - high) * (1.0 / 12.0), d)
                RA[c, r : r + 8, :] = rise
                EA[c, r : r + 8, :] = d - rise
        for r in FACE2:
            left, right = [], []
            for c in range(8):
                rise, rise_next = RA[c, r : r + 8, :], RA[c, r + 1 : r + 9, :]
                fall, fall_next = EA[c, r - 1 : r + 7, :], EA[c, r : r + 8, :]
                left.append(W[c, r : r + 8, :] + limited(rise, 2.0 * fall))
                right.append(W[c, r + 1 : r + 9, :] - limited(fall_next, 2.0 * rise_next))
            for c, v in enumerate(face_flux(left, right, 1)):
                GX2[c, r : r + 8, :] = v
        for r in LAST:
            left, right = [], []
            for c in range(8):
                w = W[c, r : r + 8, :]
                ahead_w = roll(w, -1)
                d = ahead_w - w
                rise = limited(0.5 * d + (roll(d, 1) - roll(d, -1)) * (1.0 / 12.0), d)
                fall = d - rise
                left.append(w + limited(rise, 2.0 * roll(fall, 1)))
                right.append(ahead_w - limited(fall, 2.0 * roll(rise, -1)))
            for c, v in enumerate(face_flux(left, right, 2)):
                change = GX2[c, r : r + 8, :] - GX2[c, r - 1 : r + 7, :] + (v - roll(v, 1))
                O[t, c, r - 4 : r + 4, :] = U[at_u, c, r : r + 8, :] - rate * change
        return carry

    lax.fori_loop(0, 2, second, 0)

    def finish_local():
        for c in range(8):
            o0, o1 = O[0, c], O[1, c]
            out[c, :, 0:128] = roll(o0, 92)
            x = jnp.where(lane32 < 64, roll(o0, -52), roll(o1, 60))
            out[c, :, 128:256] = jnp.where(lane32 < 32, roll(o0, -44), x)

    finish_local()

    for copy in moves:
        copy.wait_recv()

    def pick(t):
        from_left = jnp.where(excess > 0, 4, 2)
        from_right = jnp.where(excess + count < CAP, 5, 3)
        return jnp.where(t == 2, from_left, jnp.where(t == 3, from_right, t))

    lax.fori_loop(2, 4, functools.partial(first, pick=pick), 0)
    lax.fori_loop(2, 4, functools.partial(second, pick=pick), 0)

    def finish():
        for c in range(8):
            o2, o3 = O[2, c], O[3, c]
            x = jnp.where(lane32 < 32, roll(o2, -4), jnp.where(lane32 < 64, roll(o2, -12), roll(o2, -20)))
            pltpu.store(out.at[c, :, pl.ds(0, 128)], x, mask=lane32 < 96)
            pltpu.store(out.at[c, :, pl.ds(128, 128)], roll(o3, 92), mask=lane32 >= 96)
            x = jnp.where(lane32 < 32, roll(o3, -44), roll(o3, -52))
            out[c, :, 256:320] = x[:, 0:64]

    finish()


def shards(ngx, ngy, fields, refined):
    vmem = lambda *shape: pltpu.VMEM(shape, F32)
    scratch = [
        pltpu.SMEM((2 * ngy, 2 * ngx), jnp.int32),
        pltpu.VMEM((2 * ngy, 2 * ngx), jnp.int32),
        vmem(8, 32, 512),
        vmem(8, 2, BS, 128),
        vmem(8, PAD_ROWS, 128),
        vmem(6, 8, EXT, 128),
        vmem(8, EXT, 128),
        vmem(8, EXT, 128),
        vmem(2, 8, 8, 128),
        vmem(2, 8, 8, 128),
        vmem(2, 8, 128),
        vmem(4, 8, 128),
        vmem(2, 2, 32, 128),
        vmem(2, 2, 32, 128),
        vmem(4, 8, 128),
        vmem(2, 1, 128),
        vmem(ngy - 1, 1, 128),
        vmem(ngx - 1, 1, 128),
        vmem(8, EXT, 128),
        vmem(4, 8, EXT, 128),
        vmem(4, 8, EXT, 128),
        vmem(8, EXT, 128),
        vmem(8, EXT, 128),
        vmem(8, EXT, 128),
        vmem(8, EXT, 128),
        vmem(4, 8, BS, 128),
        pltpu.SemaphoreType.DMA((3,)),
        pltpu.SemaphoreType.DMA((ngx + ngy + 10,)),
        pltpu.SemaphoreType.DMA((ngx + ngy + 10,)),
    ]
    return pl.pallas_call(
        functools.partial(kernel, ngx, ngy),
        out_shape=jax.ShapeDtypeStruct((8, BS, CAP * BS), F32),
        in_specs=[
            pl.BlockSpec(memory_space=pltpu.HBM),
            pl.BlockSpec(memory_space=pltpu.HBM),
        ],
        out_specs=pl.BlockSpec(memory_space=pltpu.VMEM),
        scratch_shapes=scratch,
        compiler_params=pltpu.CompilerParams(
            collective_id=0, has_side_effects=True, vmem_limit_bytes=56_000_000
        ),
    )(refined.T, fields)


def solution(mesh):
    ngx, ngy = mesh.shape["gx"], mesh.shape["gy"]
    return jax.shard_map(
        functools.partial(shards, ngx, ngy),
        mesh=mesh,
        in_specs=(P(None, None, ("gx", "gy")), P()),
        out_specs=P(None, None, ("gx", "gy")),
        check_vma=False,
    )
```
